32 devices in a mesh: row: 4 (over y, x), col: 8 (over z, core).
Axes of the slice: x: 2, y: 2, z: 4, core: 2. Of those that a mesh axis runs over, the one named last changes fastest.
Arguments:
- evecs: float32 [2048, 1024], P('row', 'col'), may hold values from -6 to 6
- offsets: int32 [4, 2], replicated, may hold values from 0 to 127, as said below
- refl: float32 [4, 2, 16, 64, 192], P(None, None, 'row', 'col'), may hold values from -6 to 6, as said below
Outputs:
- rotated: float32 [2048, 1024], P('row', 'col')
The draws below stay inside these ranges and needn't reach their ends.
Inputs may be any that keep to these rules, and one draw needn't show every extreme that they name: Within each round and sweep the windows start at offsets plus multiples of 128; some entry is 0 and some is 127 in every draw. `refl`: each block's triangular factor T is the inverse of the strictly upper part of V^T V plus half its diagonal, so that I - V T V^T is orthogonal.
All inputs are finite; a program needn't handle non-finite values.
Results may differ from the reference program's by a relative error of at most 0.0003.
Values sent between devices are 32-bit elements; how exact they have to be, the bound alone decides.
No kernel may reach another device: no remote copies, remote signals or barrier semaphores. Data moves between devices by JAX's collectives and lax.ppermute only.
A program may use at most 64 MiB of HBM per device.

```python
import jax
import jax.numpy as jnp
from jax import lax

WINDOW_ROWS = 128
BLOCK_REFLECTORS = 64
SWEEP_ROUNDS = 4
NR = 2048
NC = 1024
SWEEP_WINDOWS = 16


def reflector_blocks(key):
    vector_key = jax.random.fold_in(key, 0)
    householder_vectors = jax.random.normal(vector_key, (SWEEP_ROUNDS, 2, SWEEP_WINDOWS, BLOCK_REFLECTORS, WINDOW_ROWS), jnp.float32)
    householder_vectors = jnp.clip(householder_vectors, -6.0, 6.0)
    gram = jnp.einsum('abkiw,abkjw->abkij', householder_vectors, householder_vectors, precision=lax.Precision.HIGHEST)
    unit = jnp.eye(BLOCK_REFLECTORS, dtype=jnp.float32)
    inverse = jnp.triu(gram, 1) + 0.5 * gram * unit
    target = jnp.broadcast_to(unit, inverse.shape)
    factor = jax.scipy.linalg.solve_triangular(inverse, target, lower=False)
    return jnp.concatenate([householder_vectors, factor], -1)


def draw_refl(key, part):
    return reflector_blocks(jax.random.fold_in(key, 11))


def draw_offsets(key, part):
    akey, bkey = jax.random.split(jax.random.fold_in(key, 7))
    values = jax.random.randint(akey, (SWEEP_ROUNDS * 2,), 1, 127)
    order = jax.random.permutation(bkey, SWEEP_ROUNDS * 2)
    values = jnp.where(order == 0, 0, jnp.where(order == 1, 127, values))
    return values.reshape(SWEEP_ROUNDS, 2).astype(jnp.int32)


def shard_levels(key, extent, cuts, smallest, largest):
    gain = 1.0
    for dim, blocks in cuts:
        draws = jax.random.uniform(jax.random.fold_in(jax.random.fold_in(key, 6), dim), (blocks,), jnp.float32, smallest / len(cuts), largest / len(cuts))
        gain = gain * jnp.repeat(jnp.exp(draws), extent[dim] // blocks).reshape((-1,) + (1,) * (len(extent) - 1 - dim))
    return gain


def centred(rng, shape, width, bound, pieces=(), kind=jnp.bfloat16):
    drawn = width * jax.random.normal(rng, shape, jnp.float32)
    if pieces:
        drawn = drawn * shard_levels(rng, shape, pieces, -0.22, 0.18)
    return jnp.clip(drawn, -bound, bound).astype(kind)


def setup_inputs(seed: int = 0) -> dict:
    key_list = jax.random.split(jax.random.key(seed), 4)
    return {
        "evecs": centred(key_list[0], (NR, NC), 1.0, 6.0, ((0, 4), (1, 8)), jnp.float32),
        "offsets": draw_offsets(jax.random.fold_in(key_list[3], 71), 0),
        "refl": draw_refl(jax.random.fold_in(key_list[3], 71), 0),
    }


def reference(evecs, offsets, refl):
    rows, cols = evecs.shape
    padded = jnp.concatenate([evecs, jnp.zeros((WINDOW_ROWS, cols), jnp.float32)], 0)
    for rnd in range(SWEEP_ROUNDS):
        for sweep in range(2):
            start = offsets[rnd, sweep]

            def step(index, field):
                first = (start + index * WINDOW_ROWS).astype(jnp.int32)
                window = lax.dynamic_slice_in_dim(field, first, WINDOW_ROWS, 0)
                block = refl[rnd, sweep, index]
                reflect = block[:, :WINDOW_ROWS]
                factor = block[:, WINDOW_ROWS:]
                proj = jnp.dot(reflect, window, precision=lax.Precision.HIGHEST)
                scaled = jnp.dot(factor, proj, precision=lax.Precision.HIGHEST)
                window = window - jnp.dot(reflect.T, scaled, precision=lax.Precision.HIGHEST)
                return lax.dynamic_update_slice_in_dim(field, window, first, 0)
            padded = lax.fori_loop(0, SWEEP_WINDOWS, step, padded)
            padded = jnp.concatenate([padded[:rows], jnp.zeros((WINDOW_ROWS, cols), jnp.float32)], 0)
    return padded[:rows]
```

```python
import functools

import jax
import jax.numpy as jnp
from jax import lax
from jax.experimental import pallas as pl
from jax.experimental.pallas import tpu as pltpu
from jax.sharding import PartitionSpec as P

WINDOW = 128
HALF = 2 * WINDOW
VMEM_LIMIT = 24 * 1024 * 1024


def shifted(value, axis, by):
    devices = lax.axis_size(axis)
    return lax.ppermute(value, axis, [(i, (i + by) % devices) for i in range(devices)])


def pack(refl):
    rounds, sweeps, nwin, mine, width = refl.shape
    vectors = refl[..., :WINDOW].reshape(rounds * sweeps * nwin, mine, WINDOW)
    first = refl[:, :, 0::2, :, WINDOW:]
    second = refl[:, :, 1::2, :, WINDOW:]
    factors = jnp.concatenate([first, second], -1)
    factors = factors.reshape(rounds * sweeps * nwin // 2, mine, WINDOW)
    edge_vectors = refl[:, :, 0, :, :WINDOW].reshape(rounds * sweeps, mine, WINDOW)
    edge_factors = jnp.concatenate([refl[:, 0, 0, :, WINDOW:], refl[:, 1, 0, :, WINDOW:]], -1)
    edge = jnp.concatenate([edge_vectors, edge_factors], 0)
    return jnp.concatenate([vectors, factors], 0), edge


def round_matrices(rnd, rounds, nwin, offsets_ref, tiles_ref, high_ref, low_ref):
    size = tiles_ref.shape[0] * tiles_ref.shape[2]
    last = lax.axis_index("row") == lax.axis_size("row") - 1
    lane = lax.broadcasted_iota(jnp.int32, (size, WINDOW), 1)
    row_id = lax.broadcasted_iota(jnp.int32, (WINDOW, WINDOW), 0)
    col_id = lax.broadcasted_iota(jnp.int32, (WINDOW, WINDOW), 1)
    unit = jnp.where(row_id == col_id, 1.0, 0.0).astype(jnp.float32)
    own = rounds * 2 * nwin
    for sweep in range(2):
        index = rnd * 2 + sweep
        for k in range(nwin + 1):
            if k < nwin:
                vec_tile = index * nwin + k
                fac_tile = own + index * (nwin // 2) + k // 2
                side = k % 2
            else:
                vec_tile = own + own // 2 + index
                fac_tile = own + own // 2 + rounds * 2 + rnd
                side = sweep
            vectors = tiles_ref[:, vec_tile].reshape(size, WINDOW)
            factor = tiles_ref[:, fac_tile].reshape(size, WINDOW)[:, side * size : (side + 1) * size]
            if k == nwin - 1:
                limit = jnp.where(last, WINDOW - offsets_ref[rnd, sweep], WINDOW)
                vectors = jnp.where(lane < limit, vectors, 0.0)
            scaled = lax.dot_general(
                factor, vectors, (((1,), (0,)), ((), ())),
                precision=lax.Precision.HIGHEST, preferred_element_type=jnp.float32,
            )
            product = lax.dot_general(
                vectors, scaled, (((0,), (0,)), ((), ())),
                precision=lax.Precision.HIGHEST, preferred_element_type=jnp.float32,
            )
            full = unit - product
            high = full.astype(jnp.bfloat16)
            high_ref[sweep * (nwin + 1) + k] = high
            low_ref[sweep * (nwin + 1) + k] = (full - high.astype(jnp.float32)).astype(jnp.bfloat16)


def matrices(rnd, rounds, nwin, offsets, tiles):
    count = 2 * (nwin + 1)
    shape = jax.ShapeDtypeStruct((count, WINDOW, WINDOW), jnp.bfloat16)
    return pl.pallas_call(
        functools.partial(round_matrices, rnd, rounds, nwin),
        out_shape=(shape, shape),
        in_specs=[
            pl.BlockSpec(memory_space=pltpu.SMEM),
            pl.BlockSpec(memory_space=pltpu.VMEM),
        ],
        out_specs=(pl.BlockSpec(memory_space=pltpu.VMEM),) * 2,
        compiler_params=pltpu.CompilerParams(vmem_limit_bytes=VMEM_LIMIT),
        cost_estimate=pl.CostEstimate(
            flops=count * 12 * 64 * 128 * 192, bytes_accessed=count * 100000, transcendentals=0
        ),
    )(offsets, tiles)


def apply_windows(field, at, count, first, high_ref, low_ref):
    rows = field[pl.ds(at, count * WINDOW), :]
    cols = rows.shape[1]
    updated = []
    for k in range(count):
        window = rows[k * WINDOW : (k + 1) * WINDOW]
        top = window.astype(jnp.bfloat16)
        rest = (window - top.astype(jnp.float32)).astype(jnp.bfloat16)
        high = high_ref[first + k]
        low = low_ref[first + k]
        both = jnp.dot(
            high, jnp.concatenate([top, rest], 1), preferred_element_type=jnp.float32
        )
        small = jnp.dot(low, top, preferred_element_type=jnp.float32)
        updated.append(both[:, :cols] + (both[:, cols:] + small))
    field[pl.ds(at, count * WINDOW), :] = jnp.concatenate(updated, 0)


def phase_kernel(kind, before, after, nwin, offsets_ref, *refs):
    refs = list(refs)
    parts = [refs.pop(0) for _ in range(1 if before is None else 2)]
    old = None if before is None else (refs.pop(0), refs.pop(0))
    new = None if after is None else (refs.pop(0), refs.pop(0))
    field = refs.pop()
    outs = refs
    rows = field.shape[0]
    place = 0
    for part in parts:
        field[place : place + part.shape[0], :] = part[...]
        place += part.shape[0]
    base = 2 if kind == "shifted" else 0
    if old is not None:
        a = offsets_ref[before, 0]
        b = offsets_ref[before, 1]
        step = jnp.where(b < a, 1, 0)
        if kind == "shifted":
            k_a, k_b = nwin - 1, nwin - 2 + step
        else:
            k_a, k_b = 1, step
        apply_windows(field, a + WINDOW * (k_a - base), 1, k_a, *old)
        apply_windows(field, b + WINDOW * (k_b - base), 2, nwin + 1 + k_b, *old)
    if new is not None:
        a = offsets_ref[after, 0]
        b = offsets_ref[after, 1]
        step = jnp.where(b < a, 1, 0)
        apply_windows(field, a, nwin - 1, base, *new)
        apply_windows(field, b + WINDOW * step, nwin - 2, nwin + 1 + base + step, *new)
    place = 0
    for out in outs:
        out[...] = field[place : place + out.shape[0], :]
        place += out.shape[0]


def phase(kind, before, after, nwin, offsets, parts, old, new, split):
    rows = sum(part.shape[0] for part in parts)
    cols = parts[0].shape[1]
    operands = [offsets, *parts, *(old or ()), *(new or ())]
    vmem = pl.BlockSpec(memory_space=pltpu.VMEM)
    return pl.pallas_call(
        functools.partial(phase_kernel, kind, before, after, nwin),
        out_shape=tuple(jax.ShapeDtypeStruct((n, cols), jnp.float32) for n in split),
        in_specs=[pl.BlockSpec(memory_space=pltpu.SMEM)] + [vmem] * (len(operands) - 1),
        out_specs=(vmem,) * len(split),
        scratch_shapes=[pltpu.VMEM((rows, cols), jnp.float32)],
        compiler_params=pltpu.CompilerParams(vmem_limit_bytes=VMEM_LIMIT),
        cost_estimate=pl.CostEstimate(
            flops=8 * 6 * WINDOW * WINDOW * cols, bytes_accessed=2000000, transcendentals=0
        ),
    )(*operands)


def shards(evecs, offsets, refl):
    rows = evecs.shape[0]
    nwin = rows // WINDOW
    rounds, _, _, mine, width = refl.shape
    size = width - WINDOW
    packed, edge = pack(refl)
    ahead = shifted(edge, "row", -1)
    tiles = lax.all_gather(jnp.concatenate([packed, ahead], 0), "col", axis=0)
    if mine % 8:
        tiles = jnp.moveaxis(tiles, 0, 1).reshape(1, tiles.shape[1], size, WINDOW)
    mats = [matrices(rnd, rounds, nwin, offsets, tiles) for rnd in range(rounds)]
    rest = rows - HALF
    parts = [evecs]
    before = None
    for rnd in range(rounds):
        kind = "shifted" if rnd % 2 else "home"
        old = None if before is None else mats[before]
        split = (HALF, rest) if kind == "home" else (rest, HALF)
        halves = phase(kind, before, rnd, nwin, offsets, parts, old, mats[rnd], split)
        if kind == "home":
            parts = [halves[1], shifted(halves[0], "row", -1)]
        else:
            parts = [shifted(halves[1], "row", 1), halves[0]]
        before = rnd
    kind = "shifted" if rounds % 2 else "home"
    (result,) = phase(kind, before, None, nwin, offsets, parts, mats[before], None, (rows,))
    if kind == "shifted":
        result = jnp.concatenate([shifted(result[rest:], "row", 1), result[:rest]], 0)
    return result


def solution(mesh):
    placed = (P("row", "col"), P(), P(None, None, "row", "col", None))
    return jax.shard_map(
        shards, mesh=mesh, in_specs=placed, out_specs=P("row", "col"), check_vma=False
    )
```

```python
import functools

import jax
import jax.numpy as jnp
from jax import lax
from jax.experimental import pallas as pl
from jax.experimental.pallas import tpu as pltpu
from jax.sharding import PartitionSpec as P

WINDOW = 128
HALF = 2 * WINDOW
CORES = 2
VMEM_LIMIT = 24 * 1024 * 1024
VMEM = pl.BlockSpec(memory_space=pltpu.VMEM)
SMEM = pl.BlockSpec(memory_space=pltpu.SMEM)


def shifted(value, axis, by):
    devices = lax.axis_size(axis)
    return lax.ppermute(value, axis, [(i, (i + by) % devices) for i in range(devices)])


def chip_shifted(value, by):
    devices = lax.axis_size("col")
    step = by * CORES
    return lax.ppermute(value, "col", [(i, (i + step) % devices) for i in range(devices)])


def core_swapped(value):
    devices = lax.axis_size("col")
    return lax.ppermute(value, "col", [(i, i ^ 1) for i in range(devices)])


class Plan:
    def __init__(self, rounds, nwin):
        self.nwin = nwin
        self.phases = []
        for ph in range(rounds + 1):
            away = ph % 2 == 1
            entries = []
            self_carry = None
            if ph > 0:
                a, b = 2 * ph - 2, 2 * ph - 1
                if away:
                    entries += [(a, nwin - 1), None, (b, nwin - 1), (b, nwin)]
                    self_carry = (1, self.count(ph - 1) - 1)
                else:
                    entries += [(a, 1), (b, 0), (b, 1), None]
                    self_carry = (3, self.count(ph - 1) - (nwin - 1))
            if ph < rounds:
                base = 2 if away else 0
                for sweep in (2 * ph, 2 * ph + 1):
                    entries += [(sweep, base + k) for k in range(nwin - 1)]
            self.phases.append((entries, self_carry))
        groups = [[ph] for ph in range(rounds - 1)] + [[rounds - 1, rounds]]
        self.groups = []
        self.where = {}
        edge_at = 0
        for g, members in enumerate(groups):
            wanted = [w for ph in members for w in self.phases[ph][0] if w is not None]
            own = [w for w in wanted if w[1] < nwin]
            edge = [w for w in wanted if w[1] == nwin]
            place = 0
            for part in (own, edge):
                for i, w in enumerate(part):
                    self.where[w] = (g, place + i, place + len(part) + i // 2, i % 2)
                place += len(part) + (len(part) + 1) // 2
            own_tiles = len(own) + (len(own) + 1) // 2
            edge_tiles = place - own_tiles
            self.groups.append((own, edge, own_tiles, edge_tiles, edge_at))
            edge_at += edge_tiles
        self.edge_tiles = edge_at

    def count(self, ph):
        return len(self.phases[ph][0])


def pack_kernel(plan, refl_ref, *outs):
    size = refl_ref.shape[-1] - WINDOW
    mine = refl_ref.shape[-2]

    def fill(out, at, windows):
        for i, (sweep, k) in enumerate(windows):
            out[at + i] = refl_ref[sweep // 2, sweep % 2, k, :, :WINDOW]
        at += len(windows)
        for i in range(0, len(windows), 2):
            halves = []
            for sweep, k in windows[i : i + 2]:
                halves.append(refl_ref[sweep // 2, sweep % 2, k, :, WINDOW:])
            if len(halves) == 1:
                halves.append(jnp.zeros((mine, size), jnp.float32))
            out[at + i // 2] = jnp.concatenate(halves, -1)

    for group, out in zip(plan.groups, outs):
        fill(out, 0, group[0])
    for group in plan.groups:
        if group[1]:
            fill(outs[-1], group[4], [(sweep, 0) for sweep, _ in group[1]])


def pack(plan, refl):
    mine = refl.shape[3]
    counts = [group[2] for group in plan.groups] + [plan.edge_tiles]
    return pl.pallas_call(
        functools.partial(pack_kernel, plan),
        out_shape=tuple(jax.ShapeDtypeStruct((n, mine, WINDOW), jnp.float32) for n in counts),
        in_specs=[VMEM],
        out_specs=(VMEM,) * len(counts),
        compiler_params=pltpu.CompilerParams(vmem_limit_bytes=VMEM_LIMIT),
    )(refl)


def matrix_kernel(plan, ph, offsets_ref, *refs):
    entries, carry = plan.phases[ph]
    refs = list(refs)
    old_high, old_low = (refs.pop(0), refs.pop(0)) if carry else (None, None)
    tiles = refs.pop()
    high_ref, low_ref = refs[-2:]
    parts = refs[:-2]
    if len(parts) == 2:
        here = lax.axis_index("col")
        chips = parts[0].shape[0]
        core = here % CORES
        for m in range(chips):
            tiles[CORES * m + core] = parts[0][m]
            tiles[CORES * m + (CORES - 1 - core)] = parts[1][m]
    else:
        tiles = parts[0]
    size = tiles.shape[0] * tiles.shape[2]
    last = lax.axis_index("row") == lax.axis_size("row") - 1
    lane = lax.broadcasted_iota(jnp.int32, (size, WINDOW), 1)
    row_id = lax.broadcasted_iota(jnp.int32, (WINDOW, WINDOW), 0)
    col_id = lax.broadcasted_iota(jnp.int32, (WINDOW, WINDOW), 1)
    unit = jnp.where(row_id == col_id, 1.0, 0.0).astype(jnp.float32)
    for i, window in enumerate(entries):
        if window is None:
            source = carry[1]
            high_ref[i] = old_high[source]
            low_ref[i] = old_low[source]
            continue
        sweep, k = window
        _, vec_tile, fac_tile, side = plan.where[window]
        vectors = tiles[:, vec_tile].reshape(size, WINDOW)
        factor = tiles[:, fac_tile].reshape(size, WINDOW)[:, side * size : (side + 1) * size]
        if k == plan.nwin - 1:
            limit = jnp.where(last, WINDOW - offsets_ref[sweep // 2, sweep % 2], WINDOW)
            vectors = jnp.where(lane < limit, vectors, 0.0)
        scaled = lax.dot_general(
            factor, vectors, (((1,), (0,)), ((), ())),
            precision=lax.Precision.HIGHEST, preferred_element_type=jnp.float32,
        )
        product = lax.dot_general(
            vectors, scaled, (((0,), (0,)), ((), ())),
            precision=lax.Precision.HIGHEST, preferred_element_type=jnp.float32,
        )
        full = unit - product
        high = full.astype(jnp.bfloat16)
        high_ref[i] = high
        low_ref[i] = (full - high.astype(jnp.float32)).astype(jnp.bfloat16)


def matrices(plan, ph, offsets, before, parts):
    count = plan.count(ph)
    shape = jax.ShapeDtypeStruct((count, WINDOW, WINDOW), jnp.bfloat16)
    carried = before if plan.phases[ph][1] else ()
    operands = [offsets, *carried, *parts]
    whole = (sum(part.shape[0] for part in parts),) + parts[0].shape[1:]
    return pl.pallas_call(
        functools.partial(matrix_kernel, plan, ph),
        out_shape=(shape, shape),
        in_specs=[SMEM] + [VMEM] * (len(operands) - 1),
        out_specs=(VMEM,) * 2,
        scratch_shapes=[pltpu.VMEM(whole, jnp.float32)],
        compiler_params=pltpu.CompilerParams(vmem_limit_bytes=VMEM_LIMIT),
        cost_estimate=pl.CostEstimate(
            flops=count * 12 * 64 * 128 * 192, bytes_accessed=count * 100000, transcendentals=0
        ),
    )(*operands)


def apply_windows(field, at, count, first, high_ref, low_ref):
    rows = field[pl.ds(at, count * WINDOW), :]
    cols = rows.shape[1]
    updated = []
    for k in range(count):
        window = rows[k * WINDOW : (k + 1) * WINDOW]
        top = window.astype(jnp.bfloat16)
        rest = (window - top.astype(jnp.float32)).astype(jnp.bfloat16)
        high = high_ref[first + k]
        low = low_ref[first + k]
        both = jnp.dot(
            high, jnp.concatenate([top, rest], 1), preferred_element_type=jnp.float32
        )
        small = jnp.dot(low, top, preferred_element_type=jnp.float32)
        updated.append(both[:, :cols] + (both[:, cols:] + small))
    field[pl.ds(at, count * WINDOW), :] = jnp.concatenate(updated, 0)


def phase_kernel(ph, rounds, nwin, nparts, offsets_ref, *refs):
    parts = refs[:nparts]
    mats = refs[nparts : nparts + 2]
    outs = refs[nparts + 2 : -1]
    field = refs[-1]
    place = 0
    for part in parts:
        field[place : place + part.shape[0], :] = part[...]
        place += part.shape[0]
    at = 0
    if ph > 0:
        a = offsets_ref[ph - 1, 0]
        b = offsets_ref[ph - 1, 1]
        step = jnp.where(b < a, 1, 0)
        start = nwin - 3 if ph % 2 else 1
        apply_windows(field, a + WINDOW * start, 1, 0, *mats)
        start = nwin - 4 if ph % 2 else 0
        apply_windows(field, b + WINDOW * (start + step), 2, 1 + step, *mats)
        at = 4
    if ph < rounds:
        a = offsets_ref[ph, 0]
        b = offsets_ref[ph, 1]
        step = jnp.where(b < a, 1, 0)
        apply_windows(field, a, nwin - 1, at, *mats)
        apply_windows(field, b + WINDOW * step, nwin - 2, at + nwin - 1 + step, *mats)
    place = 0
    for out in outs:
        out[...] = field[place : place + out.shape[0], :]
        place += out.shape[0]


def phase(ph, rounds, nwin, offsets, parts, mats, split):
    rows = sum(part.shape[0] for part in parts)
    cols = parts[0].shape[1]
    operands = [offsets, *parts, *mats]
    return pl.pallas_call(
        functools.partial(phase_kernel, ph, rounds, nwin, len(parts)),
        out_shape=tuple(jax.ShapeDtypeStruct((n, cols), jnp.float32) for n in split),
        in_specs=[SMEM] + [VMEM] * (len(operands) - 1),
        out_specs=(VMEM,) * len(split),
        scratch_shapes=[pltpu.VMEM((rows, cols), jnp.float32)],
        compiler_params=pltpu.CompilerParams(vmem_limit_bytes=VMEM_LIMIT),
        cost_estimate=pl.CostEstimate(
            flops=8 * 6 * WINDOW * WINDOW * cols, bytes_accessed=2000000, transcendentals=0
        ),
    )(*operands)


def gather(plan, packed, size):
    devices = lax.axis_size("col")
    *own, edge = packed
    mine = edge.shape[1]
    ahead = shifted(edge, "row", -1)
    chips = devices // CORES
    stepwise = mine % 8 == 0 and devices % CORES == 0 and chips <= 4
    gathered = []
    previous = None
    for (_, _, _, edge_tiles, edge_at), tiles in zip(plan.groups, own):
        if edge_tiles:
            tiles = jnp.concatenate([tiles, ahead[edge_at : edge_at + edge_tiles]], 0)
        if stepwise:
            if previous is not None:
                tiles, _ = lax.optimization_barrier((tiles, previous))
            copies = jnp.broadcast_to(tiles[None], (chips,) + tiles.shape)
            same = lax.all_to_all(
                copies, "col", 0, 0,
                axis_index_groups=[list(range(c, devices, CORES)) for c in range(CORES)],
            )
            previous = same
            gathered.append((same, core_swapped(same)))
        else:
            whole = lax.all_gather(tiles, "col", axis=0)
            whole = jnp.moveaxis(whole, 0, 1).reshape(1, whole.shape[1], size, WINDOW)
            gathered.append((whole,))
    return gathered


def shards(evecs, offsets, refl):
    rows = evecs.shape[0]
    nwin = rows // WINDOW
    rounds = refl.shape[0]
    size = refl.shape[4] - WINDOW
    plan = Plan(rounds, nwin)
    gathered = gather(plan, pack(plan, refl), size)
    mats = []
    for ph in range(rounds + 1):
        before = mats[-1] if mats else None
        mats.append(matrices(plan, ph, offsets, before, gathered[min(ph, rounds - 1)]))
    rest = rows - HALF
    parts = [evecs]
    for ph in range(rounds):
        away = ph % 2 == 1
        split = (rest, HALF) if away else (HALF, rest)
        halves = phase(ph, rounds, nwin, offsets, parts, mats[ph], split)
        if away:
            parts = [shifted(halves[1], "row", 1), halves[0]]
        else:
            parts = [halves[1], shifted(halves[0], "row", -1)]
    (result,) = phase(rounds, rounds, nwin, offsets, parts, mats[rounds], (rows,))
    if rounds % 2:
        result = jnp.concatenate([shifted(result[rest:], "row", 1), result[:rest]], 0)
    return result


def solution(mesh):
    placed = (P("row", "col"), P(), P(None, None, "row", "col", None))
    return jax.shard_map(
        shards, mesh=mesh, in_specs=placed, out_specs=P("row", "col"), check_vma=False
    )
```

```python
import functools

import jax
import jax.numpy as jnp
from jax import lax
from jax.experimental import pallas as pl
from jax.experimental.pallas import tpu as pltpu
from jax.sharding import PartitionSpec as P

WINDOW = 128
HALF = 2 * WINDOW
CORES = 2
VMEM_LIMIT = 24 * 1024 * 1024
VMEM = pl.BlockSpec(memory_space=pltpu.VMEM)
SMEM = pl.BlockSpec(memory_space=pltpu.SMEM)


def shifted(value, axis, by):
    devices = lax.axis_size(axis)
    return lax.ppermute(value, axis, [(i, (i + by) % devices) for i in range(devices)])


def chip_shifted(value, by):
    devices = lax.axis_size("col")
    step = by * CORES
    return lax.ppermute(value, "col", [(i, (i + step) % devices) for i in range(devices)])


def core_swapped(value):
    devices = lax.axis_size("col")
    return lax.ppermute(value, "col", [(i, i ^ 1) for i in range(devices)])


class Plan:
    def __init__(self, rounds, nwin):
        self.nwin = nwin
        self.phases = []
        for ph in range(rounds + 1):
            away = ph % 2 == 1
            entries = []
            self_carry = None
            if ph > 0:
                a, b = 2 * ph - 2, 2 * ph - 1
                if away:
                    entries += [(a, nwin - 1), None, (b, nwin - 1), (b, nwin)]
                    self_carry = (1, self.count(ph - 1) - 1)
                else:
                    entries += [(a, 1), (b, 0), (b, 1), None]
                    self_carry = (3, self.count(ph - 1) - (nwin - 1))
            if ph < rounds:
                base = 2 if away else 0
                for sweep in (2 * ph, 2 * ph + 1):
                    entries += [(sweep, base + k) for k in range(nwin - 1)]
            self.phases.append((entries, self_carry))
        groups = [[ph] for ph in range(rounds - 1)] + [[rounds - 1, rounds]]
        self.groups = []
        self.where = {}
        edge_at = 0
        for g, members in enumerate(groups):
            wanted = [w for ph in members for w in self.phases[ph][0] if w is not None]
            own = [w for w in wanted if w[1] < nwin]
            edge = [w for w in wanted if w[1] == nwin]
            place = 0
            for part in (own, edge):
                for i, w in enumerate(part):
                    self.where[w] = (g, place + i, place + len(part) + i // 2, i % 2)
                place += len(part) + (len(part) + 1) // 2
            own_tiles = len(own) + (len(own) + 1) // 2
            edge_tiles = place - own_tiles
            self.groups.append((own, edge, own_tiles, edge_tiles, edge_at))
            edge_at += edge_tiles
        self.edge_tiles = edge_at

    def count(self, ph):
        return len(self.phases[ph][0])


def pack_kernel(plan, refl_ref, *outs):
    size = refl_ref.shape[-1] - WINDOW
    mine = refl_ref.shape[-2]

    def fill(out, at, windows):
        for i, (sweep, k) in enumerate(windows):
            out[at + i] = refl_ref[sweep // 2, sweep % 2, k, :, :WINDOW]
        at += len(windows)
        for i in range(0, len(windows), 2):
            halves = []
            for sweep, k in windows[i : i + 2]:
                halves.append(refl_ref[sweep // 2, sweep % 2, k, :, WINDOW:])
            if len(halves) == 1:
                halves.append(jnp.zeros((mine, size), jnp.float32))
            out[at + i // 2] = jnp.concatenate(halves, -1)

    for group, out in zip(plan.groups, outs):
        fill(out, 0, group[0])
    for group in plan.groups:
        if group[1]:
            fill(outs[-1], group[4], [(sweep, 0) for sweep, _ in group[1]])


def pack(plan, refl):
    mine = refl.shape[3]
    counts = [group[2] for group in plan.groups] + [plan.edge_tiles]
    return pl.pallas_call(
        functools.partial(pack_kernel, plan),
        out_shape=tuple(jax.ShapeDtypeStruct((n, mine, WINDOW), jnp.float32) for n in counts),
        in_specs=[VMEM],
        out_specs=(VMEM,) * len(counts),
        compiler_params=pltpu.CompilerParams(vmem_limit_bytes=VMEM_LIMIT),
    )(refl)


def split(value):
    high = value.astype(jnp.bfloat16)
    return high, (value - high.astype(jnp.float32)).astype(jnp.bfloat16)


def matrix_kernel(plan, ph, offsets_ref, *refs):
    entries, carry = plan.phases[ph]
    refs = list(refs)
    old_ref = refs.pop(0) if carry else None
    tiles = refs.pop()
    out_ref = refs.pop()
    parts = refs
    if len(parts) == 2:
        here = lax.axis_index("col")
        chips = parts[0].shape[0]
        chip, core = here // CORES, here % CORES
        for m in range(chips):
            source = CORES * lax.rem(chip + (chips - m), chips)
            tiles[source + core] = parts[0][m]
            tiles[source + (CORES - 1 - core)] = parts[1][m]
    else:
        tiles = parts[0]
    size = tiles.shape[0] * tiles.shape[2]
    last = lax.axis_index("row") == lax.axis_size("row") - 1
    lane = lax.broadcasted_iota(jnp.int32, (size, WINDOW), 1)
    row_id = lax.broadcasted_iota(jnp.int32, (WINDOW, WINDOW), 0)
    col_id = lax.broadcasted_iota(jnp.int32, (WINDOW, WINDOW), 1)
    unit = jnp.where(row_id == col_id, 1.0, 0.0).astype(jnp.float32)
    for i, window in enumerate(entries):
        if window is None:
            out_ref[i] = old_ref[carry[1]]
            continue
        sweep, k = window
        _, vec_tile, fac_tile, side = plan.where[window]
        vectors = tiles[:, vec_tile].reshape(size, WINDOW)
        factor = tiles[:, fac_tile].reshape(size, WINDOW)[:, side * size : (side + 1) * size]
        if k == plan.nwin - 1:
            limit = jnp.where(last, WINDOW - offsets_ref[sweep // 2, sweep % 2], WINDOW)
            vectors = jnp.where(lane < limit, vectors, 0.0)
        rows_hi, rows_lo = split(vectors)
        fac_hi, fac_lo = split(factor)
        scaled = jnp.dot(
            jnp.concatenate([fac_hi, fac_lo, fac_hi, fac_lo], 1),
            jnp.concatenate([rows_hi, rows_hi, rows_lo, rows_lo], 0),
            preferred_element_type=jnp.float32,
        )
        scaled_hi, scaled_lo = split(scaled)
        product = lax.dot_general(
            jnp.concatenate([rows_hi, rows_lo, rows_hi, rows_lo], 0),
            jnp.concatenate([scaled_hi, scaled_hi, scaled_lo, scaled_lo], 0),
            (((0,), (0,)), ((), ())),
            preferred_element_type=jnp.float32,
        )
        high, low = split(unit - product)
        out_ref[i] = jnp.concatenate([high, low], 1)


def matrices(plan, ph, offsets, before, parts):
    count = plan.count(ph)
    carried = (before,) if plan.phases[ph][1] else ()
    operands = [offsets, *carried, *parts]
    whole = (sum(part.shape[0] for part in parts),) + parts[0].shape[1:]
    return pl.pallas_call(
        functools.partial(matrix_kernel, plan, ph),
        out_shape=jax.ShapeDtypeStruct((count, WINDOW, 2 * WINDOW), jnp.bfloat16),
        in_specs=[SMEM] + [VMEM] * (len(operands) - 1),
        out_specs=VMEM,
        scratch_shapes=[pltpu.VMEM(whole, jnp.float32)],
        compiler_params=pltpu.CompilerParams(vmem_limit_bytes=VMEM_LIMIT),
        cost_estimate=pl.CostEstimate(
            flops=count * 12 * 64 * 128 * 192, bytes_accessed=count * 100000, transcendentals=0
        ),
    )(*operands)


def apply_windows(field, at, count, first, mats):
    rows = field[pl.ds(at, count * WINDOW), :]
    cols = rows.shape[1]
    updated = []
    for k in range(count):
        pair = jnp.concatenate(split(rows[k * WINDOW : (k + 1) * WINDOW]), 1)
        both = jnp.dot(
            mats[first + k],
            jnp.concatenate([pair, pair], 0),
            preferred_element_type=jnp.float32,
        )
        updated.append(both[:, :cols] + both[:, cols:])
    field[pl.ds(at, count * WINDOW), :] = jnp.concatenate(updated, 0)


def phase_kernel(ph, rounds, nwin, nparts, offsets_ref, *refs):
    parts = refs[:nparts]
    mats = refs[nparts]
    outs = refs[nparts + 1 : -1]
    field = refs[-1]
    place = 0
    for part in parts:
        field[place : place + part.shape[0], :] = part[...]
        place += part.shape[0]
    at = 0
    if ph > 0:
        a = offsets_ref[ph - 1, 0]
        b = offsets_ref[ph - 1, 1]
        step = jnp.where(b < a, 1, 0)
        start = nwin - 3 if ph % 2 else 1
        apply_windows(field, a + WINDOW * start, 1, 0, mats)
        start = nwin - 4 if ph % 2 else 0
        apply_windows(field, b + WINDOW * (start + step), 2, 1 + step, mats)
        at = 4
    if ph < rounds:
        a = offsets_ref[ph, 0]
        b = offsets_ref[ph, 1]
        step = jnp.where(b < a, 1, 0)
        apply_windows(field, a, nwin - 1, at, mats)
        apply_windows(field, b + WINDOW * step, nwin - 2, at + nwin - 1 + step, mats)
    place = 0
    for out in outs:
        out[...] = field[place : place + out.shape[0], :]
        place += out.shape[0]


def phase(ph, rounds, nwin, offsets, parts, mats, sizes):
    rows = sum(part.shape[0] for part in parts)
    cols = parts[0].shape[1]
    operands = [offsets, *parts, mats]
    return pl.pallas_call(
        functools.partial(phase_kernel, ph, rounds, nwin, len(parts)),
        out_shape=tuple(jax.ShapeDtypeStruct((n, cols), jnp.float32) for n in sizes),
        in_specs=[SMEM] + [VMEM] * (len(operands) - 1),
        out_specs=(VMEM,) * len(sizes),
        scratch_shapes=[pltpu.VMEM((rows, cols), jnp.float32)],
        compiler_params=pltpu.CompilerParams(vmem_limit_bytes=VMEM_LIMIT),
        cost_estimate=pl.CostEstimate(
            flops=8 * 6 * WINDOW * WINDOW * cols, bytes_accessed=2000000, transcendentals=0
        ),
    )(*operands)


def after(value, earlier):
    return lax.optimization_barrier((value, earlier))[0]


class Gather:
    def __init__(self, plan, packed, size):
        self.plan = plan
        self.size = size
        *self.own, edge = packed
        self.ahead = shifted(edge, "row", -1)
        devices = lax.axis_size("col")
        self.chips = devices // CORES
        self.stepwise = edge.shape[1] % 8 == 0 and devices % CORES == 0 and self.chips <= 4
        self.sent = {}

    def send(self, g, earlier=None):
        _, _, _, edge_tiles, edge_at = self.plan.groups[g]
        tiles = self.own[g]
        if edge_tiles:
            tiles = jnp.concatenate([tiles, self.ahead[edge_at : edge_at + edge_tiles]], 0)
        if earlier is not None:
            tiles = after(tiles, earlier)
        self.sent[g] = [tiles]
        if self.stepwise:
            self.sent[g] += [chip_shifted(tiles, m) for m in range(1, self.chips)]

    def receive(self, g, earlier=None):
        if self.stepwise:
            pieces = self.sent[g]
            if earlier is not None:
                pieces = after(pieces, earlier)
            same = jnp.stack(pieces)
            return (same, core_swapped(same))
        whole = lax.all_gather(self.sent[g][0], "col", axis=0)
        whole = jnp.moveaxis(whole, 0, 1).reshape(1, whole.shape[1], self.size, WINDOW)
        return (whole,)


def shards(evecs, offsets, refl):
    rows = evecs.shape[0]
    nwin = rows // WINDOW
    rounds = refl.shape[0]
    size = refl.shape[4] - WINDOW
    plan = Plan(rounds, nwin)
    groups = len(plan.groups)
    gather = Gather(plan, pack(plan, refl), size)
    gather.send(0)
    if groups > 1:
        gather.send(1)
    rest = rows - HALF
    parts = [evecs]
    mats = None
    result = None
    for ph in range(rounds):
        tiles = gather.receive(ph, result)
        mats = matrices(plan, ph, offsets, mats, tiles)
        away = ph % 2 == 1
        sizes = (rest, HALF) if away else (HALF, rest)
        halves = phase(ph, rounds, nwin, offsets, parts, mats, sizes)
        if away:
            result, kept = halves[1], halves[0]
            parts = [shifted(result, "row", 1), kept]
        else:
            result, kept = halves
            parts = [kept, shifted(result, "row", -1)]
        if ph + 2 < groups:
            gather.send(ph + 2, result)
    mats = matrices(plan, rounds, offsets, mats, tiles)
    (result,) = phase(rounds, rounds, nwin, offsets, parts, mats, (rows,))
    if rounds % 2:
        result = jnp.concatenate([shifted(result[rest:], "row", 1), result[:rest]], 0)
    return result


def solution(mesh):
    placed = (P("row", "col"), P(), P(None, None, "row", "col", None))
    return jax.shard_map(
        shards, mesh=mesh, in_specs=placed, out_specs=P("row", "col"), check_vma=False
    )
```

```python
import functools

import jax
import jax.numpy as jnp
from jax import lax
from jax.experimental import pallas as pl
from jax.experimental.pallas import tpu as pltpu
from jax.sharding import PartitionSpec as P

WINDOW = 128
HALF = 2 * WINDOW
CORES = 2
VMEM_LIMIT = 24 * 1024 * 1024
VMEM = pl.BlockSpec(memory_space=pltpu.VMEM)
SMEM = pl.BlockSpec(memory_space=pltpu.SMEM)


def shifted(value, axis, by):
    devices = lax.axis_size(axis)
    return lax.ppermute(value, axis, [(i, (i + by) % devices) for i in range(devices)])


def swapped(value, bit):
    devices = lax.axis_size("col")
    return lax.ppermute(value, "col", [(i, i ^ bit) for i in range(devices)])


class Plan:
    def __init__(self, rounds, nwin):
        self.nwin = nwin
        self.phases = []
        for ph in range(rounds + 1):
            away = ph % 2 == 1
            entries = []
            self_carry = None
            if ph > 0:
                a, b = 2 * ph - 2, 2 * ph - 1
                if away:
                    entries += [(a, nwin - 1), None, (b, nwin - 1), (b, nwin)]
                    self_carry = (1, self.count(ph - 1) - 1)
                else:
                    entries += [(a, 1), (b, 0), (b, 1), None]
                    self_carry = (3, self.count(ph - 1) - (nwin - 1))
            if ph < rounds:
                base = 2 if away else 0
                for sweep in (2 * ph, 2 * ph + 1):
                    entries += [(sweep, base + k) for k in range(nwin - 1)]
            self.phases.append((entries, self_carry))
        groups = [[ph] for ph in range(rounds - 1)] + [[rounds - 1, rounds]]
        self.groups = []
        self.where = {}
        edge_at = 0
        for g, members in enumerate(groups):
            wanted = [w for ph in members for w in self.phases[ph][0] if w is not None]
            own = [w for w in wanted if w[1] < nwin]
            edge = [w for w in wanted if w[1] == nwin]
            place = 0
            for part in (own, edge):
                for i, w in enumerate(part):
                    self.where[w] = (g, place + i, place + len(part) + i // 2, i % 2)
                place += len(part) + (len(part) + 1) // 2
            own_tiles = len(own) + (len(own) + 1) // 2
            edge_tiles = place - own_tiles
            self.groups.append((own, edge, own_tiles, edge_tiles, edge_at))
            edge_at += edge_tiles
        self.edge_tiles = edge_at

    def count(self, ph):
        return len(self.phases[ph][0])


def pack_kernel(plan, refl_ref, *outs):
    size = refl_ref.shape[-1] - WINDOW
    mine = refl_ref.shape[-2]

    def fill(out, at, windows):
        for i, (sweep, k) in enumerate(windows):
            out[at + i] = refl_ref[sweep // 2, sweep % 2, k, :, :WINDOW]
        at += len(windows)
        for i in range(0, len(windows), 2):
            halves = []
            for sweep, k in windows[i : i + 2]:
                halves.append(refl_ref[sweep // 2, sweep % 2, k, :, WINDOW:])
            if len(halves) == 1:
                halves.append(jnp.zeros((mine, size), jnp.float32))
            out[at + i // 2] = jnp.concatenate(halves, -1)

    for group, out in zip(plan.groups, outs):
        fill(out, 0, group[0])
    for group in plan.groups:
        if group[1]:
            fill(outs[-1], group[4], [(sweep, 0) for sweep, _ in group[1]])


def pack(plan, refl):
    mine = refl.shape[3]
    counts = [group[2] for group in plan.groups] + [plan.edge_tiles]
    return pl.pallas_call(
        functools.partial(pack_kernel, plan),
        out_shape=tuple(jax.ShapeDtypeStruct((n, mine, WINDOW), jnp.float32) for n in counts),
        in_specs=[VMEM],
        out_specs=(VMEM,) * len(counts),
        compiler_params=pltpu.CompilerParams(vmem_limit_bytes=VMEM_LIMIT),
    )(refl)


def split(value):
    high = value.astype(jnp.bfloat16)
    return high, (value - high.astype(jnp.float32)).astype(jnp.bfloat16)


def matrix_kernel(plan, ph, offsets_ref, *refs):
    entries, carry = plan.phases[ph]
    refs = list(refs)
    old_ref = refs.pop(0) if carry else None
    tiles = refs.pop()
    out_ref = refs.pop()
    parts = refs
    if len(parts) == 2:
        here = lax.axis_index("col")
        for m in range(parts[0].shape[0]):
            other = lax.bitwise_xor(here, m * CORES)
            tiles[other] = parts[0][m]
            tiles[lax.bitwise_xor(other, 1)] = parts[1][m]
    else:
        tiles = parts[0]
    size = tiles.shape[0] * tiles.shape[2]
    last = lax.axis_index("row") == lax.axis_size("row") - 1
    lane = lax.broadcasted_iota(jnp.int32, (size, WINDOW), 1)
    row_id = lax.broadcasted_iota(jnp.int32, (WINDOW, WINDOW), 0)
    col_id = lax.broadcasted_iota(jnp.int32, (WINDOW, WINDOW), 1)
    unit = jnp.where(row_id == col_id, 1.0, 0.0).astype(jnp.float32)
    for i, window in enumerate(entries):
        if window is None:
            out_ref[i] = old_ref[carry[1]]
            continue
        sweep, k = window
        _, vec_tile, fac_tile, side = plan.where[window]
        vectors = tiles[:, vec_tile].reshape(size, WINDOW)
        factor = tiles[:, fac_tile].reshape(size, WINDOW)[:, side * size : (side + 1) * size]
        if k == plan.nwin - 1:
            limit = jnp.where(last, WINDOW - offsets_ref[sweep // 2, sweep % 2], WINDOW)
            vectors = jnp.where(lane < limit, vectors, 0.0)
        rows_hi, rows_lo = split(vectors)
        fac_hi, fac_lo = split(factor)
        scaled = jnp.dot(
            jnp.concatenate([fac_hi, fac_lo, fac_hi, fac_lo], 1),
            jnp.concatenate([rows_hi, rows_hi, rows_lo, rows_lo], 0),
            preferred_element_type=jnp.float32,
        )
        scaled_hi, scaled_lo = split(scaled)
        product = lax.dot_general(
            jnp.concatenate([rows_hi, rows_lo, rows_hi, rows_lo], 0),
            jnp.concatenate([scaled_hi, scaled_hi, scaled_lo, scaled_lo], 0),
            (((0,), (0,)), ((), ())),
            preferred_element_type=jnp.float32,
        )
        high, low = split(unit - product)
        out_ref[i] = jnp.concatenate([high, low], 1)


def matrices(plan, ph, offsets, before, parts):
    count = plan.count(ph)
    carried = (before,) if plan.phases[ph][1] else ()
    operands = [offsets, *carried, *parts]
    whole = (sum(part.shape[0] for part in parts),) + parts[0].shape[1:]
    return pl.pallas_call(
        functools.partial(matrix_kernel, plan, ph),
        out_shape=jax.ShapeDtypeStruct((count, WINDOW, 2 * WINDOW), jnp.bfloat16),
        in_specs=[SMEM] + [VMEM] * (len(operands) - 1),
        out_specs=VMEM,
        scratch_shapes=[pltpu.VMEM(whole, jnp.float32)],
        compiler_params=pltpu.CompilerParams(vmem_limit_bytes=VMEM_LIMIT),
        cost_estimate=pl.CostEstimate(
            flops=count * 12 * 64 * 128 * 192, bytes_accessed=count * 100000, transcendentals=0
        ),
    )(*operands)


def apply_windows(field, at, count, first, mats):
    rows = field[pl.ds(at, count * WINDOW), :]
    cols = rows.shape[1]
    updated = []
    for k in range(count):
        pair = jnp.concatenate(split(rows[k * WINDOW : (k + 1) * WINDOW]), 1)
        both = jnp.dot(
            mats[first + k],
            jnp.concatenate([pair, pair], 0),
            preferred_element_type=jnp.float32,
        )
        updated.append(both[:, :cols] + both[:, cols:])
    field[pl.ds(at, count * WINDOW), :] = jnp.concatenate(updated, 0)


def phase_kernel(ph, rounds, nwin, nparts, offsets_ref, *refs):
    parts = refs[:nparts]
    mats = refs[nparts]
    outs = refs[nparts + 1 : -1]
    field = refs[-1]
    place = 0
    for part in parts:
        field[place : place + part.shape[0], :] = part[...]
        place += part.shape[0]
    at = 0
    if ph > 0:
        a = offsets_ref[ph - 1, 0]
        b = offsets_ref[ph - 1, 1]
        step = jnp.where(b < a, 1, 0)
        start = nwin - 3 if ph % 2 else 1
        apply_windows(field, a + WINDOW * start, 1, 0, mats)
        start = nwin - 4 if ph % 2 else 0
        apply_windows(field, b + WINDOW * (start + step), 2, 1 + step, mats)
        at = 4
    if ph < rounds:
        a = offsets_ref[ph, 0]
        b = offsets_ref[ph, 1]
        step = jnp.where(b < a, 1, 0)
        apply_windows(field, a, nwin - 1, at, mats)
        apply_windows(field, b + WINDOW * step, nwin - 2, at + nwin - 1 + step, mats)
    place = 0
    for out in outs:
        out[...] = field[place : place + out.shape[0], :]
        place += out.shape[0]


def phase(ph, rounds, nwin, offsets, parts, mats, sizes):
    rows = sum(part.shape[0] for part in parts)
    cols = parts[0].shape[1]
    operands = [offsets, *parts, mats]
    return pl.pallas_call(
        functools.partial(phase_kernel, ph, rounds, nwin, len(parts)),
        out_shape=tuple(jax.ShapeDtypeStruct((n, cols), jnp.float32) for n in sizes),
        in_specs=[SMEM] + [VMEM] * (len(operands) - 1),
        out_specs=(VMEM,) * len(sizes),
        scratch_shapes=[pltpu.VMEM((rows, cols), jnp.float32)],
        compiler_params=pltpu.CompilerParams(vmem_limit_bytes=VMEM_LIMIT),
        cost_estimate=pl.CostEstimate(
            flops=8 * 6 * WINDOW * WINDOW * cols, bytes_accessed=2000000, transcendentals=0
        ),
    )(*operands)


def after(value, earlier):
    return lax.optimization_barrier((value, earlier))[0]


class Gather:
    def __init__(self, plan, packed, size):
        self.plan = plan
        self.size = size
        *own, edge = packed
        devices = lax.axis_size("col")
        self.stepwise = edge.shape[1] % 8 == 0 and devices == 4 * CORES
        if self.stepwise:
            near = swapped(own[0], CORES)
            self.pairs = [jnp.stack([own[0], near])]
            self.fours = [self.double(self.pairs[0])]
        ahead = shifted(edge, "row", -1)
        self.own = []
        for (_, _, _, edge_tiles, edge_at), tiles in zip(plan.groups, own):
            if edge_tiles:
                tiles = jnp.concatenate([tiles, ahead[edge_at : edge_at + edge_tiles]], 0)
            self.own.append(tiles)
        if self.stepwise and len(self.own) > 1:
            later = after(jnp.concatenate(self.own[1:], 0), near)
            near = swapped(later, CORES)
            at = 0
            for tiles in self.own[1:]:
                count = tiles.shape[0]
                self.pairs.append(jnp.stack([later[at : at + count], near[at : at + count]]))
                at += count
            self.fours.append(self.double(self.pairs[1]))

    def double(self, pair):
        return pair, swapped(pair, 2 * CORES)

    def send(self, g, earlier):
        if self.stepwise:
            self.fours.append(self.double(after(self.pairs[g], earlier)))

    def receive(self, g, earlier=None):
        if self.stepwise:
            pieces = self.fours[g]
            if earlier is not None:
                pieces = after(pieces, earlier)
            same = jnp.concatenate(pieces, 0)
            return (same, swapped(same, 1))
        whole = lax.all_gather(self.own[g], "col", axis=0)
        whole = jnp.moveaxis(whole, 0, 1).reshape(1, whole.shape[1], self.size, WINDOW)
        return (whole,)


def shards(evecs, offsets, refl):
    rows = evecs.shape[0]
    nwin = rows // WINDOW
    rounds = refl.shape[0]
    size = refl.shape[4] - WINDOW
    plan = Plan(rounds, nwin)
    groups = len(plan.groups)
    gather = Gather(plan, pack(plan, refl), size)
    rest = rows - HALF
    parts = [evecs]
    mats = None
    result = None
    for ph in range(rounds):
        tiles = gather.receive(ph, result)
        mats = matrices(plan, ph, offsets, mats, tiles)
        away = ph % 2 == 1
        sizes = (rest, HALF) if away else (HALF, rest)
        halves = phase(ph, rounds, nwin, offsets, parts, mats, sizes)
        if away:
            result, kept = halves[1], halves[0]
            parts = [shifted(result, "row", 1), kept]
        else:
            result, kept = halves
            parts = [kept, shifted(result, "row", -1)]
        if ph + 2 < groups:
            gather.send(ph + 2, result)
    mats = matrices(plan, rounds, offsets, mats, tiles)
    (result,) = phase(rounds, rounds, nwin, offsets, parts, mats, (rows,))
    if rounds % 2:
        result = jnp.concatenate([shifted(result[rest:], "row", 1), result[:rest]], 0)
    return result


def solution(mesh):
    placed = (P("row", "col"), P(), P(None, None, "row", "col", None))
    return jax.shard_map(
        shards, mesh=mesh, in_specs=placed, out_specs=P("row", "col"), check_vma=False
    )
```

```python
import functools

import jax
import jax.numpy as jnp
from jax import lax
from jax.experimental import pallas as pl
from jax.experimental.pallas import tpu as pltpu
from jax.sharding import PartitionSpec as P

WINDOW = 128
HALF = 2 * WINDOW
CORES = 2
VMEM_LIMIT = 24 * 1024 * 1024
VMEM = pl.BlockSpec(memory_space=pltpu.VMEM)
SMEM = pl.BlockSpec(memory_space=pltpu.SMEM)


def shifted(value, axis, by):
    devices = lax.axis_size(axis)
    return lax.ppermute(value, axis, [(i, (i + by) % devices) for i in range(devices)])


def swapped(value, bit):
    devices = lax.axis_size("col")
    return lax.ppermute(value, "col", [(i, i ^ bit) for i in range(devices)])


class Plan:
    def __init__(self, rounds, nwin):
        self.nwin = nwin
        self.phases = []
        for ph in range(rounds + 1):
            away = ph % 2 == 1
            entries = []
            self_carry = None
            if ph > 0:
                a, b = 2 * ph - 2, 2 * ph - 1
                if away:
                    entries += [(a, nwin - 1), None, (b, nwin - 1), (b, nwin)]
                    self_carry = (1, self.count(ph - 1) - 1)
                else:
                    entries += [(a, 1), (b, 0), (b, 1), None]
                    self_carry = (3, self.count(ph - 1) - (nwin - 1))
            if ph < rounds:
                base = 2 if away else 0
                for sweep in (2 * ph, 2 * ph + 1):
                    entries += [(sweep, base + k) for k in range(nwin - 1)]
            self.phases.append((entries, self_carry))
        groups = [[ph] for ph in range(rounds - 1)] + [[rounds - 1, rounds]]
        self.groups = []
        self.where = {}
        edge_at = 0
        for g, members in enumerate(groups):
            wanted = [w for ph in members for w in self.phases[ph][0] if w is not None]
            own = [w for w in wanted if w[1] < nwin]
            edge = [w for w in wanted if w[1] == nwin]
            place = 0
            for part in (own, edge):
                for i, w in enumerate(part):
                    self.where[w] = (g, place + i, place + len(part) + i // 2, i % 2)
                place += len(part) + (len(part) + 1) // 2
            own_tiles = len(own) + (len(own) + 1) // 2
            edge_tiles = place - own_tiles
            self.groups.append((own, edge, own_tiles, edge_tiles, edge_at))
            edge_at += edge_tiles
        self.edge_tiles = edge_at

    def count(self, ph):
        return len(self.phases[ph][0])


def pack_kernel(plan, offsets_ref, refl_ref, *outs):
    size = refl_ref.shape[-1] - WINDOW
    mine = refl_ref.shape[-2]

    def fill(out, at, windows):
        for i, (sweep, k) in enumerate(windows):
            out[at + i] = refl_ref[sweep // 2, sweep % 2, k, :, :WINDOW]
        at += len(windows)
        for i in range(0, len(windows), 2):
            halves = []
            for sweep, k in windows[i : i + 2]:
                halves.append(refl_ref[sweep // 2, sweep % 2, k, :, WINDOW:])
            if len(halves) == 1:
                halves.append(jnp.zeros((mine, size), jnp.float32))
            out[at + i // 2] = jnp.concatenate(halves, -1)

    for group, out in zip(plan.groups, outs):
        fill(out, 0, group[0])
    for group in plan.groups:
        if group[1]:
            fill(outs[-1], group[4], [(sweep, 0) for sweep, _ in group[1]])


def pack(plan, offsets, refl):
    mine = refl.shape[3]
    counts = [group[2] for group in plan.groups] + [plan.edge_tiles]
    return pl.pallas_call(
        functools.partial(pack_kernel, plan),
        out_shape=tuple(jax.ShapeDtypeStruct((n, mine, WINDOW), jnp.float32) for n in counts),
        in_specs=[SMEM, VMEM],
        out_specs=(VMEM,) * len(counts),
        compiler_params=pltpu.CompilerParams(vmem_limit_bytes=VMEM_LIMIT),
    )(offsets, refl)


def split(value):
    high = value.astype(jnp.bfloat16)
    return high, (value - high.astype(jnp.float32)).astype(jnp.bfloat16)


def fold(value):
    half = value.shape[1] // 2
    return value[:, :half] + value[:, half:]


def matrix_kernel(plan, ph, offsets_ref, *refs):
    entries, carry = plan.phases[ph]
    refs = list(refs)
    old_ref = refs.pop(0) if carry else None
    tiles = refs.pop()
    out_ref = refs.pop()
    parts = refs
    if len(parts) == 2:
        here = lax.axis_index("col")
        for m in range(parts[0].shape[0]):
            other = lax.bitwise_xor(here, m * CORES)
            tiles[other] = parts[0][m]
            tiles[lax.bitwise_xor(other, 1)] = parts[1][m]
    else:
        tiles = parts[0]
    size = tiles.shape[0] * tiles.shape[2]
    last = lax.axis_index("row") == lax.axis_size("row") - 1
    lane = lax.broadcasted_iota(jnp.int32, (size, WINDOW), 1)
    row_id = lax.broadcasted_iota(jnp.int32, (WINDOW, WINDOW), 0)
    col_id = lax.broadcasted_iota(jnp.int32, (WINDOW, WINDOW), 1)
    unit = jnp.where(row_id == col_id, 1.0, 0.0).astype(jnp.float32)
    for i, window in enumerate(entries):
        if window is None:
            out_ref[i] = old_ref[carry[1]]
            continue
        sweep, k = window
        _, vec_tile, fac_tile, side = plan.where[window]
        vectors = tiles[:, vec_tile].reshape(size, WINDOW)
        factors = tiles[:, fac_tile].reshape(size, WINDOW)
        if k == plan.nwin - 1:
            limit = jnp.where(last, WINDOW - offsets_ref[sweep // 2, sweep % 2], WINDOW)
            vectors = jnp.where(lane < limit, vectors, 0.0)
        rows_hi, rows_lo = split(vectors)
        pair = jnp.concatenate([rows_hi, rows_lo], 1)
        blank = jnp.zeros_like(pair)
        stack = [blank, pair, blank, pair] if side else [pair, blank, pair, blank]
        scaled = fold(jnp.dot(
            jnp.concatenate(split(factors), 1),
            jnp.concatenate(stack, 0),
            preferred_element_type=jnp.float32,
        ))
        pair = jnp.concatenate(split(scaled), 1)
        product = fold(lax.dot_general(
            jnp.concatenate([rows_hi, rows_lo], 0),
            jnp.concatenate([pair, pair], 0),
            (((0,), (0,)), ((), ())),
            preferred_element_type=jnp.float32,
        ))
        high, low = split(unit - product)
        out_ref[i] = jnp.concatenate([high, low], 1)


def matrices(plan, ph, offsets, before, parts):
    count = plan.count(ph)
    carried = (before,) if plan.phases[ph][1] else ()
    operands = [offsets, *carried, *parts]
    whole = (sum(part.shape[0] for part in parts),) + parts[0].shape[1:]
    return pl.pallas_call(
        functools.partial(matrix_kernel, plan, ph),
        out_shape=jax.ShapeDtypeStruct((count, WINDOW, 2 * WINDOW), jnp.bfloat16),
        in_specs=[SMEM] + [VMEM] * (len(operands) - 1),
        out_specs=VMEM,
        scratch_shapes=[pltpu.VMEM(whole, jnp.float32)],
        compiler_params=pltpu.CompilerParams(vmem_limit_bytes=VMEM_LIMIT),
        cost_estimate=pl.CostEstimate(
            flops=count * 12 * 64 * 128 * 192, bytes_accessed=count * 100000, transcendentals=0
        ),
    )(*operands)


def apply_windows(field, at, count, first, mats):
    rows = field[pl.ds(at, count * WINDOW), :]
    updated = []
    for k in range(count):
        pair = jnp.concatenate(split(rows[k * WINDOW : (k + 1) * WINDOW]), 1)
        both = jnp.dot(
            mats[first + k],
            jnp.concatenate([pair, pair], 0),
            preferred_element_type=jnp.float32,
        )
        updated.append(fold(both))
    field[pl.ds(at, count * WINDOW), :] = jnp.concatenate(updated, 0)


def phase_kernel(ph, rounds, nwin, nparts, offsets_ref, *refs):
    parts = refs[:nparts]
    mats = refs[nparts]
    outs = refs[nparts + 1 : -1]
    field = refs[-1]
    place = 0
    for part in parts:
        field[place : place + part.shape[0], :] = part[...]
        place += part.shape[0]
    at = 0
    if ph > 0:
        a = offsets_ref[ph - 1, 0]
        b = offsets_ref[ph - 1, 1]
        step = jnp.where(b < a, 1, 0)
        start = nwin - 3 if ph % 2 else 1
        apply_windows(field, a + WINDOW * start, 1, 0, mats)
        start = nwin - 4 if ph % 2 else 0
        apply_windows(field, b + WINDOW * (start + step), 2, 1 + step, mats)
        at = 4
    if ph < rounds:
        a = offsets_ref[ph, 0]
        b = offsets_ref[ph, 1]
        step = jnp.where(b < a, 1, 0)
        apply_windows(field, a, nwin - 1, at, mats)
        apply_windows(field, b + WINDOW * step, nwin - 2, at + nwin - 1 + step, mats)
    place = 0
    for out in outs:
        out[...] = field[place : place + out.shape[0], :]
        place += out.shape[0]


def phase(ph, rounds, nwin, offsets, parts, mats, sizes):
    rows = sum(part.shape[0] for part in parts)
    cols = parts[0].shape[1]
    operands = [offsets, *parts, mats]
    return pl.pallas_call(
        functools.partial(phase_kernel, ph, rounds, nwin, len(parts)),
        out_shape=tuple(jax.ShapeDtypeStruct((n, cols), jnp.float32) for n in sizes),
        in_specs=[SMEM] + [VMEM] * (len(operands) - 1),
        out_specs=(VMEM,) * len(sizes),
        scratch_shapes=[pltpu.VMEM((rows, cols), jnp.float32)],
        compiler_params=pltpu.CompilerParams(vmem_limit_bytes=VMEM_LIMIT),
        cost_estimate=pl.CostEstimate(
            flops=8 * 6 * WINDOW * WINDOW * cols, bytes_accessed=2000000, transcendentals=0
        ),
    )(*operands)


def after(value, earlier):
    return lax.optimization_barrier((value, earlier))[0]


class Gather:
    def __init__(self, plan, packed, size):
        self.plan = plan
        self.size = size
        *own, edge = packed
        devices = lax.axis_size("col")
        self.stepwise = edge.shape[1] % 8 == 0 and devices == 4 * CORES
        if self.stepwise:
            near = swapped(own[0], CORES)
            self.pairs = [jnp.stack([own[0], near])]
            self.fours = [self.double(self.pairs[0])]
        ahead = shifted(edge, "row", -1)
        self.own = []
        for (_, _, _, edge_tiles, edge_at), tiles in zip(plan.groups, own):
            if edge_tiles:
                tiles = jnp.concatenate([tiles, ahead[edge_at : edge_at + edge_tiles]], 0)
            self.own.append(tiles)
        if self.stepwise and len(self.own) > 1:
            near = self.spread(self.own[1:2], near)
            self.send(1, self.fours[0][1])
            if len(self.own) > 2:
                self.spread(self.own[2:], self.pairs[0])

    def spread(self, tiles, earlier):
        whole = after(jnp.concatenate(tiles, 0), earlier)
        near = swapped(whole, CORES)
        at = 0
        for part in tiles:
            self.pairs.append((whole, near, at, part.shape[0]))
            at += part.shape[0]
        return near

    def double(self, pair):
        return pair, swapped(pair, 2 * CORES)

    def send(self, g, earlier):
        if self.stepwise:
            whole, near, at, count = self.pairs[g]
            near = after(near, earlier)
            pair = jnp.stack([whole[at : at + count], near[at : at + count]])
            self.fours.append(self.double(pair))

    def receive(self, g, earlier=None):
        if self.stepwise:
            pieces = self.fours[g]
            if earlier is not None:
                pieces = after(pieces, earlier)
            same = jnp.concatenate(pieces, 0)
            return (same, swapped(same, 1))
        whole = lax.all_gather(self.own[g], "col", axis=0)
        whole = jnp.moveaxis(whole, 0, 1).reshape(1, whole.shape[1], self.size, WINDOW)
        return (whole,)


def shards(evecs, offsets, refl):
    rows = evecs.shape[0]
    nwin = rows // WINDOW
    rounds = refl.shape[0]
    size = refl.shape[4] - WINDOW
    plan = Plan(rounds, nwin)
    groups = len(plan.groups)
    gather = Gather(plan, pack(plan, offsets, refl), size)
    rest = rows - HALF
    parts = [evecs]
    mats = None
    result = None
    for ph in range(rounds):
        tiles = gather.receive(ph, result)
        mats = matrices(plan, ph, offsets, mats, tiles)
        away = ph % 2 == 1
        sizes = (rest, HALF) if away else (HALF, rest)
        halves = phase(ph, rounds, nwin, offsets, parts, mats, sizes)
        if away:
            result, kept = halves[1], halves[0]
            parts = [shifted(result, "row", 1), kept]
        else:
            result, kept = halves
            parts = [kept, shifted(result, "row", -1)]
        if ph + 2 < groups:
            gather.send(ph + 2, result)
    mats = matrices(plan, rounds, offsets, mats, tiles)
    (result,) = phase(rounds, rounds, nwin, offsets, parts, mats, (rows,))
    if rounds % 2:
        result = jnp.concatenate([shifted(result[rest:], "row", 1), result[:rest]], 0)
    return result


def solution(mesh):
    placed = (P("row", "col"), P(), P(None, None, "row", "col", None))
    return jax.shard_map(
        shards, mesh=mesh, in_specs=placed, out_specs=P("row", "col"), check_vma=False
    )
```

```python
import functools

import jax
import jax.numpy as jnp
from jax import lax
from jax.experimental import pallas as pl
from jax.experimental.pallas import tpu as pltpu
from jax.sharding import PartitionSpec as P

WINDOW = 128
HALF = 2 * WINDOW
CORES = 2
DIRECT = 2
VMEM_LIMIT = 24 * 1024 * 1024
VMEM = pl.BlockSpec(memory_space=pltpu.VMEM)


def shifted(value, axis, by):
    devices = lax.axis_size(axis)
    return lax.ppermute(value, axis, [(i, (i + by) % devices) for i in range(devices)])


def swapped(value, bit):
    devices = lax.axis_size("col")
    return lax.ppermute(value, "col", [(i, i ^ bit) for i in range(devices)])


class Plan:
    def __init__(self, rounds, nwin):
        self.nwin = nwin
        self.phases = []
        for ph in range(rounds + 1):
            away = ph % 2 == 1
            entries = []
            self_carry = None
            if ph > 0:
                a, b = 2 * ph - 2, 2 * ph - 1
                if away:
                    entries += [(a, nwin - 1), None, (b, nwin - 1), (b, nwin)]
                    self_carry = (1, self.count(ph - 1) - 1)
                else:
                    entries += [(a, 1), (b, 0), (b, 1), None]
                    self_carry = (3, self.count(ph - 1) - (nwin - 1))
            if ph < rounds:
                base = 2 if away else 0
                for sweep in (2 * ph, 2 * ph + 1):
                    entries += [(sweep, base + k) for k in range(nwin - 1)]
            self.phases.append((entries, self_carry))
        groups = [[ph] for ph in range(rounds - 1)] + [[rounds - 1, rounds]]
        self.groups = []
        self.where = {}
        edge_at = 0
        for g, members in enumerate(groups):
            wanted = [w for ph in members for w in self.phases[ph][0] if w is not None]
            own = [w for w in wanted if w[1] < nwin]
            edge = [w for w in wanted if w[1] == nwin]
            place = 0
            for part in (own, edge):
                for i, w in enumerate(part):
                    self.where[w] = (g, place + i, place + len(part) + i // 2, i % 2)
                place += len(part) + (len(part) + 1) // 2
            own_tiles = len(own) + (len(own) + 1) // 2
            edge_tiles = place - own_tiles
            self.groups.append((own, edge, own_tiles, edge_tiles, edge_at))
            edge_at += edge_tiles
        self.edge_tiles = edge_at

    def count(self, ph):
        return len(self.phases[ph][0])


def pack_kernel(plan, refl_ref, *outs):
    size = refl_ref.shape[-1] - WINDOW
    mine = refl_ref.shape[-2]

    def fill(out, at, windows):
        for i, (sweep, k) in enumerate(windows):
            out[at + i] = refl_ref[sweep // 2, sweep % 2, k, :, :WINDOW]
        at += len(windows)
        for i in range(0, len(windows), 2):
            halves = []
            for sweep, k in windows[i : i + 2]:
                halves.append(refl_ref[sweep // 2, sweep % 2, k, :, WINDOW:])
            if len(halves) == 1:
                halves.append(jnp.zeros((mine, size), jnp.float32))
            out[at + i // 2] = jnp.concatenate(halves, -1)

    for group, out in zip(plan.groups, outs):
        fill(out, 0, group[0])
    for group in plan.groups:
        if group[1]:
            fill(outs[-1], group[4], [(sweep, 0) for sweep, _ in group[1]])


def pack(plan, refl):
    mine = refl.shape[3]
    counts = [group[2] for group in plan.groups] + [plan.edge_tiles]
    return pl.pallas_call(
        functools.partial(pack_kernel, plan),
        out_shape=tuple(jax.ShapeDtypeStruct((n, mine, WINDOW), jnp.float32) for n in counts),
        in_specs=[VMEM],
        out_specs=(VMEM,) * len(counts),
        compiler_params=pltpu.CompilerParams(vmem_limit_bytes=VMEM_LIMIT),
    )(refl)


def split(value):
    high = value.astype(jnp.bfloat16)
    return high, (value - high.astype(jnp.float32)).astype(jnp.bfloat16)


def fold(value):
    half = value.shape[1] // 2
    return value[:, :half] + value[:, half:]


def matrix_kernel(plan, ph, offsets_ref, *refs):
    entries, carry = plan.phases[ph]
    refs = list(refs)
    old_ref = refs.pop(0) if carry else None
    tiles = refs.pop()
    out_ref = refs.pop()
    parts = refs
    if len(parts) == 2:
        here = lax.axis_index("col")
        for m in range(parts[0].shape[0]):
            other = lax.bitwise_xor(here, m * CORES)
            tiles[other] = parts[0][m]
            tiles[lax.bitwise_xor(other, 1)] = parts[1][m]
    else:
        tiles = parts[0]
    size = tiles.shape[0] * tiles.shape[2]
    offsets = offsets_ref[...]
    last = lax.axis_index("row") == lax.axis_size("row") - 1
    lane = lax.broadcasted_iota(jnp.int32, (size, WINDOW), 1)
    row_id = lax.broadcasted_iota(jnp.int32, (WINDOW, WINDOW), 0)
    col_id = lax.broadcasted_iota(jnp.int32, (WINDOW, WINDOW), 1)
    unit = jnp.where(row_id == col_id, 1.0, 0.0).astype(jnp.float32)
    for i, window in enumerate(entries):
        if window is None:
            out_ref[i] = old_ref[carry[1]]
            continue
        sweep, k = window
        _, vec_tile, fac_tile, side = plan.where[window]
        vectors = tiles[:, vec_tile].reshape(size, WINDOW)
        factors = tiles[:, fac_tile].reshape(size, WINDOW)
        if k == plan.nwin - 1:
            start = offsets[sweep % 2 : sweep % 2 + 1, sweep // 2 : sweep // 2 + 1]
            limit = jnp.where(last, WINDOW - start, WINDOW)
            vectors = jnp.where(lane < limit, vectors, 0.0)
        rows_hi, rows_lo = split(vectors)
        pair = jnp.concatenate([rows_hi, rows_lo], 1)
        blank = jnp.zeros_like(pair)
        stack = [blank, pair, blank, pair] if side else [pair, blank, pair, blank]
        scaled = fold(jnp.dot(
            jnp.concatenate(split(factors), 1),
            jnp.concatenate(stack, 0),
            preferred_element_type=jnp.float32,
        ))
        pair = jnp.concatenate(split(scaled), 1)
        product = fold(lax.dot_general(
            jnp.concatenate([rows_hi, rows_lo], 0),
            jnp.concatenate([pair, pair], 0),
            (((0,), (0,)), ((), ())),
            preferred_element_type=jnp.float32,
        ))
        high, low = split(unit - product)
        out_ref[i] = jnp.concatenate([high, low], 1)


def matrices(plan, ph, offsets, before, parts):
    count = plan.count(ph)
    carried = (before,) if plan.phases[ph][1] else ()
    operands = [offsets, *carried, *parts]
    whole = (sum(part.shape[0] for part in parts),) + parts[0].shape[1:]
    return pl.pallas_call(
        functools.partial(matrix_kernel, plan, ph),
        out_shape=jax.ShapeDtypeStruct((count, WINDOW, 2 * WINDOW), jnp.bfloat16),
        in_specs=[VMEM] * len(operands),
        out_specs=VMEM,
        scratch_shapes=[pltpu.VMEM(whole, jnp.float32)],
        compiler_params=pltpu.CompilerParams(vmem_limit_bytes=VMEM_LIMIT),
        cost_estimate=pl.CostEstimate(
            flops=count * 12 * 64 * 128 * 192, bytes_accessed=count * 100000, transcendentals=0
        ),
    )(*operands)


def apply_windows(field, at, count, first, mats):
    rows = field[pl.ds(at, count * WINDOW), :]
    updated = []
    for k in range(count):
        pair = jnp.concatenate(split(rows[k * WINDOW : (k + 1) * WINDOW]), 1)
        both = jnp.dot(
            mats[first + k],
            jnp.concatenate([pair, pair], 0),
            preferred_element_type=jnp.float32,
        )
        updated.append(fold(both))
    field[pl.ds(at, count * WINDOW), :] = jnp.concatenate(updated, 0)


def phase_kernel(ph, rounds, nwin, nparts, offsets_ref, *refs):
    parts = refs[:nparts]
    mats = refs[nparts]
    outs = refs[nparts + 1 : -1]
    field = refs[-1]
    place = 0
    for part in parts:
        field[place : place + part.shape[0], :] = part[...]
        place += part.shape[0]
    offsets = offsets_ref[...]
    at = 0
    if ph > 0:
        a, b = offsets[0, ph - 1], offsets[1, ph - 1]
        step = jnp.where(b < a, 1, 0)
        start = nwin - 3 if ph % 2 else 1
        apply_windows(field, a + WINDOW * start, 1, 0, mats)
        start = nwin - 4 if ph % 2 else 0
        apply_windows(field, b + WINDOW * (start + step), 2, 1 + step, mats)
        at = 4
    if ph < rounds:
        a, b = offsets[0, ph], offsets[1, ph]
        step = jnp.where(b < a, 1, 0)
        apply_windows(field, a, nwin - 1, at, mats)
        apply_windows(field, b + WINDOW * step, nwin - 2, at + nwin - 1 + step, mats)
    place = 0
    for out in outs:
        out[...] = field[place : place + out.shape[0], :]
        place += out.shape[0]


def phase(ph, rounds, nwin, offsets, parts, mats, sizes):
    rows = sum(part.shape[0] for part in parts)
    cols = parts[0].shape[1]
    operands = [offsets, *parts, mats]
    return pl.pallas_call(
        functools.partial(phase_kernel, ph, rounds, nwin, len(parts)),
        out_shape=tuple(jax.ShapeDtypeStruct((n, cols), jnp.float32) for n in sizes),
        in_specs=[VMEM] * len(operands),
        out_specs=(VMEM,) * len(sizes),
        scratch_shapes=[pltpu.VMEM((rows, cols), jnp.float32)],
        compiler_params=pltpu.CompilerParams(vmem_limit_bytes=VMEM_LIMIT),
        cost_estimate=pl.CostEstimate(
            flops=8 * 6 * WINDOW * WINDOW * cols, bytes_accessed=2000000, transcendentals=0
        ),
    )(*operands)


def after(value, earlier):
    return lax.optimization_barrier((value, earlier))[0]


class Gather:
    def __init__(self, plan, packed, size):
        self.plan = plan
        self.size = size
        *own, edge = packed
        devices = lax.axis_size("col")
        self.chips = devices // CORES
        self.stepwise = edge.shape[1] % 8 == 0 and devices == 4 * CORES
        self.held = {}
        self.pairs = {}
        if self.stepwise:
            self.direct(0, own[0])
        ahead = shifted(edge, "row", -1)
        self.own = []
        for (_, _, _, edge_tiles, edge_at), tiles in zip(plan.groups, own):
            if edge_tiles:
                tiles = jnp.concatenate([tiles, ahead[edge_at : edge_at + edge_tiles]], 0)
            self.own.append(tiles)
        if self.stepwise:
            for g in range(1, min(DIRECT, len(own))):
                self.direct(g, self.own[g])
            if len(own) > DIRECT:
                self.spread(DIRECT, self.held[0][-1])

    def direct(self, g, tiles):
        others = [swapped(tiles, CORES * m) for m in range(1, self.chips)]
        self.held[g] = [part.reshape((1,) + tiles.shape) for part in [tiles] + others]

    def spread(self, first, earlier):
        groups = range(first, len(self.own))
        whole = after(jnp.concatenate([self.own[g] for g in groups], 0), earlier)
        near = swapped(whole, CORES)
        at = 0
        for g in groups:
            self.pairs[g] = (whole, near, at, self.own[g].shape[0])
            at += self.own[g].shape[0]

    def send(self, g, earlier):
        if g in self.pairs:
            whole, near, at, count = self.pairs[g]
            near = after(near, earlier)
            pair = jnp.stack([whole[at : at + count], near[at : at + count]])
            far = swapped(pair, 2 * CORES)
            self.held[g] = [pair, far]

    def receive(self, g, earlier=None):
        if self.stepwise:
            pieces = self.held[g]
            if earlier is not None:
                pieces = after(pieces, earlier)
            same = jnp.concatenate(pieces, 0)
            return (same, swapped(same, 1))
        whole = lax.all_gather(self.own[g], "col", axis=0)
        whole = jnp.moveaxis(whole, 0, 1).reshape(1, whole.shape[1], self.size, WINDOW)
        return (whole,)


def shards(evecs, offsets, refl):
    rows = evecs.shape[0]
    nwin = rows // WINDOW
    rounds = refl.shape[0]
    size = refl.shape[4] - WINDOW
    plan = Plan(rounds, nwin)
    offsets = offsets.T
    groups = len(plan.groups)
    gather = Gather(plan, pack(plan, refl), size)
    rest = rows - HALF
    parts = [evecs]
    mats = None
    result = None
    for ph in range(rounds):
        tiles = gather.receive(ph, result)
        mats = matrices(plan, ph, offsets, mats, tiles)
        away = ph % 2 == 1
        sizes = (rest, HALF) if away else (HALF, rest)
        halves = phase(ph, rounds, nwin, offsets, parts, mats, sizes)
        if away:
            result, kept = halves[1], halves[0]
            parts = [shifted(result, "row", 1), kept]
        else:
            result, kept = halves
            parts = [kept, shifted(result, "row", -1)]
        if ph + 2 < groups:
            gather.send(ph + 2, result)
    mats = matrices(plan, rounds, offsets, mats, tiles)
    (result,) = phase(rounds, rounds, nwin, offsets, parts, mats, (rows,))
    if rounds % 2:
        result = jnp.concatenate([shifted(result[rest:], "row", 1), result[:rest]], 0)
    return result


def solution(mesh):
    placed = (P("row", "col"), P(), P(None, None, "row", "col", None))
    return jax.shard_map(
        shards, mesh=mesh, in_specs=placed, out_specs=P("row", "col"), check_vma=False
    )
```

```python
import functools

import jax
import jax.numpy as jnp
from jax import lax
from jax.experimental import pallas as pl
from jax.experimental.pallas import tpu as pltpu
from jax.sharding import PartitionSpec as P

WINDOW = 128
HALF = 2 * WINDOW
CORES = 2
VMEM_LIMIT = 24 * 1024 * 1024
VMEM = pl.BlockSpec(memory_space=pltpu.VMEM)


def shifted(value, axis, by):
    devices = lax.axis_size(axis)
    return lax.ppermute(value, axis, [(i, (i + by) % devices) for i in range(devices)])


def swapped(value, bit):
    devices = lax.axis_size("col")
    return lax.ppermute(value, "col", [(i, i ^ bit) for i in range(devices)])


class Plan:
    def __init__(self, rounds, nwin):
        self.nwin = nwin
        self.phases = []
        for ph in range(rounds + 1):
            away = ph % 2 == 1
            entries = []
            self_carry = None
            if ph > 0:
                a, b = 2 * ph - 2, 2 * ph - 1
                if away:
                    entries += [(a, nwin - 1), None, (b, nwin - 1), (b, nwin)]
                    self_carry = (1, self.count(ph - 1) - 1)
                else:
                    entries += [(a, 1), (b, 0), (b, 1), None]
                    self_carry = (3, self.count(ph - 1) - (nwin - 1))
            if ph < rounds:
                base = 2 if away else 0
                for sweep in (2 * ph, 2 * ph + 1):
                    entries += [(sweep, base + k) for k in range(nwin - 1)]
            self.phases.append((entries, self_carry))
        groups = [[0], [1], list(range(2, rounds + 1))]
        self.groups = []
        self.where = {}
        edge_at = 0
        for g, members in enumerate(groups):
            wanted = [w for ph in members for w in self.phases[ph][0] if w is not None]
            own = [w for w in wanted if w[1] < nwin]
            edge = [w for w in wanted if w[1] == nwin]
            place = 0
            for part in (own, edge):
                for i, w in enumerate(part):
                    self.where[w] = (g, place + i, place + len(part) + i // 2, i % 2)
                place += len(part) + (len(part) + 1) // 2
            own_tiles = len(own) + (len(own) + 1) // 2
            edge_tiles = place - own_tiles
            self.groups.append((own, edge, own_tiles, edge_tiles, edge_at))
            edge_at += edge_tiles
        self.edge_tiles = edge_at

    def count(self, ph):
        return len(self.phases[ph][0])


def pack_kernel(plan, offsets_ref, refl_ref, *outs):
    size = refl_ref.shape[-1] - WINDOW
    mine = refl_ref.shape[-2]

    def fill(out, at, windows):
        for i, (sweep, k) in enumerate(windows):
            out[at + i] = refl_ref[sweep // 2, sweep % 2, k, :, :WINDOW]
        at += len(windows)
        for i in range(0, len(windows), 2):
            halves = []
            for sweep, k in windows[i : i + 2]:
                halves.append(refl_ref[sweep // 2, sweep % 2, k, :, WINDOW:])
            if len(halves) == 1:
                halves.append(jnp.zeros((mine, size), jnp.float32))
            out[at + i // 2] = jnp.concatenate(halves, -1)

    for group, out in zip(plan.groups, outs):
        fill(out, 0, group[0])
    for group in plan.groups:
        if group[1]:
            fill(outs[-1], group[4], [(sweep, 0) for sweep, _ in group[1]])


def pack(plan, offsets, refl):
    mine = refl.shape[3]
    counts = [group[2] for group in plan.groups] + [plan.edge_tiles]
    return pl.pallas_call(
        functools.partial(pack_kernel, plan),
        out_shape=tuple(jax.ShapeDtypeStruct((n, mine, WINDOW), jnp.float32) for n in counts),
        in_specs=[VMEM, VMEM],
        out_specs=(VMEM,) * len(counts),
        compiler_params=pltpu.CompilerParams(vmem_limit_bytes=VMEM_LIMIT),
    )(offsets, refl)


def split(value):
    high = value.astype(jnp.bfloat16)
    return high, (value - high.astype(jnp.float32)).astype(jnp.bfloat16)


def fold(value):
    half = value.shape[1] // 2
    return value[:, :half] + value[:, half:]


def matrix_kernel(plan, ph, offsets_ref, *refs):
    entries, carry = plan.phases[ph]
    refs = list(refs)
    old_ref = refs.pop(0) if carry else None
    tiles = refs.pop()
    out_ref = refs.pop()
    parts = refs
    if len(parts) == 2:
        here = lax.axis_index("col")
        for m in range(parts[0].shape[0]):
            other = lax.bitwise_xor(here, m * CORES)
            tiles[other] = parts[0][m]
            tiles[lax.bitwise_xor(other, 1)] = parts[1][m]
    else:
        tiles = parts[0]
    size = tiles.shape[0] * tiles.shape[2]
    offsets = offsets_ref[...]
    last = lax.axis_index("row") == lax.axis_size("row") - 1
    lane = lax.broadcasted_iota(jnp.int32, (size, WINDOW), 1)
    row_id = lax.broadcasted_iota(jnp.int32, (WINDOW, WINDOW), 0)
    col_id = lax.broadcasted_iota(jnp.int32, (WINDOW, WINDOW), 1)
    unit = jnp.where(row_id == col_id, 1.0, 0.0).astype(jnp.float32)
    for i, window in enumerate(entries):
        if window is None:
            out_ref[i] = old_ref[carry[1]]
            continue
        sweep, k = window
        _, vec_tile, fac_tile, side = plan.where[window]
        vectors = tiles[:, vec_tile].reshape(size, WINDOW)
        factors = tiles[:, fac_tile].reshape(size, WINDOW)
        if k == plan.nwin - 1:
            start = offsets[sweep % 2 : sweep % 2 + 1, sweep // 2 : sweep // 2 + 1]
            limit = jnp.where(last, WINDOW - start, WINDOW)
            vectors = jnp.where(lane < limit, vectors, 0.0)
        rows_hi, rows_lo = split(vectors)
        pair = jnp.concatenate([rows_hi, rows_lo], 1)
        blank = jnp.zeros_like(pair)
        stack = [blank, pair, blank, pair] if side else [pair, blank, pair, blank]
        scaled = fold(jnp.dot(
            jnp.concatenate(split(factors), 1),
            jnp.concatenate(stack, 0),
            preferred_element_type=jnp.float32,
        ))
        pair = jnp.concatenate(split(scaled), 1)
        product = fold(lax.dot_general(
            jnp.concatenate([rows_hi, rows_lo], 0),
            jnp.concatenate([pair, pair], 0),
            (((0,), (0,)), ((), ())),
            preferred_element_type=jnp.float32,
        ))
        high, low = split(unit - product)
        out_ref[i] = jnp.concatenate([high, low], 1)


def matrices(plan, ph, offsets, before, parts):
    count = plan.count(ph)
    carried = (before,) if plan.phases[ph][1] else ()
    operands = [offsets, *carried, *parts]
    whole = (sum(part.shape[0] for part in parts),) + parts[0].shape[1:]
    return pl.pallas_call(
        functools.partial(matrix_kernel, plan, ph),
        out_shape=jax.ShapeDtypeStruct((count, WINDOW, 2 * WINDOW), jnp.bfloat16),
        in_specs=[VMEM] * len(operands),
        out_specs=VMEM,
        scratch_shapes=[pltpu.VMEM(whole, jnp.float32)],
        compiler_params=pltpu.CompilerParams(vmem_limit_bytes=VMEM_LIMIT),
        cost_estimate=pl.CostEstimate(
            flops=count * 12 * 64 * 128 * 192, bytes_accessed=count * 100000, transcendentals=0
        ),
    )(*operands)


def apply_windows(field, at, count, first, mats):
    rows = field[pl.ds(at, count * WINDOW), :]
    updated = []
    for k in range(count):
        pair = jnp.concatenate(split(rows[k * WINDOW : (k + 1) * WINDOW]), 1)
        both = jnp.dot(
            mats[first + k],
            jnp.concatenate([pair, pair], 0),
            preferred_element_type=jnp.float32,
        )
        updated.append(fold(both))
    field[pl.ds(at, count * WINDOW), :] = jnp.concatenate(updated, 0)


def phase_kernel(ph, rounds, nwin, nparts, offsets_ref, *refs):
    parts = refs[:nparts]
    mats = refs[nparts]
    outs = refs[nparts + 1 : -1]
    field = refs[-1]
    place = 0
    for part in parts:
        field[place : place + part.shape[0], :] = part[...]
        place += part.shape[0]
    offsets = offsets_ref[...]
    at = 0
    if ph > 0:
        a, b = offsets[0, ph - 1], offsets[1, ph - 1]
        step = jnp.where(b < a, 1, 0)
        start = nwin - 3 if ph % 2 else 1
        apply_windows(field, a + WINDOW * start, 1, 0, mats)
        start = nwin - 4 if ph % 2 else 0
        apply_windows(field, b + WINDOW * (start + step), 2, 1 + step, mats)
        at = 4
    if ph < rounds:
        a, b = offsets[0, ph], offsets[1, ph]
        step = jnp.where(b < a, 1, 0)
        apply_windows(field, a, nwin - 1, at, mats)
        apply_windows(field, b + WINDOW * step, nwin - 2, at + nwin - 1 + step, mats)
    place = 0
    for out in outs:
        out[...] = field[place : place + out.shape[0], :]
        place += out.shape[0]


def phase(ph, rounds, nwin, offsets, parts, mats, sizes):
    rows = sum(part.shape[0] for part in parts)
    cols = parts[0].shape[1]
    operands = [offsets, *parts, mats]
    return pl.pallas_call(
        functools.partial(phase_kernel, ph, rounds, nwin, len(parts)),
        out_shape=tuple(jax.ShapeDtypeStruct((n, cols), jnp.float32) for n in sizes),
        in_specs=[VMEM] * len(operands),
        out_specs=(VMEM,) * len(sizes),
        scratch_shapes=[pltpu.VMEM((rows, cols), jnp.float32)],
        compiler_params=pltpu.CompilerParams(vmem_limit_bytes=VMEM_LIMIT),
        cost_estimate=pl.CostEstimate(
            flops=8 * 6 * WINDOW * WINDOW * cols, bytes_accessed=2000000, transcendentals=0
        ),
    )(*operands)


def after(value, earlier):
    return lax.optimization_barrier((value, earlier))[0]


class Gather:
    def __init__(self, plan, packed, size):
        self.plan = plan
        self.size = size
        *own, edge = packed
        devices = lax.axis_size("col")
        self.chips = devices // CORES
        self.stepwise = edge.shape[1] % 8 == 0 and devices == 4 * CORES
        self.held = {}
        if self.stepwise:
            self.direct(0, own[0])
        ahead = shifted(edge, "row", -1)
        self.own = []
        for (_, _, _, edge_tiles, edge_at), tiles in zip(plan.groups, own):
            if edge_tiles:
                tiles = jnp.concatenate([tiles, ahead[edge_at : edge_at + edge_tiles]], 0)
            self.own.append(tiles)
        self.send(1)

    def direct(self, g, tiles):
        others = [swapped(tiles, CORES * m) for m in range(1, self.chips)]
        self.held[g] = [part.reshape((1,) + tiles.shape) for part in [tiles] + others]

    def send(self, g, earlier=None):
        if self.stepwise and g < len(self.own):
            tiles = self.own[g]
            self.direct(g, tiles if earlier is None else after(tiles, earlier))

    def receive(self, g, earlier=None):
        if self.stepwise:
            pieces = self.held[g]
            if earlier is not None:
                pieces = after(pieces, earlier)
            same = jnp.concatenate(pieces, 0)
            return (same, swapped(same, 1))
        whole = lax.all_gather(self.own[g], "col", axis=0)
        whole = jnp.moveaxis(whole, 0, 1).reshape(1, whole.shape[1], self.size, WINDOW)
        return (whole,)


def shards(evecs, offsets, refl):
    rows = evecs.shape[0]
    nwin = rows // WINDOW
    rounds = refl.shape[0]
    size = refl.shape[4] - WINDOW
    plan = Plan(rounds, nwin)
    offsets = offsets.T
    groups = len(plan.groups)
    gather = Gather(plan, pack(plan, offsets, refl), size)
    rest = rows - HALF
    parts = [evecs]
    mats = None
    result = None
    gather.send(2)
    for ph in range(rounds):
        if ph < groups:
            tiles = gather.receive(ph, parts if ph > 1 else result)
        mats = matrices(plan, ph, offsets, mats, tiles)
        away = ph % 2 == 1
        sizes = (rest, HALF) if away else (HALF, rest)
        halves = phase(ph, rounds, nwin, offsets, parts, mats, sizes)
        result, kept = (halves[1], halves[0]) if away else halves
        moved = shifted(result, "row", 1 if away else -1)
        parts = [moved, kept] if away else [kept, moved]
    mats = matrices(plan, rounds, offsets, mats, tiles)
    (result,) = phase(rounds, rounds, nwin, offsets, parts, mats, (rows,))
    if rounds % 2:
        result = jnp.concatenate([shifted(result[rest:], "row", 1), result[:rest]], 0)
    return result


def solution(mesh):
    placed = (P("row", "col"), P(), P(None, None, "row", "col", None))
    return jax.shard_map(
        shards, mesh=mesh, in_specs=placed, out_specs=P("row", "col"), check_vma=False
    )
```

```python
import functools

import jax
import jax.numpy as jnp
from jax import lax
from jax.experimental import pallas as pl
from jax.experimental.pallas import tpu as pltpu
from jax.sharding import PartitionSpec as P

WINDOW = 128
HALF = 2 * WINDOW
CORES = 2
VMEM_LIMIT = 24 * 1024 * 1024
VMEM = pl.BlockSpec(memory_space=pltpu.VMEM)


def shifted(value, axis, by):
    devices = lax.axis_size(axis)
    return lax.ppermute(value, axis, [(i, (i + by) % devices) for i in range(devices)])


def swapped(value, bit):
    devices = lax.axis_size("col")
    return lax.ppermute(value, "col", [(i, i ^ bit) for i in range(devices)])


class Plan:
    def __init__(self, rounds, nwin):
        self.nwin = nwin
        self.phases = []
        for ph in range(rounds + 1):
            away = ph % 2 == 1
            entries = []
            self_carry = None
            if ph > 0:
                a, b = 2 * ph - 2, 2 * ph - 1
                if away:
                    entries += [(a, nwin - 1), None, (b, nwin - 1), (b, nwin)]
                    self_carry = (1, self.count(ph - 1) - 1)
                else:
                    entries += [(a, 1), (b, 0), (b, 1), None]
                    self_carry = (3, self.count(ph - 1) - (nwin - 1))
            if ph < rounds:
                base = 2 if away else 0
                for sweep in (2 * ph, 2 * ph + 1):
                    entries += [(sweep, base + k) for k in range(nwin - 1)]
            self.phases.append((entries, self_carry))
        groups = [[0], [1], list(range(2, rounds + 1))]
        self.groups = []
        self.where = {}
        edge_at = 0
        for g, members in enumerate(groups):
            wanted = [w for ph in members for w in self.phases[ph][0] if w is not None]
            own = [w for w in wanted if w[1] < nwin]
            edge = [w for w in wanted if w[1] == nwin]
            place = 0
            for part in (own, edge):
                for i, w in enumerate(part):
                    self.where[w] = (g, place + i, place + len(part) + i // 2, i % 2)
                place += len(part) + (len(part) + 1) // 2
            own_tiles = len(own) + (len(own) + 1) // 2
            edge_tiles = place - own_tiles
            self.groups.append((own, edge, own_tiles, edge_tiles, edge_at))
            edge_at += edge_tiles
        self.edge_tiles = edge_at

    def count(self, ph):
        return len(self.phases[ph][0])


def pack_kernel(plan, refl_ref, *outs):
    size = refl_ref.shape[-1] - WINDOW
    mine = refl_ref.shape[-2]

    def fill(out, at, windows):
        for i, (sweep, k) in enumerate(windows):
            out[at + i] = refl_ref[sweep // 2, sweep % 2, k, :, :WINDOW]
        at += len(windows)
        for i in range(0, len(windows), 2):
            halves = []
            for sweep, k in windows[i : i + 2]:
                halves.append(refl_ref[sweep // 2, sweep % 2, k, :, WINDOW:])
            if len(halves) == 1:
                halves.append(jnp.zeros((mine, size), jnp.float32))
            out[at + i // 2] = jnp.concatenate(halves, -1)

    for group, out in zip(plan.groups, outs):
        fill(out, 0, group[0])
    for group in plan.groups:
        if group[1]:
            fill(outs[-1], group[4], [(sweep, 0) for sweep, _ in group[1]])


def pack(plan, refl):
    mine = refl.shape[3]
    counts = [group[2] for group in plan.groups] + [plan.edge_tiles]
    return pl.pallas_call(
        functools.partial(pack_kernel, plan),
        out_shape=tuple(jax.ShapeDtypeStruct((n, mine, WINDOW), jnp.float32) for n in counts),
        in_specs=[VMEM],
        out_specs=(VMEM,) * len(counts),
        compiler_params=pltpu.CompilerParams(vmem_limit_bytes=VMEM_LIMIT),
    )(refl)


def split(value):
    high = value.astype(jnp.bfloat16)
    return high, (value - high.astype(jnp.float32)).astype(jnp.bfloat16)


def fold(value):
    half = value.shape[1] // 2
    return value[:, :half] + value[:, half:]


def matrix_kernel(plan, ph, masked, *refs):
    entries, carry = plan.phases[ph]
    operands = list(refs)
    refs = operands[1:] if masked else operands
    offsets = operands[0][...] if masked else None
    old_ref = refs.pop(0) if carry else None
    tiles = refs.pop()
    out_ref = refs.pop()
    parts = refs
    if len(parts) == 2:
        here = lax.axis_index("col")
        for m in range(parts[0].shape[0]):
            other = lax.bitwise_xor(here, m * CORES)
            tiles[other] = parts[0][m]
            tiles[lax.bitwise_xor(other, 1)] = parts[1][m]
    else:
        tiles = parts[0]
    size = tiles.shape[0] * tiles.shape[2]
    last = lax.axis_index("row") == lax.axis_size("row") - 1
    lane = lax.broadcasted_iota(jnp.int32, (size, WINDOW), 1)
    row_id = lax.broadcasted_iota(jnp.int32, (WINDOW, WINDOW), 0)
    col_id = lax.broadcasted_iota(jnp.int32, (WINDOW, WINDOW), 1)
    unit = jnp.where(row_id == col_id, 1.0, 0.0).astype(jnp.float32)
    for i, window in enumerate(entries):
        if window is None:
            out_ref[i] = old_ref[carry[1]]
            continue
        sweep, k = window
        _, vec_tile, fac_tile, side = plan.where[window]
        vectors = tiles[:, vec_tile].reshape(size, WINDOW)
        factors = tiles[:, fac_tile].reshape(size, WINDOW)
        if k == plan.nwin - 1:
            start = offsets[sweep % 2 : sweep % 2 + 1, sweep // 2 : sweep // 2 + 1]
            limit = jnp.where(last, WINDOW - start, WINDOW)
            vectors = jnp.where(lane < limit, vectors, 0.0)
        rows_hi, rows_lo = split(vectors)
        pair = jnp.concatenate([rows_hi, rows_lo], 1)
        blank = jnp.zeros_like(pair)
        stack = [blank, pair, blank, pair] if side else [pair, blank, pair, blank]
        scaled = fold(jnp.dot(
            jnp.concatenate(split(factors), 1),
            jnp.concatenate(stack, 0),
            preferred_element_type=jnp.float32,
        ))
        pair = jnp.concatenate(split(scaled), 1)
        product = fold(lax.dot_general(
            jnp.concatenate([rows_hi, rows_lo], 0),
            jnp.concatenate([pair, pair], 0),
            (((0,), (0,)), ((), ())),
            preferred_element_type=jnp.float32,
        ))
        high, low = split(unit - product)
        out_ref[i] = jnp.concatenate([high, low], 1)


def matrices(plan, ph, offsets, before, parts):
    count = plan.count(ph)
    carried = (before,) if plan.phases[ph][1] else ()
    masked = any(w is not None and w[1] == plan.nwin - 1 for w in plan.phases[ph][0])
    operands = [*([offsets] if masked else []), *carried, *parts]
    whole = (sum(part.shape[0] for part in parts),) + parts[0].shape[1:]
    return pl.pallas_call(
        functools.partial(matrix_kernel, plan, ph, masked),
        out_shape=jax.ShapeDtypeStruct((count, WINDOW, 2 * WINDOW), jnp.bfloat16),
        in_specs=[VMEM] * len(operands),
        out_specs=VMEM,
        scratch_shapes=[pltpu.VMEM(whole, jnp.float32)],
        compiler_params=pltpu.CompilerParams(vmem_limit_bytes=VMEM_LIMIT),
        cost_estimate=pl.CostEstimate(
            flops=count * 12 * 64 * 128 * 192, bytes_accessed=count * 100000, transcendentals=0
        ),
    )(*operands)


def apply_windows(field, at, count, first, mats):
    rows = field[pl.ds(at, count * WINDOW), :]
    updated = []
    for k in range(count):
        pair = jnp.concatenate(split(rows[k * WINDOW : (k + 1) * WINDOW]), 1)
        both = jnp.dot(
            mats[first + k],
            jnp.concatenate([pair, pair], 0),
            preferred_element_type=jnp.float32,
        )
        updated.append(fold(both))
    field[pl.ds(at, count * WINDOW), :] = jnp.concatenate(updated, 0)


def phase_kernel(ph, rounds, nwin, nparts, offsets_ref, *refs):
    parts = refs[:nparts]
    mats = refs[nparts]
    outs = refs[nparts + 1 : -1]
    field = refs[-1]
    place = 0
    for part in parts:
        field[place : place + part.shape[0], :] = part[...]
        place += part.shape[0]
    offsets = offsets_ref[...]
    at = 0
    if ph > 0:
        a, b = offsets[0, ph - 1], offsets[1, ph - 1]
        step = jnp.where(b < a, 1, 0)
        start = nwin - 3 if ph % 2 else 1
        apply_windows(field, a + WINDOW * start, 1, 0, mats)
        start = nwin - 4 if ph % 2 else 0
        apply_windows(field, b + WINDOW * (start + step), 2, 1 + step, mats)
        at = 4
    if ph < rounds:
        a, b = offsets[0, ph], offsets[1, ph]
        step = jnp.where(b < a, 1, 0)
        apply_windows(field, a, nwin - 1, at, mats)
        apply_windows(field, b + WINDOW * step, nwin - 2, at + nwin - 1 + step, mats)
    place = 0
    for out in outs:
        out[...] = field[place : place + out.shape[0], :]
        place += out.shape[0]


def phase(ph, rounds, nwin, offsets, parts, mats, sizes):
    rows = sum(part.shape[0] for part in parts)
    cols = parts[0].shape[1]
    operands = [offsets, *parts, mats]
    return pl.pallas_call(
        functools.partial(phase_kernel, ph, rounds, nwin, len(parts)),
        out_shape=tuple(jax.ShapeDtypeStruct((n, cols), jnp.float32) for n in sizes),
        in_specs=[VMEM] * len(operands),
        out_specs=(VMEM,) * len(sizes),
        scratch_shapes=[pltpu.VMEM((rows, cols), jnp.float32)],
        compiler_params=pltpu.CompilerParams(vmem_limit_bytes=VMEM_LIMIT),
        cost_estimate=pl.CostEstimate(
            flops=8 * 6 * WINDOW * WINDOW * cols, bytes_accessed=2000000, transcendentals=0
        ),
    )(*operands)


def after(value, earlier):
    return lax.optimization_barrier((value, earlier))[0]


class Gather:
    def __init__(self, plan, packed, size):
        self.plan = plan
        self.size = size
        *own, edge = packed
        devices = lax.axis_size("col")
        self.chips = devices // CORES
        self.stepwise = edge.shape[1] % 8 == 0 and devices == 4 * CORES
        self.held = {}
        if self.stepwise:
            self.direct(0, own[0])
        ahead = shifted(edge, "row", -1)
        self.own = []
        for (_, _, _, edge_tiles, edge_at), tiles in zip(plan.groups, own):
            if edge_tiles:
                tiles = jnp.concatenate([tiles, ahead[edge_at : edge_at + edge_tiles]], 0)
            self.own.append(tiles)
        if self.stepwise:
            self.doubled(1, self.own[1], self.held[0][-1])

    def direct(self, g, tiles):
        others = [swapped(tiles, CORES * m) for m in range(1, self.chips)]
        self.held[g] = [part.reshape((1,) + tiles.shape) for part in [tiles] + others]

    def doubled(self, g, tiles, earlier=None):
        pair = (tiles, swapped(tiles, CORES))
        pair = jnp.stack(pair if earlier is None else after(pair, earlier))
        self.held[g] = [pair, swapped(pair, 2 * CORES)]

    def send(self, g, earlier=None):
        if self.stepwise and g < len(self.own):
            tiles = self.own[g]
            self.direct(g, tiles if earlier is None else after(tiles, earlier))

    def receive(self, g, earlier=None):
        if self.stepwise:
            pieces = self.held[g]
            if earlier is not None:
                pieces = after(pieces, earlier)
            same = jnp.concatenate(pieces, 0)
            return (same, swapped(same, 1))
        whole = lax.all_gather(self.own[g], "col", axis=0)
        whole = jnp.moveaxis(whole, 0, 1).reshape(1, whole.shape[1], self.size, WINDOW)
        return (whole,)


def shards(evecs, offsets, refl):
    rows = evecs.shape[0]
    nwin = rows // WINDOW
    rounds = refl.shape[0]
    size = refl.shape[4] - WINDOW
    plan = Plan(rounds, nwin)
    offsets = offsets.T
    groups = len(plan.groups)
    gather = Gather(plan, pack(plan, refl), size)
    rest = rows - HALF
    parts = [evecs]
    mats = None
    result = None
    gather.send(2)
    for ph in range(rounds):
        if ph < groups:
            tiles = gather.receive(ph, parts if ph > 1 else result)
        mats = matrices(plan, ph, offsets, mats, tiles)
        away = ph % 2 == 1
        sizes = (rest, HALF) if away else (HALF, rest)
        halves = phase(ph, rounds, nwin, offsets, parts, mats, sizes)
        result, kept = (halves[1], halves[0]) if away else halves
        moved = shifted(result, "row", 1 if away else -1)
        parts = [moved, kept] if away else [kept, moved]
    mats = matrices(plan, rounds, offsets, mats, tiles)
    (result,) = phase(rounds, rounds, nwin, offsets, parts, mats, (rows,))
    if rounds % 2:
        result = jnp.concatenate([shifted(result[rest:], "row", 1), result[:rest]], 0)
    return result


def solution(mesh):
    placed = (P("row", "col"), P(), P(None, None, "row", "col", None))
    return jax.shard_map(
        shards, mesh=mesh, in_specs=placed, out_specs=P("row", "col"), check_vma=False
    )
```

```python
import functools

import jax
import jax.numpy as jnp
from jax import lax
from jax.experimental import pallas as pl
from jax.experimental.pallas import tpu as pltpu
from jax.sharding import PartitionSpec as P

WINDOW = 128
HALF = 2 * WINDOW
CORES = 2
VMEM_LIMIT = 24 * 1024 * 1024
VMEM = pl.BlockSpec(memory_space=pltpu.VMEM)


def shifted(value, axis, by):
    devices = lax.axis_size(axis)
    return lax.ppermute(value, axis, [(i, (i + by) % devices) for i in range(devices)])


def swapped(value, bit):
    devices = lax.axis_size("col")
    return lax.ppermute(value, "col", [(i, i ^ bit) for i in range(devices)])


class Plan:
    def __init__(self, rounds, nwin):
        self.nwin = nwin
        self.phases = []
        for ph in range(rounds + 1):
            away = ph % 2 == 1
            entries = []
            self_carry = None
            if ph > 0:
                a, b = 2 * ph - 2, 2 * ph - 1
                if away:
                    entries += [(a, nwin - 1), None, (b, nwin - 1), (b, nwin)]
                    self_carry = (1, self.count(ph - 1) - 1)
                else:
                    entries += [(a, 1), (b, 0), (b, 1), None]
                    self_carry = (3, self.count(ph - 1) - (nwin - 1))
            if ph < rounds:
                base = 2 if away else 0
                for sweep in (2 * ph, 2 * ph + 1):
                    entries += [(sweep, base + k) for k in range(nwin - 1)]
            self.phases.append((entries, self_carry))
        groups = [[ph] for ph in range(rounds - 1)] + [[rounds - 1, rounds]]
        self.groups = []
        self.where = {}
        edge_at = 0
        for g, members in enumerate(groups):
            wanted = [w for ph in members for w in self.phases[ph][0] if w is not None]
            own = [w for w in wanted if w[1] < nwin]
            edge = [w for w in wanted if w[1] == nwin]
            place = 0
            for part in (own, edge):
                for i, w in enumerate(part):
                    self.where[w] = (g, place + i, place + len(part) + i // 2, i % 2)
                place += len(part) + (len(part) + 1) // 2
            own_tiles = len(own) + (len(own) + 1) // 2
            edge_tiles = place - own_tiles
            self.groups.append((own, edge, own_tiles, edge_tiles, edge_at))
            edge_at += edge_tiles
        self.edge_tiles = edge_at

    def count(self, ph):
        return len(self.phases[ph][0])


def pack_kernel(plan, refl_ref, *outs):
    size = refl_ref.shape[-1] - WINDOW
    mine = refl_ref.shape[-2]

    def fill(out, at, windows):
        for i, (sweep, k) in enumerate(windows):
            out[at + i] = refl_ref[sweep // 2, sweep % 2, k, :, :WINDOW]
        at += len(windows)
        for i in range(0, len(windows), 2):
            halves = []
            for sweep, k in windows[i : i + 2]:
                halves.append(refl_ref[sweep // 2, sweep % 2, k, :, WINDOW:])
            if len(halves) == 1:
                halves.append(jnp.zeros((mine, size), jnp.float32))
            out[at + i // 2] = jnp.concatenate(halves, -1)

    for group, out in zip(plan.groups, outs):
        fill(out, 0, group[0])
    for group in plan.groups:
        if group[1]:
            fill(outs[-1], group[4], [(sweep, 0) for sweep, _ in group[1]])


def pack(plan, refl):
    mine = refl.shape[3]
    counts = [group[2] for group in plan.groups] + [plan.edge_tiles]
    return pl.pallas_call(
        functools.partial(pack_kernel, plan),
        out_shape=tuple(jax.ShapeDtypeStruct((n, mine, WINDOW), jnp.float32) for n in counts),
        in_specs=[VMEM],
        out_specs=(VMEM,) * len(counts),
        compiler_params=pltpu.CompilerParams(vmem_limit_bytes=VMEM_LIMIT),
    )(refl)


def split(value):
    high = value.astype(jnp.bfloat16)
    return high, (value - high.astype(jnp.float32)).astype(jnp.bfloat16)


def fold(value):
    half = value.shape[1] // 2
    return value[:, :half] + value[:, half:]


def matrix_kernel(plan, ph, masked, *refs):
    entries, carry = plan.phases[ph]
    operands = list(refs)
    refs = operands[1:] if masked else operands
    offsets = operands[0][...] if masked else None
    old_ref = refs.pop(0) if carry else None
    tiles = refs.pop()
    out_ref = refs.pop()
    parts = refs
    here = lax.axis_index("col")
    if len(parts) == 2:
        for m in range(parts[0].shape[0]):
            other = lax.bitwise_xor(here, m * CORES)
            tiles[other] = parts[0][m]
            tiles[lax.bitwise_xor(other, 1)] = parts[1][m]
    else:
        tiles = parts[0]
    size = tiles.shape[0] * tiles.shape[2]
    last = lax.axis_index("row") == lax.axis_size("row") - 1
    lane = lax.broadcasted_iota(jnp.int32, (size, WINDOW), 1)
    row_id = lax.broadcasted_iota(jnp.int32, (WINDOW, WINDOW), 0)
    col_id = lax.broadcasted_iota(jnp.int32, (WINDOW, WINDOW), 1)
    unit = jnp.where(row_id == col_id, 1.0, 0.0).astype(jnp.float32)
    for i, window in enumerate(entries):
        if window is None:
            out_ref[i] = old_ref[carry[1]]
            continue
        sweep, k = window
        _, vec_tile, fac_tile, side = plan.where[window]
        vectors = tiles[:, vec_tile].reshape(size, WINDOW)
        factors = tiles[:, fac_tile].reshape(size, WINDOW)
        limit = WINDOW + lax.shift_right_logical(here, 16)
        if k == plan.nwin - 1:
            start = offsets[sweep % 2 : sweep % 2 + 1, sweep // 2 : sweep // 2 + 1]
            limit = jnp.where(last, WINDOW - start, WINDOW)
        vectors = jnp.where(lane < limit, vectors, 0.0)
        rows_hi, rows_lo = split(vectors)
        pair = jnp.concatenate([rows_hi, rows_lo], 1)
        blank = jnp.zeros_like(pair)
        stack = [blank, pair, blank, pair] if side else [pair, blank, pair, blank]
        scaled = fold(jnp.dot(
            jnp.concatenate(split(factors), 1),
            jnp.concatenate(stack, 0),
            preferred_element_type=jnp.float32,
        ))
        pair = jnp.concatenate(split(scaled), 1)
        product = fold(lax.dot_general(
            jnp.concatenate([rows_hi, rows_lo], 0),
            jnp.concatenate([pair, pair], 0),
            (((0,), (0,)), ((), ())),
            preferred_element_type=jnp.float32,
        ))
        high, low = split(unit - product)
        out_ref[i] = jnp.concatenate([high, low], 1)


def matrices(plan, ph, offsets, before, parts):
    count = plan.count(ph)
    carried = (before,) if plan.phases[ph][1] else ()
    masked = any(w is not None and w[1] == plan.nwin - 1 for w in plan.phases[ph][0])
    operands = [*([offsets] if masked else []), *carried, *parts]
    whole = (sum(part.shape[0] for part in parts),) + parts[0].shape[1:]
    return pl.pallas_call(
        functools.partial(matrix_kernel, plan, ph, masked),
        out_shape=jax.ShapeDtypeStruct((count, WINDOW, 2 * WINDOW), jnp.bfloat16),
        in_specs=[VMEM] * len(operands),
        out_specs=VMEM,
        scratch_shapes=[pltpu.VMEM(whole, jnp.float32)],
        compiler_params=pltpu.CompilerParams(vmem_limit_bytes=VMEM_LIMIT),
        cost_estimate=pl.CostEstimate(
            flops=count * 12 * 64 * 128 * 192, bytes_accessed=count * 100000, transcendentals=0
        ),
    )(*operands)


def apply_windows(field, at, count, first, mats):
    rows = field[pl.ds(at, count * WINDOW), :]
    updated = []
    for k in range(count):
        pair = jnp.concatenate(split(rows[k * WINDOW : (k + 1) * WINDOW]), 1)
        both = jnp.dot(
            mats[first + k],
            jnp.concatenate([pair, pair], 0),
            preferred_element_type=jnp.float32,
        )
        updated.append(fold(both))
    field[pl.ds(at, count * WINDOW), :] = jnp.concatenate(updated, 0)


def phase_kernel(ph, rounds, nwin, nparts, offsets_ref, *refs):
    parts = refs[:nparts]
    mats = refs[nparts]
    outs = refs[nparts + 1 : -1]
    field = refs[-1]
    place = 0
    for part in parts:
        field[place : place + part.shape[0], :] = part[...]
        place += part.shape[0]
    offsets = offsets_ref[...]
    at = 0
    if ph > 0:
        a, b = offsets[0, ph - 1], offsets[1, ph - 1]
        step = jnp.where(b < a, 1, 0)
        start = nwin - 3 if ph % 2 else 1
        apply_windows(field, a + WINDOW * start, 1, 0, mats)
        start = nwin - 4 if ph % 2 else 0
        apply_windows(field, b + WINDOW * (start + step), 2, 1 + step, mats)
        at = 4
    if ph < rounds:
        a, b = offsets[0, ph], offsets[1, ph]
        step = jnp.where(b < a, 1, 0)
        apply_windows(field, a, nwin - 1, at, mats)
        apply_windows(field, b + WINDOW * step, nwin - 2, at + nwin - 1 + step, mats)
    place = 0
    for out in outs:
        out[...] = field[place : place + out.shape[0], :]
        place += out.shape[0]


def phase(ph, rounds, nwin, offsets, parts, mats, sizes):
    rows = sum(part.shape[0] for part in parts)
    cols = parts[0].shape[1]
    operands = [offsets, *parts, mats]
    return pl.pallas_call(
        functools.partial(phase_kernel, ph, rounds, nwin, len(parts)),
        out_shape=tuple(jax.ShapeDtypeStruct((n, cols), jnp.float32) for n in sizes),
        in_specs=[VMEM] * len(operands),
        out_specs=(VMEM,) * len(sizes),
        scratch_shapes=[pltpu.VMEM((rows, cols), jnp.float32)],
        compiler_params=pltpu.CompilerParams(vmem_limit_bytes=VMEM_LIMIT),
        cost_estimate=pl.CostEstimate(
            flops=8 * 6 * WINDOW * WINDOW * cols, bytes_accessed=2000000, transcendentals=0
        ),
    )(*operands)


def after(value, earlier):
    return lax.optimization_barrier((value, earlier))[0]


class Gather:
    def __init__(self, plan, packed, size):
        self.plan = plan
        self.size = size
        *own, edge = packed
        devices = lax.axis_size("col")
        self.chips = devices // CORES
        self.stepwise = edge.shape[1] % 8 == 0 and devices == 4 * CORES
        self.held = {}
        self.shared = {}
        if self.stepwise:
            self.direct(0, own[0])
        ahead = shifted(edge, "row", -1)
        self.own = []
        for (_, _, _, edge_tiles, edge_at), tiles in zip(plan.groups, own):
            if edge_tiles:
                tiles = jnp.concatenate([tiles, ahead[edge_at : edge_at + edge_tiles]], 0)
            self.own.append(tiles)
        if self.stepwise:
            self.doubled(1, self.own[1], self.held[0][-1])

    def direct(self, g, tiles):
        others = [swapped(tiles, CORES * m) for m in range(1, self.chips)]
        self.held[g] = [part.reshape((1,) + tiles.shape) for part in [tiles] + others]

    def doubled(self, g, tiles, earlier=None):
        pair = (tiles, swapped(tiles, CORES))
        pair = jnp.stack(pair if earlier is None else after(pair, earlier))
        self.held[g] = [pair, swapped(pair, 2 * CORES)]

    def together(self, groups):
        if self.stepwise:
            self.direct(groups[0], jnp.concatenate([self.own[g] for g in groups], 0))
            at = 0
            for g in groups:
                self.shared[g] = (groups[0], at, self.own[g].shape[0])
                at += self.own[g].shape[0]

    def receive(self, g, earlier=None, ready=None):
        if self.stepwise:
            source, at, count = self.shared.get(g, (g, 0, self.own[g].shape[0]))
            pieces = self.held[source]
            if ready is not None:
                pieces = after(pieces, ready)
            same = jnp.concatenate([piece[:, at : at + count] for piece in pieces], 0)
            if earlier is not None:
                same = after(same, earlier)
            return (same, swapped(same, 1))
        whole = lax.all_gather(self.own[g], "col", axis=0)
        whole = jnp.moveaxis(whole, 0, 1).reshape(1, whole.shape[1], self.size, WINDOW)
        return (whole,)


def shards(evecs, offsets, refl):
    rows = evecs.shape[0]
    nwin = rows // WINDOW
    rounds = refl.shape[0]
    size = refl.shape[4] - WINDOW
    plan = Plan(rounds, nwin)
    offsets = offsets.T
    groups = len(plan.groups)
    gather = Gather(plan, pack(plan, refl), size)
    rest = rows - HALF
    parts = [evecs]
    mats = None
    results = []
    gather.together(range(2, groups))
    for ph in range(rounds):
        if ph < groups:
            ready = results[min(ph, 2) - 1] if ph else None
            tiles = gather.receive(ph, {2: parts, 3: results[-1]}.get(ph) if ph else None, ready)
        mats = matrices(plan, ph, offsets, mats, tiles)
        away = ph % 2 == 1
        sizes = (rest, HALF) if away else (HALF, rest)
        halves = phase(ph, rounds, nwin, offsets, parts, mats, sizes)
        result, kept = (halves[1], halves[0]) if away else halves
        results.append(result)
        moved = shifted(result, "row", 1 if away else -1)
        parts = [moved, kept] if away else [kept, moved]
    mats = matrices(plan, rounds, offsets, mats, tiles)
    (result,) = phase(rounds, rounds, nwin, offsets, parts, mats, (rows,))
    if rounds % 2:
        result = jnp.concatenate([shifted(result[rest:], "row", 1), result[:rest]], 0)
    return result


def solution(mesh):
    placed = (P("row", "col"), P(), P(None, None, "row", "col", None))
    return jax.shard_map(
        shards, mesh=mesh, in_specs=placed, out_specs=P("row", "col"), check_vma=False
    )
```

```python
import functools

import jax
import jax.numpy as jnp
from jax import lax
from jax.experimental import pallas as pl
from jax.experimental.pallas import tpu as pltpu
from jax.sharding import PartitionSpec as P

WINDOW = 128
HALF = 2 * WINDOW
CORES = 2
VMEM_LIMIT = 24 * 1024 * 1024
VMEM = pl.BlockSpec(memory_space=pltpu.VMEM)


def shifted(value, axis, by):
    devices = lax.axis_size(axis)
    return lax.ppermute(value, axis, [(i, (i + by) % devices) for i in range(devices)])


def swapped(value, bit):
    devices = lax.axis_size("col")
    return lax.ppermute(value, "col", [(i, i ^ bit) for i in range(devices)])


class Plan:
    def __init__(self, rounds, nwin):
        self.nwin = nwin
        self.phases = []
        for ph in range(rounds + 1):
            away = ph % 2 == 1
            entries = []
            self_carry = None
            if ph > 0:
                a, b = 2 * ph - 2, 2 * ph - 1
                if away:
                    entries += [(a, nwin - 1), None, (b, nwin - 1), (b, nwin)]
                    self_carry = (1, self.count(ph - 1) - 1)
                else:
                    entries += [(a, 1), (b, 0), (b, 1), None]
                    self_carry = (3, self.count(ph - 1) - (nwin - 1))
            if ph < rounds:
                base = 2 if away else 0
                for sweep in (2 * ph, 2 * ph + 1):
                    entries += [(sweep, base + k) for k in range(nwin - 1)]
            self.phases.append((entries, self_carry))
        groups = [[ph] for ph in range(rounds - 1)] + [[rounds - 1, rounds]]
        self.groups = []
        self.where = {}
        edge_at = 0
        for g, members in enumerate(groups):
            wanted = [w for ph in members for w in self.phases[ph][0] if w is not None]
            own = [w for w in wanted if w[1] < nwin]
            edge = [w for w in wanted if w[1] == nwin]
            place = 0
            for part in (own, edge):
                for i, w in enumerate(part):
                    self.where[w] = (g, place + i, place + len(part) + i // 2, i % 2)
                place += len(part) + (len(part) + 1) // 2
            own_tiles = len(own) + (len(own) + 1) // 2
            edge_tiles = place - own_tiles
            self.groups.append((own, edge, own_tiles, edge_tiles, edge_at))
            edge_at += edge_tiles
        self.edge_tiles = edge_at

    def count(self, ph):
        return len(self.phases[ph][0])


def pack_kernel(plan, refl_ref, *outs):
    size = refl_ref.shape[-1] - WINDOW
    mine = refl_ref.shape[-2]

    def fill(out, at, windows):
        for i, (sweep, k) in enumerate(windows):
            out[at + i] = refl_ref[sweep // 2, sweep % 2, k, :, :WINDOW]
        at += len(windows)
        for i in range(0, len(windows), 2):
            halves = []
            for sweep, k in windows[i : i + 2]:
                halves.append(refl_ref[sweep // 2, sweep % 2, k, :, WINDOW:])
            if len(halves) == 1:
                halves.append(jnp.zeros((mine, size), jnp.float32))
            out[at + i // 2] = jnp.concatenate(halves, -1)

    for group, out in zip(plan.groups, outs):
        fill(out, 0, group[0])
    for group in plan.groups:
        if group[1]:
            fill(outs[-1], group[4], [(sweep, 0) for sweep, _ in group[1]])


def pack(plan, refl):
    mine = refl.shape[3]
    counts = [group[2] for group in plan.groups] + [plan.edge_tiles]
    return pl.pallas_call(
        functools.partial(pack_kernel, plan),
        out_shape=tuple(jax.ShapeDtypeStruct((n, mine, WINDOW), jnp.float32) for n in counts),
        in_specs=[VMEM],
        out_specs=(VMEM,) * len(counts),
        compiler_params=pltpu.CompilerParams(vmem_limit_bytes=VMEM_LIMIT),
    )(refl)


def split(value):
    high = value.astype(jnp.bfloat16)
    return high, (value - high.astype(jnp.float32)).astype(jnp.bfloat16)


def fold(value):
    half = value.shape[1] // 2
    return value[:, :half] + value[:, half:]


def matrix_kernel(plan, ph, masked, *refs):
    entries, carry = plan.phases[ph]
    operands = list(refs)
    refs = operands[1:] if masked else operands
    offsets = operands[0][...] if masked else None
    old_ref = refs.pop(0) if carry else None
    tiles = refs.pop()
    out_ref = refs.pop()
    parts = refs
    here = lax.axis_index("col")
    if len(parts) == 2:
        for m in range(parts[0].shape[0]):
            other = lax.bitwise_xor(here, m * CORES)
            tiles[other] = parts[0][m]
            tiles[lax.bitwise_xor(other, 1)] = parts[1][m]
    else:
        tiles = parts[0]
    size = tiles.shape[0] * tiles.shape[2]
    last = lax.axis_index("row") == lax.axis_size("row") - 1
    lane = lax.broadcasted_iota(jnp.int32, (size, WINDOW), 1)
    row_id = lax.broadcasted_iota(jnp.int32, (WINDOW, WINDOW), 0)
    col_id = lax.broadcasted_iota(jnp.int32, (WINDOW, WINDOW), 1)
    unit = jnp.where(row_id == col_id, 1.0, 0.0).astype(jnp.float32)
    for i, window in enumerate(entries):
        if window is None:
            out_ref[i] = old_ref[carry[1]]
            continue
        sweep, k = window
        _, vec_tile, fac_tile, side = plan.where[window]
        vectors = tiles[:, vec_tile].reshape(size, WINDOW)
        factors = tiles[:, fac_tile].reshape(size, WINDOW)
        limit = WINDOW + lax.shift_right_logical(here, 16)
        if k == plan.nwin - 1:
            start = offsets[sweep % 2 : sweep % 2 + 1, sweep // 2 : sweep // 2 + 1]
            limit = jnp.where(last, WINDOW - start, WINDOW)
        vectors = jnp.where(lane < limit, vectors, 0.0)
        rows_hi, rows_lo = split(vectors)
        pair = jnp.concatenate([rows_hi, rows_lo], 1)
        blank = jnp.zeros_like(pair)
        stack = [blank, pair, blank, pair] if side else [pair, blank, pair, blank]
        scaled = fold(jnp.dot(
            jnp.concatenate(split(factors), 1),
            jnp.concatenate(stack, 0),
            preferred_element_type=jnp.float32,
        ))
        pair = jnp.concatenate(split(scaled), 1)
        product = fold(lax.dot_general(
            jnp.concatenate([rows_hi, rows_lo], 0),
            jnp.concatenate([pair, pair], 0),
            (((0,), (0,)), ((), ())),
            preferred_element_type=jnp.float32,
        ))
        high, low = split(unit - product)
        out_ref[i] = jnp.concatenate([high, low], 1)


def matrices(plan, ph, offsets, before, parts):
    count = plan.count(ph)
    carried = (before,) if plan.phases[ph][1] else ()
    masked = any(w is not None and w[1] == plan.nwin - 1 for w in plan.phases[ph][0])
    operands = [*([offsets] if masked else []), *carried, *parts]
    whole = (sum(part.shape[0] for part in parts),) + parts[0].shape[1:]
    return pl.pallas_call(
        functools.partial(matrix_kernel, plan, ph, masked),
        out_shape=jax.ShapeDtypeStruct((count, WINDOW, 2 * WINDOW), jnp.bfloat16),
        in_specs=[VMEM] * len(operands),
        out_specs=VMEM,
        scratch_shapes=[pltpu.VMEM(whole, jnp.float32)],
        compiler_params=pltpu.CompilerParams(vmem_limit_bytes=VMEM_LIMIT),
        cost_estimate=pl.CostEstimate(
            flops=count * 12 * 64 * 128 * 192, bytes_accessed=count * 100000, transcendentals=0
        ),
    )(*operands)


def apply_windows(field, at, count, first, mats):
    rows = field[pl.ds(at, count * WINDOW), :]
    updated = []
    for k in range(count):
        pair = jnp.concatenate(split(rows[k * WINDOW : (k + 1) * WINDOW]), 1)
        both = jnp.dot(
            mats[first + k],
            jnp.concatenate([pair, pair], 0),
            preferred_element_type=jnp.float32,
        )
        updated.append(fold(both))
    field[pl.ds(at, count * WINDOW), :] = jnp.concatenate(updated, 0)


def phase_kernel(ph, rounds, nwin, nparts, offsets_ref, *refs):
    parts = refs[:nparts]
    mats = refs[nparts]
    outs = refs[nparts + 1 : -1]
    field = refs[-1]
    place = 0
    for part in parts:
        field[place : place + part.shape[0], :] = part[...]
        place += part.shape[0]
    offsets = offsets_ref[...]
    at = 0
    if ph > 0:
        a, b = offsets[0, ph - 1], offsets[1, ph - 1]
        step = jnp.where(b < a, 1, 0)
        start = nwin - 3 if ph % 2 else 1
        apply_windows(field, a + WINDOW * start, 1, 0, mats)
        start = nwin - 4 if ph % 2 else 0
        apply_windows(field, b + WINDOW * (start + step), 2, 1 + step, mats)
        at = 4
    if ph < rounds:
        a, b = offsets[0, ph], offsets[1, ph]
        step = jnp.where(b < a, 1, 0)
        apply_windows(field, a, nwin - 1, at, mats)
        apply_windows(field, b + WINDOW * step, nwin - 2, at + nwin - 1 + step, mats)
    place = 0
    for out in outs:
        out[...] = field[place : place + out.shape[0], :]
        place += out.shape[0]


def phase(ph, rounds, nwin, offsets, parts, mats, sizes):
    rows = sum(part.shape[0] for part in parts)
    cols = parts[0].shape[1]
    operands = [offsets, *parts, mats]
    return pl.pallas_call(
        functools.partial(phase_kernel, ph, rounds, nwin, len(parts)),
        out_shape=tuple(jax.ShapeDtypeStruct((n, cols), jnp.float32) for n in sizes),
        in_specs=[VMEM] * len(operands),
        out_specs=(VMEM,) * len(sizes),
        scratch_shapes=[pltpu.VMEM((rows, cols), jnp.float32)],
        compiler_params=pltpu.CompilerParams(vmem_limit_bytes=VMEM_LIMIT),
        cost_estimate=pl.CostEstimate(
            flops=8 * 6 * WINDOW * WINDOW * cols, bytes_accessed=2000000, transcendentals=0
        ),
    )(*operands)


def after(value, earlier):
    return lax.optimization_barrier((value, earlier))[0]


class Gather:
    def __init__(self, plan, packed, size):
        self.plan = plan
        self.size = size
        *own, edge = packed
        devices = lax.axis_size("col")
        self.chips = devices // CORES
        self.stepwise = edge.shape[1] % 8 == 0 and devices == 4 * CORES
        self.held = {}
        self.shared = {}
        ahead = shifted(edge, "row", -1)
        self.own = []
        for (_, _, _, edge_tiles, edge_at), tiles in zip(plan.groups, own):
            if edge_tiles:
                tiles = jnp.concatenate([tiles, ahead[edge_at : edge_at + edge_tiles]], 0)
            self.own.append(tiles)

    def direct(self, g, tiles):
        others = [swapped(tiles, CORES * m) for m in range(1, self.chips)]
        self.held[g] = [part.reshape((1,) + tiles.shape) for part in [tiles] + others]

    def together(self, groups):
        if self.stepwise and groups:
            self.direct(groups[0], jnp.concatenate([self.own[g] for g in groups], 0))
            at = 0
            for g in groups:
                self.shared[g] = (groups[0], at, self.own[g].shape[0])
                at += self.own[g].shape[0]

    def receive(self, g, earlier=None, ready=None):
        if self.stepwise:
            source, at, count = self.shared.get(g, (g, 0, self.own[g].shape[0]))
            pieces = self.held[source]
            if ready is not None:
                pieces = after(pieces, ready)
            same = jnp.concatenate([piece[:, at : at + count] for piece in pieces], 0)
            if earlier is not None:
                same = after(same, earlier)
            return (same, swapped(same, 1))
        whole = lax.all_gather(self.own[g], "col", axis=0)
        whole = jnp.moveaxis(whole, 0, 1).reshape(1, whole.shape[1], self.size, WINDOW)
        return (whole,)


def shards(evecs, offsets, refl):
    rows = evecs.shape[0]
    nwin = rows // WINDOW
    rounds = refl.shape[0]
    size = refl.shape[4] - WINDOW
    plan = Plan(rounds, nwin)
    offsets = offsets.T
    groups = len(plan.groups)
    gather = Gather(plan, pack(plan, refl), size)
    rest = rows - HALF
    parts = [evecs]
    mats = None
    result = None
    results = []
    gather.together(range(min(2, groups)))
    gather.together(range(2, groups))
    for ph in range(rounds):
        if ph < groups:
            ready = results[1] if ph > 1 else None
            tiles = gather.receive(ph, {2: parts, 3: result}.get(ph), ready)
        mats = matrices(plan, ph, offsets, mats, tiles)
        away = ph % 2 == 1
        sizes = (rest, HALF) if away else (HALF, rest)
        halves = phase(ph, rounds, nwin, offsets, parts, mats, sizes)
        result, kept = (halves[1], halves[0]) if away else halves
        results.append(result)
        moved = shifted(result, "row", 1 if away else -1)
        parts = [moved, kept] if away else [kept, moved]
    mats = matrices(plan, rounds, offsets, mats, tiles)
    (result,) = phase(rounds, rounds, nwin, offsets, parts, mats, (rows,))
    if rounds % 2:
        result = jnp.concatenate([shifted(result[rest:], "row", 1), result[:rest]], 0)
    return result


def solution(mesh):
    placed = (P("row", "col"), P(), P(None, None, "row", "col", None))
    return jax.shard_map(
        shards, mesh=mesh, in_specs=placed, out_specs=P("row", "col"), check_vma=False
    )
```

```python
import functools

import jax
import jax.numpy as jnp
from jax import lax
from jax.experimental import pallas as pl
from jax.experimental.pallas import tpu as pltpu
from jax.sharding import PartitionSpec as P

WINDOW = 128
HALF = 2 * WINDOW
CORES = 2
VMEM_LIMIT = 24 * 1024 * 1024
VMEM = pl.BlockSpec(memory_space=pltpu.VMEM)


def shifted(value, axis, by):
    devices = lax.axis_size(axis)
    return lax.ppermute(value, axis, [(i, (i + by) % devices) for i in range(devices)])


def swapped(value, bit):
    devices = lax.axis_size("col")
    return lax.ppermute(value, "col", [(i, i ^ bit) for i in range(devices)])


class Plan:
    def __init__(self, rounds, nwin):
        self.nwin = nwin
        self.phases = []
        for ph in range(rounds + 1):
            away = ph % 2 == 1
            entries = []
            self_carry = None
            if ph > 0:
                a, b = 2 * ph - 2, 2 * ph - 1
                if away:
                    entries += [(a, nwin - 1), None, (b, nwin - 1), (b, nwin)]
                    self_carry = (1, self.count(ph - 1) - 1)
                else:
                    entries += [(a, 1), (b, 0), (b, 1), None]
                    self_carry = (3, self.count(ph - 1) - (nwin - 1))
            if ph < rounds:
                base = 2 if away else 0
                for sweep in (2 * ph, 2 * ph + 1):
                    entries += [(sweep, base + k) for k in range(nwin - 1)]
            self.phases.append((entries, self_carry))
        groups = [[ph] for ph in range(rounds - 1)] + [[rounds - 1, rounds]]
        self.groups = []
        self.where = {}
        edge_at = 0
        for g, members in enumerate(groups):
            wanted = [w for ph in members for w in self.phases[ph][0] if w is not None]
            own = [w for w in wanted if w[1] < nwin]
            edge = [w for w in wanted if w[1] == nwin]
            place = 0
            for part in (own, edge):
                for i, w in enumerate(part):
                    self.where[w] = (g, place + i, place + len(part) + i // 2, i % 2)
                place += len(part) + (len(part) + 1) // 2
            own_tiles = len(own) + (len(own) + 1) // 2
            edge_tiles = place - own_tiles
            self.groups.append((own, edge, own_tiles, edge_tiles, edge_at))
            edge_at += edge_tiles
        self.edge_tiles = edge_at

    def count(self, ph):
        return len(self.phases[ph][0])


def pack_kernel(plan, refl_ref, *outs):
    size = refl_ref.shape[-1] - WINDOW
    mine = refl_ref.shape[-2]

    def fill(out, at, windows):
        for i, (sweep, k) in enumerate(windows):
            out[at + i] = refl_ref[sweep // 2, sweep % 2, k, :, :WINDOW]
        at += len(windows)
        for i in range(0, len(windows), 2):
            halves = []
            for sweep, k in windows[i : i + 2]:
                halves.append(refl_ref[sweep // 2, sweep % 2, k, :, WINDOW:])
            if len(halves) == 1:
                halves.append(jnp.zeros((mine, size), jnp.float32))
            out[at + i // 2] = jnp.concatenate(halves, -1)

    for group, out in zip(plan.groups, outs):
        fill(out, 0, group[0])
    for group in plan.groups:
        if group[1]:
            fill(outs[-1], group[4], [(sweep, 0) for sweep, _ in group[1]])


def pack(plan, refl):
    mine = refl.shape[3]
    counts = [group[2] for group in plan.groups] + [plan.edge_tiles]
    return pl.pallas_call(
        functools.partial(pack_kernel, plan),
        out_shape=tuple(jax.ShapeDtypeStruct((n, mine, WINDOW), jnp.float32) for n in counts),
        in_specs=[VMEM],
        out_specs=(VMEM,) * len(counts),
        compiler_params=pltpu.CompilerParams(vmem_limit_bytes=VMEM_LIMIT),
    )(refl)


def split(value):
    high = value.astype(jnp.bfloat16)
    return high, (value - high.astype(jnp.float32)).astype(jnp.bfloat16)


def fold(value):
    half = value.shape[1] // 2
    return value[:, :half] + value[:, half:]


def matrix_kernel(plan, ph, masked, *refs):
    entries, carry = plan.phases[ph]
    operands = list(refs)
    refs = operands[1:] if masked else operands
    offsets = operands[0][...] if masked else None
    old_ref = refs.pop(0) if carry else None
    tiles = refs.pop()
    out_ref = refs.pop()
    parts = refs
    here = lax.axis_index("col")
    if len(parts) == 2:
        for m in range(parts[0].shape[0]):
            other = lax.bitwise_xor(here, m * CORES)
            tiles[other] = parts[0][m]
            tiles[lax.bitwise_xor(other, 1)] = parts[1][m]
    else:
        tiles = parts[0]
    size = tiles.shape[0] * tiles.shape[2]
    last = lax.axis_index("row") == lax.axis_size("row") - 1
    lane = lax.broadcasted_iota(jnp.int32, (size, WINDOW), 1)
    row_id = lax.broadcasted_iota(jnp.int32, (WINDOW, WINDOW), 0)
    col_id = lax.broadcasted_iota(jnp.int32, (WINDOW, WINDOW), 1)
    unit = jnp.where(row_id == col_id, 1.0, 0.0).astype(jnp.float32)
    for i, window in enumerate(entries):
        if window is None:
            out_ref[i] = old_ref[carry[1]]
            continue
        sweep, k = window
        _, vec_tile, fac_tile, side = plan.where[window]
        vectors = tiles[:, vec_tile].reshape(size, WINDOW)
        factors = tiles[:, fac_tile].reshape(size, WINDOW)
        limit = WINDOW + lax.shift_right_logical(here, 16)
        if k == plan.nwin - 1:
            start = offsets[sweep % 2 : sweep % 2 + 1, sweep // 2 : sweep // 2 + 1]
            limit = jnp.where(last, WINDOW - start, WINDOW)
        vectors = jnp.where(lane < limit, vectors, 0.0)
        rows_hi, rows_lo = split(vectors)
        pair = jnp.concatenate([rows_hi, rows_lo], 1)
        blank = jnp.zeros_like(pair)
        stack = [blank, pair, blank, pair] if side else [pair, blank, pair, blank]
        scaled = fold(jnp.dot(
            jnp.concatenate(split(factors), 1),
            jnp.concatenate(stack, 0),
            preferred_element_type=jnp.float32,
        ))
        pair = jnp.concatenate(split(scaled), 1)
        product = fold(lax.dot_general(
            jnp.concatenate([rows_hi, rows_lo], 0),
            jnp.concatenate([pair, pair], 0),
            (((0,), (0,)), ((), ())),
            preferred_element_type=jnp.float32,
        ))
        high, low = split(unit - product)
        out_ref[i] = jnp.concatenate([high, low], 1)


def matrices(plan, ph, offsets, before, parts):
    count = plan.count(ph)
    carried = (before,) if plan.phases[ph][1] else ()
    masked = any(w is not None and w[1] == plan.nwin - 1 for w in plan.phases[ph][0])
    operands = [*([offsets] if masked else []), *carried, *parts]
    whole = (sum(part.shape[0] for part in parts),) + parts[0].shape[1:]
    return pl.pallas_call(
        functools.partial(matrix_kernel, plan, ph, masked),
        out_shape=jax.ShapeDtypeStruct((count, WINDOW, 2 * WINDOW), jnp.bfloat16),
        in_specs=[VMEM] * len(operands),
        out_specs=VMEM,
        scratch_shapes=[pltpu.VMEM(whole, jnp.float32)],
        compiler_params=pltpu.CompilerParams(vmem_limit_bytes=VMEM_LIMIT),
        cost_estimate=pl.CostEstimate(
            flops=count * 12 * 64 * 128 * 192, bytes_accessed=count * 100000, transcendentals=0
        ),
    )(*operands)


def apply_windows(field, at, count, first, mats):
    rows = field[pl.ds(at, count * WINDOW), :]
    updated = []
    for k in range(count):
        pair = jnp.concatenate(split(rows[k * WINDOW : (k + 1) * WINDOW]), 1)
        both = jnp.dot(
            mats[first + k],
            jnp.concatenate([pair, pair], 0),
            preferred_element_type=jnp.float32,
        )
        updated.append(fold(both))
    field[pl.ds(at, count * WINDOW), :] = jnp.concatenate(updated, 0)


def phase_kernel(ph, rounds, nwin, nparts, offsets_ref, *refs):
    parts = refs[:nparts]
    mats = refs[nparts]
    outs = refs[nparts + 1 : -1]
    field = refs[-1]
    place = 0
    for part in parts:
        field[place : place + part.shape[0], :] = part[...]
        place += part.shape[0]
    offsets = offsets_ref[...]
    at = 0
    if ph > 0:
        a, b = offsets[0, ph - 1], offsets[1, ph - 1]
        step = jnp.where(b < a, 1, 0)
        start = nwin - 3 if ph % 2 else 1
        apply_windows(field, a + WINDOW * start, 1, 0, mats)
        start = nwin - 4 if ph % 2 else 0
        apply_windows(field, b + WINDOW * (start + step), 2, 1 + step, mats)
        at = 4
    if ph < rounds:
        a, b = offsets[0, ph], offsets[1, ph]
        step = jnp.where(b < a, 1, 0)
        apply_windows(field, a, nwin - 1, at, mats)
        apply_windows(field, b + WINDOW * step, nwin - 2, at + nwin - 1 + step, mats)
    place = 0
    for out in outs:
        out[...] = field[place : place + out.shape[0], :]
        place += out.shape[0]


def phase(ph, rounds, nwin, offsets, parts, mats, sizes):
    rows = sum(part.shape[0] for part in parts)
    cols = parts[0].shape[1]
    operands = [offsets, *parts, mats]
    return pl.pallas_call(
        functools.partial(phase_kernel, ph, rounds, nwin, len(parts)),
        out_shape=tuple(jax.ShapeDtypeStruct((n, cols), jnp.float32) for n in sizes),
        in_specs=[VMEM] * len(operands),
        out_specs=(VMEM,) * len(sizes),
        scratch_shapes=[pltpu.VMEM((rows, cols), jnp.float32)],
        compiler_params=pltpu.CompilerParams(vmem_limit_bytes=VMEM_LIMIT),
        cost_estimate=pl.CostEstimate(
            flops=8 * 6 * WINDOW * WINDOW * cols, bytes_accessed=2000000, transcendentals=0
        ),
    )(*operands)


def after(value, earlier):
    return lax.optimization_barrier((value, earlier))[0]


class Gather:
    def __init__(self, plan, packed, size):
        self.plan = plan
        self.size = size
        *own, edge = packed
        devices = lax.axis_size("col")
        self.chips = devices // CORES
        self.stepwise = edge.shape[1] % 8 == 0 and devices == 4 * CORES
        self.held = {}
        self.shared = {}
        self.own = own
        self.ahead = shifted(edge, "row", -1)

    def doubled(self):
        if self.stepwise:
            pair = jnp.stack([self.ahead, swapped(self.ahead, CORES)])
            self.edges = [pair, swapped(pair, 2 * CORES)]

    def direct(self, g, tiles):
        others = [swapped(tiles, CORES * m) for m in range(1, self.chips)]
        self.held[g] = [part.reshape((1,) + tiles.shape) for part in [tiles] + others]

    def together(self, groups):
        if self.stepwise and groups:
            self.direct(groups[0], jnp.concatenate([self.own[g] for g in groups], 0))
            at = 0
            for g in groups:
                self.shared[g] = (groups[0], at, self.own[g].shape[0])
                at += self.own[g].shape[0]

    def receive(self, g, earlier=None, ready=None):
        _, _, _, edge_tiles, edge_at = self.plan.groups[g]
        if self.stepwise:
            source, at, count = self.shared.get(g, (g, 0, self.own[g].shape[0]))
            pieces = self.held[source]
            if ready is not None:
                pieces = after(pieces, ready)
            same = jnp.concatenate([piece[:, at : at + count] for piece in pieces], 0)
            if edge_tiles:
                edges = self.edges if ready is None else after(self.edges, ready)
                edges = [piece[:, edge_at : edge_at + edge_tiles] for piece in edges]
                same = jnp.concatenate([same, jnp.concatenate(edges, 0)], 1)
            if earlier is not None:
                same = after(same, earlier)
            return (same, swapped(same, 1))
        tiles = self.own[g]
        if edge_tiles:
            tiles = jnp.concatenate([tiles, self.ahead[edge_at : edge_at + edge_tiles]], 0)
        whole = lax.all_gather(tiles, "col", axis=0)
        whole = jnp.moveaxis(whole, 0, 1).reshape(1, whole.shape[1], self.size, WINDOW)
        return (whole,)


def shards(evecs, offsets, refl):
    rows = evecs.shape[0]
    nwin = rows // WINDOW
    rounds = refl.shape[0]
    size = refl.shape[4] - WINDOW
    plan = Plan(rounds, nwin)
    offsets = offsets.T
    groups = len(plan.groups)
    gather = Gather(plan, pack(plan, refl), size)
    rest = rows - HALF
    parts = [evecs]
    mats = None
    result = None
    results = []
    gather.together(range(min(2, groups)))
    gather.doubled()
    gather.together(range(2, groups))
    for ph in range(rounds):
        if ph < groups:
            ready = results[min(ph, 2) - 1] if ph else None
            tiles = gather.receive(ph, {2: parts, 3: result}.get(ph), ready)
        mats = matrices(plan, ph, offsets, mats, tiles)
        away = ph % 2 == 1
        sizes = (rest, HALF) if away else (HALF, rest)
        halves = phase(ph, rounds, nwin, offsets, parts, mats, sizes)
        result, kept = (halves[1], halves[0]) if away else halves
        results.append(result)
        moved = shifted(result, "row", 1 if away else -1)
        parts = [moved, kept] if away else [kept, moved]
    mats = matrices(plan, rounds, offsets, mats, tiles)
    (result,) = phase(rounds, rounds, nwin, offsets, parts, mats, (rows,))
    if rounds % 2:
        result = jnp.concatenate([shifted(result[rest:], "row", 1), result[:rest]], 0)
    return result


def solution(mesh):
    placed = (P("row", "col"), P(), P(None, None, "row", "col", None))
    return jax.shard_map(
        shards, mesh=mesh, in_specs=placed, out_specs=P("row", "col"), check_vma=False
    )
```

```python
import functools

import jax
import jax.numpy as jnp
from jax import lax
from jax.experimental import pallas as pl
from jax.experimental.pallas import tpu as pltpu
from jax.sharding import PartitionSpec as P

WINDOW = 128
HALF = 2 * WINDOW
CORES = 2
STAGE = 3
VMEM_LIMIT = 24 * 1024 * 1024
VMEM = pl.BlockSpec(memory_space=pltpu.VMEM)


def shifted(value, axis, by):
    devices = lax.axis_size(axis)
    return lax.ppermute(value, axis, [(i, (i + by) % devices) for i in range(devices)])


def swapped(value, bit):
    devices = lax.axis_size("col")
    return lax.ppermute(value, "col", [(i, i ^ bit) for i in range(devices)])


class Plan:
    def __init__(self, rounds, nwin):
        self.nwin = nwin
        self.phases = []
        for ph in range(rounds + 1):
            away = ph % 2 == 1
            entries = []
            self_carry = None
            if ph > 0:
                a, b = 2 * ph - 2, 2 * ph - 1
                if away:
                    entries += [(a, nwin - 1), None, (b, nwin - 1), (b, nwin)]
                    self_carry = (1, self.count(ph - 1) - 1)
                else:
                    entries += [(a, 1), (b, 0), (b, 1), None]
                    self_carry = (3, self.count(ph - 1) - (nwin - 1))
            if ph < rounds:
                base = 2 if away else 0
                for sweep in (2 * ph, 2 * ph + 1):
                    entries += [(sweep, base + k) for k in range(nwin - 1)]
            self.phases.append((entries, self_carry))
        groups = [[ph] for ph in range(rounds - 1)] + [[rounds - 1, rounds]]
        self.groups = []
        self.where = {}
        edge_at = 0
        for g, members in enumerate(groups):
            wanted = [w for ph in members for w in self.phases[ph][0] if w is not None]
            own = [w for w in wanted if w[1] < nwin]
            edge = [w for w in wanted if w[1] == nwin]
            place = 0
            for part in (own, edge):
                for i, w in enumerate(part):
                    self.where[w] = (g, place + i, place + len(part) + i // 2, i % 2)
                place += len(part) + (len(part) + 1) // 2
            own_tiles = len(own) + (len(own) + 1) // 2
            edge_tiles = place - own_tiles
            self.groups.append((own, edge, own_tiles, edge_tiles, edge_at))
            edge_at += edge_tiles
        self.edge_tiles = edge_at

    def count(self, ph):
        return len(self.phases[ph][0])


def pack_kernel(plan, refl_ref, *outs):
    size = refl_ref.shape[-1] - WINDOW
    mine = refl_ref.shape[-2]

    def fill(out, at, windows):
        for i, (sweep, k) in enumerate(windows):
            out[at + i] = refl_ref[sweep // 2, sweep % 2, k, :, :WINDOW]
        at += len(windows)
        for i in range(0, len(windows), 2):
            halves = []
            for sweep, k in windows[i : i + 2]:
                halves.append(refl_ref[sweep // 2, sweep % 2, k, :, WINDOW:])
            if len(halves) == 1:
                halves.append(jnp.zeros((mine, size), jnp.float32))
            out[at + i // 2] = jnp.concatenate(halves, -1)

    for group, out in zip(plan.groups, outs):
        fill(out, 0, group[0])
    for group in plan.groups:
        if group[1]:
            fill(outs[-1], group[4], [(sweep, 0) for sweep, _ in group[1]])


def pack(plan, refl):
    mine = refl.shape[3]
    counts = [group[2] for group in plan.groups] + [plan.edge_tiles]
    return pl.pallas_call(
        functools.partial(pack_kernel, plan),
        out_shape=tuple(jax.ShapeDtypeStruct((n, mine, WINDOW), jnp.float32) for n in counts),
        in_specs=[VMEM],
        out_specs=(VMEM,) * len(counts),
        compiler_params=pltpu.CompilerParams(vmem_limit_bytes=VMEM_LIMIT),
    )(refl)


def split(value):
    high = value.astype(jnp.bfloat16)
    return high, (value - high.astype(jnp.float32)).astype(jnp.bfloat16)


def fold(value):
    half = value.shape[1] // 2
    return value[:, :half] + value[:, half:]


def matrix_kernel(plan, ph, masked, *refs):
    entries, carry = plan.phases[ph]
    operands = list(refs)
    refs = operands[1:] if masked else operands
    offsets = operands[0][...] if masked else None
    old_ref = refs.pop(0) if carry else None
    tiles = refs.pop()
    out_ref = refs.pop()
    parts = refs
    here = lax.axis_index("col")
    if len(parts) == 2:
        for m in range(parts[0].shape[0]):
            other = lax.bitwise_xor(here, m * CORES)
            tiles[other] = parts[0][m]
            tiles[lax.bitwise_xor(other, 1)] = parts[1][m]
    else:
        tiles = parts[0]
    size = tiles.shape[0] * tiles.shape[2]
    last = lax.axis_index("row") == lax.axis_size("row") - 1
    lane = lax.broadcasted_iota(jnp.int32, (size, WINDOW), 1)
    row_id = lax.broadcasted_iota(jnp.int32, (WINDOW, WINDOW), 0)
    col_id = lax.broadcasted_iota(jnp.int32, (WINDOW, WINDOW), 1)
    unit = jnp.where(row_id == col_id, 1.0, 0.0).astype(jnp.float32)

    def first(window):
        sweep, k = window
        _, vec_tile, fac_tile, side = plan.where[window]
        vectors = tiles[:, vec_tile].reshape(size, WINDOW)
        factors = tiles[:, fac_tile].reshape(size, WINDOW)
        if k == plan.nwin - 1:
            start = offsets[sweep % 2 : sweep % 2 + 1, sweep // 2 : sweep // 2 + 1]
            limit = jnp.where(last, WINDOW - start, WINDOW)
            vectors = jnp.where(lane < limit, vectors, 0.0)
        rows_hi, rows_lo = split(vectors)
        pair = jnp.concatenate([rows_hi, rows_lo], 1)
        blank = jnp.zeros_like(pair)
        stack = [blank, pair, blank, pair] if side else [pair, blank, pair, blank]
        scaled = jnp.dot(
            jnp.concatenate(split(factors), 1),
            jnp.concatenate(stack, 0),
            preferred_element_type=jnp.float32,
        )
        return jnp.concatenate([rows_hi, rows_lo], 0), scaled

    def second(rows, scaled):
        pair = jnp.concatenate(split(fold(scaled)), 1)
        product = lax.dot_general(
            rows,
            jnp.concatenate([pair, pair], 0),
            (((0,), (0,)), ((), ())),
            preferred_element_type=jnp.float32,
        )
        return jnp.concatenate(split(unit - fold(product)), 1)

    fresh = [i for i, window in enumerate(entries) if window is not None]
    for at in range(0, len(fresh), STAGE):
        some = fresh[at : at + STAGE]
        halves = [first(entries[i]) for i in some]
        for i, half in zip(some, halves):
            out_ref[i] = second(*half)
    if carry:
        out_ref[carry[0]] = old_ref[carry[1]]


def matrices(plan, ph, offsets, before, parts):
    count = plan.count(ph)
    carried = (before,) if plan.phases[ph][1] else ()
    masked = any(w is not None and w[1] == plan.nwin - 1 for w in plan.phases[ph][0])
    operands = [*([offsets] if masked else []), *carried, *parts]
    whole = (sum(part.shape[0] for part in parts),) + parts[0].shape[1:]
    return pl.pallas_call(
        functools.partial(matrix_kernel, plan, ph, masked),
        out_shape=jax.ShapeDtypeStruct((count, WINDOW, 2 * WINDOW), jnp.bfloat16),
        in_specs=[VMEM] * len(operands),
        out_specs=VMEM,
        scratch_shapes=[pltpu.VMEM(whole, jnp.float32)],
        compiler_params=pltpu.CompilerParams(vmem_limit_bytes=VMEM_LIMIT),
        cost_estimate=pl.CostEstimate(
            flops=count * 12 * 64 * 128 * 192, bytes_accessed=count * 100000, transcendentals=0
        ),
    )(*operands)


def apply_windows(field, at, count, first, mats):
    rows = field[pl.ds(at, count * WINDOW), :]
    updated = []
    for k in range(count):
        pair = jnp.concatenate(split(rows[k * WINDOW : (k + 1) * WINDOW]), 1)
        both = jnp.dot(
            mats[first + k],
            jnp.concatenate([pair, pair], 0),
            preferred_element_type=jnp.float32,
        )
        updated.append(fold(both))
    field[pl.ds(at, count * WINDOW), :] = jnp.concatenate(updated, 0)


def phase_kernel(ph, rounds, nwin, nparts, offsets_ref, *refs):
    parts = refs[:nparts]
    mats = refs[nparts]
    outs = refs[nparts + 1 : -1]
    field = refs[-1]
    place = 0
    for part in parts:
        field[place : place + part.shape[0], :] = part[...]
        place += part.shape[0]
    offsets = offsets_ref[...]
    at = 0
    if ph > 0:
        a, b = offsets[0, ph - 1], offsets[1, ph - 1]
        step = jnp.where(b < a, 1, 0)
        start = nwin - 3 if ph % 2 else 1
        apply_windows(field, a + WINDOW * start, 1, 0, mats)
        start = nwin - 4 if ph % 2 else 0
        apply_windows(field, b + WINDOW * (start + step), 2, 1 + step, mats)
        at = 4
    if ph < rounds:
        a, b = offsets[0, ph], offsets[1, ph]
        step = jnp.where(b < a, 1, 0)
        apply_windows(field, a, nwin - 1, at, mats)
        apply_windows(field, b + WINDOW * step, nwin - 2, at + nwin - 1 + step, mats)
    place = 0
    for out in outs:
        out[...] = field[place : place + out.shape[0], :]
        place += out.shape[0]


def phase(ph, rounds, nwin, offsets, parts, mats, sizes):
    rows = sum(part.shape[0] for part in parts)
    cols = parts[0].shape[1]
    operands = [offsets, *parts, mats]
    return pl.pallas_call(
        functools.partial(phase_kernel, ph, rounds, nwin, len(parts)),
        out_shape=tuple(jax.ShapeDtypeStruct((n, cols), jnp.float32) for n in sizes),
        in_specs=[VMEM] * len(operands),
        out_specs=(VMEM,) * len(sizes),
        scratch_shapes=[pltpu.VMEM((rows, cols), jnp.float32)],
        compiler_params=pltpu.CompilerParams(vmem_limit_bytes=VMEM_LIMIT),
        cost_estimate=pl.CostEstimate(
            flops=8 * 6 * WINDOW * WINDOW * cols, bytes_accessed=2000000, transcendentals=0
        ),
    )(*operands)


def after(value, earlier):
    return lax.optimization_barrier((value, earlier))[0]


class Gather:
    def __init__(self, plan, packed, size):
        self.plan = plan
        self.size = size
        *own, edge = packed
        devices = lax.axis_size("col")
        self.chips = devices // CORES
        self.stepwise = edge.shape[1] % 8 == 0 and devices == 4 * CORES
        self.held = {}
        self.shared = {}
        if self.stepwise:
            self.direct(0, own[0])
        ahead = shifted(edge, "row", -1)
        self.own = []
        for (_, _, _, edge_tiles, edge_at), tiles in zip(plan.groups, own):
            if edge_tiles:
                tiles = jnp.concatenate([tiles, ahead[edge_at : edge_at + edge_tiles]], 0)
            self.own.append(tiles)
        if self.stepwise:
            self.doubled(1, self.own[1], self.held[0][-1])

    def direct(self, g, tiles):
        others = [swapped(tiles, CORES * m) for m in range(1, self.chips)]
        self.held[g] = [part.reshape((1,) + tiles.shape) for part in [tiles] + others]

    def doubled(self, g, tiles, earlier=None):
        pair = (tiles, swapped(tiles, CORES))
        pair = jnp.stack(pair if earlier is None else after(pair, earlier))
        self.held[g] = [pair, swapped(pair, 2 * CORES)]

    def together(self, groups):
        if self.stepwise:
            self.direct(groups[0], jnp.concatenate([self.own[g] for g in groups], 0))
            at = 0
            for g in groups:
                self.shared[g] = (groups[0], at, self.own[g].shape[0])
                at += self.own[g].shape[0]

    def receive(self, g, earlier=None, ready=None):
        if self.stepwise:
            source, at, count = self.shared.get(g, (g, 0, self.own[g].shape[0]))
            pieces = self.held[source]
            if ready is not None:
                pieces = after(pieces, ready)
            same = jnp.concatenate([piece[:, at : at + count] for piece in pieces], 0)
            if earlier is not None:
                same = after(same, earlier)
            return (same, swapped(same, 1))
        whole = lax.all_gather(self.own[g], "col", axis=0)
        whole = jnp.moveaxis(whole, 0, 1).reshape(1, whole.shape[1], self.size, WINDOW)
        return (whole,)


def shards(evecs, offsets, refl):
    rows = evecs.shape[0]
    nwin = rows // WINDOW
    rounds = refl.shape[0]
    size = refl.shape[4] - WINDOW
    plan = Plan(rounds, nwin)
    offsets = offsets.T
    groups = len(plan.groups)
    gather = Gather(plan, pack(plan, refl), size)
    rest = rows - HALF
    parts = [evecs]
    mats = None
    results = []
    gather.together(range(2, groups))
    for ph in range(rounds):
        if ph < groups:
            ready = results[min(ph, 2) - 1] if ph else None
            tiles = gather.receive(ph, {2: parts, 3: results[-1]}.get(ph) if ph else None, ready)
        mats = matrices(plan, ph, offsets, mats, tiles)
        away = ph % 2 == 1
        sizes = (rest, HALF) if away else (HALF, rest)
        halves = phase(ph, rounds, nwin, offsets, parts, mats, sizes)
        result, kept = (halves[1], halves[0]) if away else halves
        results.append(result)
        moved = shifted(result, "row", 1 if away else -1)
        parts = [moved, kept] if away else [kept, moved]
    mats = matrices(plan, rounds, offsets, mats, tiles)
    (result,) = phase(rounds, rounds, nwin, offsets, parts, mats, (rows,))
    if rounds % 2:
        result = jnp.concatenate([shifted(result[rest:], "row", 1), result[:rest]], 0)
    return result


def solution(mesh):
    placed = (P("row", "col"), P(), P(None, None, "row", "col", None))
    return jax.shard_map(
        shards, mesh=mesh, in_specs=placed, out_specs=P("row", "col"), check_vma=False
    )
```

```python
import functools

import jax
import jax.numpy as jnp
from jax import lax
from jax.experimental import pallas as pl
from jax.experimental.pallas import tpu as pltpu
from jax.sharding import PartitionSpec as P

WINDOW = 128
HALF = 2 * WINDOW
CORES = 2
STAGE = 3
VMEM_LIMIT = 24 * 1024 * 1024
VMEM = pl.BlockSpec(memory_space=pltpu.VMEM)


def shifted(value, axis, by):
    devices = lax.axis_size(axis)
    return lax.ppermute(value, axis, [(i, (i + by) % devices) for i in range(devices)])


def swapped(value, bit):
    devices = lax.axis_size("col")
    return lax.ppermute(value, "col", [(i, i ^ bit) for i in range(devices)])


class Plan:
    def __init__(self, rounds, nwin):
        self.nwin = nwin
        self.phases = []
        for ph in range(rounds + 1):
            away = ph % 2 == 1
            entries = []
            self_carry = None
            if ph > 0:
                a, b = 2 * ph - 2, 2 * ph - 1
                if away:
                    entries += [(a, nwin - 1), None, (b, nwin - 1), (b, nwin)]
                    self_carry = (1, self.count(ph - 1) - 1)
                else:
                    entries += [(a, 1), (b, 0), (b, 1), None]
                    self_carry = (3, self.count(ph - 1) - (nwin - 1))
            if ph < rounds:
                base = 2 if away else 0
                for sweep in (2 * ph, 2 * ph + 1):
                    entries += [(sweep, base + k) for k in range(nwin - 1)]
            self.phases.append((entries, self_carry))
        groups = [[ph] for ph in range(rounds - 1)] + [[rounds - 1, rounds]]
        self.groups = []
        self.where = {}
        edge_at = 0
        for g, members in enumerate(groups):
            wanted = [w for ph in members for w in self.phases[ph][0] if w is not None]
            own = [w for w in wanted if w[1] < nwin]
            edge = [w for w in wanted if w[1] == nwin]
            place = 0
            for part in (own, edge):
                for i, w in enumerate(part):
                    self.where[w] = (g, place + i, place + len(part) + i // 2, i % 2)
                place += len(part) + (len(part) + 1) // 2
            own_tiles = len(own) + (len(own) + 1) // 2
            edge_tiles = place - own_tiles
            self.groups.append((own, edge, own_tiles, edge_tiles, edge_at))
            edge_at += edge_tiles
        self.edge_tiles = edge_at

    def count(self, ph):
        return len(self.phases[ph][0])


def pack_kernel(plan, refl_ref, *outs):
    size = refl_ref.shape[-1] - WINDOW
    mine = refl_ref.shape[-2]

    def fill(out, at, windows):
        for i, (sweep, k) in enumerate(windows):
            out[at + i] = refl_ref[sweep // 2, sweep % 2, k, :, :WINDOW]
        at += len(windows)
        for i in range(0, len(windows), 2):
            halves = []
            for sweep, k in windows[i : i + 2]:
                halves.append(refl_ref[sweep // 2, sweep % 2, k, :, WINDOW:])
            if len(halves) == 1:
                halves.append(jnp.zeros((mine, size), jnp.float32))
            out[at + i // 2] = jnp.concatenate(halves, -1)

    for group, out in zip(plan.groups, outs):
        fill(out, 0, group[0])
    for group in plan.groups:
        if group[1]:
            fill(outs[-1], group[4], [(sweep, 0) for sweep, _ in group[1]])


def pack(plan, refl):
    mine = refl.shape[3]
    counts = [group[2] for group in plan.groups] + [plan.edge_tiles]
    return pl.pallas_call(
        functools.partial(pack_kernel, plan),
        out_shape=tuple(jax.ShapeDtypeStruct((n, mine, WINDOW), jnp.float32) for n in counts),
        in_specs=[VMEM],
        out_specs=(VMEM,) * len(counts),
        compiler_params=pltpu.CompilerParams(vmem_limit_bytes=VMEM_LIMIT),
    )(refl)


def split(value):
    high = value.astype(jnp.bfloat16)
    return high, (value - high.astype(jnp.float32)).astype(jnp.bfloat16)


def fold(value):
    half = value.shape[1] // 2
    return value[:, :half] + value[:, half:]


def matrix_kernel(plan, ph, masked, *refs):
    entries, carry = plan.phases[ph]
    operands = list(refs)
    refs = operands[1:] if masked else operands
    offsets = operands[0][...] if masked else None
    old_ref = refs.pop(0) if carry else None
    tiles = refs.pop()
    out_ref = refs.pop()
    parts = refs
    here = lax.axis_index("col")
    if len(parts) == 2:
        for m in range(parts[0].shape[0]):
            other = lax.bitwise_xor(here, m * CORES)
            tiles[other] = parts[0][m]
            tiles[lax.bitwise_xor(other, 1)] = parts[1][m]
    else:
        tiles = parts[0]
    size = tiles.shape[0] * tiles.shape[2]
    last = lax.axis_index("row") == lax.axis_size("row") - 1
    lane = lax.broadcasted_iota(jnp.int32, (size, WINDOW), 1)
    row_id = lax.broadcasted_iota(jnp.int32, (WINDOW, WINDOW), 0)
    col_id = lax.broadcasted_iota(jnp.int32, (WINDOW, WINDOW), 1)
    unit = jnp.where(row_id == col_id, 1.0, 0.0).astype(jnp.float32)

    def first(window):
        sweep, k = window
        _, vec_tile, fac_tile, side = plan.where[window]
        vectors = tiles[:, vec_tile].reshape(size, WINDOW)
        factors = tiles[:, fac_tile].reshape(size, WINDOW)
        if k == plan.nwin - 1:
            start = offsets[sweep % 2 : sweep % 2 + 1, sweep // 2 : sweep // 2 + 1]
            limit = jnp.where(last, WINDOW - start, WINDOW)
            vectors = jnp.where(lane < limit, vectors, 0.0)
        rows_hi, rows_lo = split(vectors)
        pair = jnp.concatenate([rows_hi, rows_lo], 1)
        blank = jnp.zeros_like(pair)
        stack = [blank, pair, blank, pair] if side else [pair, blank, pair, blank]
        scaled = jnp.dot(
            jnp.concatenate(split(factors), 1),
            jnp.concatenate(stack, 0),
            preferred_element_type=jnp.float32,
        )
        return jnp.concatenate([rows_hi, rows_lo], 0), scaled

    def second(rows, scaled):
        pair = jnp.concatenate(split(fold(scaled)), 1)
        product = lax.dot_general(
            rows,
            jnp.concatenate([pair, pair], 0),
            (((0,), (0,)), ((), ())),
            preferred_element_type=jnp.float32,
        )
        return jnp.concatenate(split(unit - fold(product)), 1)

    fresh = [i for i, window in enumerate(entries) if window is not None]
    for at in range(0, len(fresh), STAGE):
        some = fresh[at : at + STAGE]
        halves = [first(entries[i]) for i in some]
        for i, half in zip(some, halves):
            out_ref[i] = second(*half)
    if carry:
        out_ref[carry[0]] = old_ref[carry[1]]


def matrices(plan, ph, offsets, before, parts):
    count = plan.count(ph)
    carried = (before,) if plan.phases[ph][1] else ()
    masked = any(w is not None and w[1] == plan.nwin - 1 for w in plan.phases[ph][0])
    operands = [*([offsets] if masked else []), *carried, *parts]
    whole = (sum(part.shape[0] for part in parts),) + parts[0].shape[1:]
    return pl.pallas_call(
        functools.partial(matrix_kernel, plan, ph, masked),
        out_shape=jax.ShapeDtypeStruct((count, WINDOW, 2 * WINDOW), jnp.bfloat16),
        in_specs=[VMEM] * len(operands),
        out_specs=VMEM,
        scratch_shapes=[pltpu.VMEM(whole, jnp.float32)],
        compiler_params=pltpu.CompilerParams(vmem_limit_bytes=VMEM_LIMIT),
        cost_estimate=pl.CostEstimate(
            flops=count * 12 * 64 * 128 * 192, bytes_accessed=count * 100000, transcendentals=0
        ),
    )(*operands)


def apply_windows(field, at, count, first, mats):
    rows = field[pl.ds(at, count * WINDOW), :]
    stacks = []
    for k in range(count):
        pair = jnp.concatenate(split(rows[k * WINDOW : (k + 1) * WINDOW]), 1)
        stacks.append(jnp.concatenate([pair, pair], 0))
    products = [
        jnp.dot(mats[first + k], stack, preferred_element_type=jnp.float32)
        for k, stack in enumerate(stacks)
    ]
    updated = jnp.concatenate([fold(product) for product in products], 0)
    field[pl.ds(at, count * WINDOW), :] = updated


def phase_kernel(ph, rounds, nwin, nparts, offsets_ref, *refs):
    parts = refs[:nparts]
    mats = refs[nparts]
    outs = refs[nparts + 1 : -1]
    field = refs[-1]
    place = 0
    for part in parts:
        field[place : place + part.shape[0], :] = part[...]
        place += part.shape[0]
    offsets = offsets_ref[...]
    at = 0
    if ph > 0:
        a, b = offsets[0, ph - 1], offsets[1, ph - 1]
        step = jnp.where(b < a, 1, 0)
        start = nwin - 3 if ph % 2 else 1
        apply_windows(field, a + WINDOW * start, 1, 0, mats)
        start = nwin - 4 if ph % 2 else 0
        apply_windows(field, b + WINDOW * (start + step), 2, 1 + step, mats)
        at = 4
    if ph < rounds:
        a, b = offsets[0, ph], offsets[1, ph]
        step = jnp.where(b < a, 1, 0)
        apply_windows(field, a, nwin - 1, at, mats)
        apply_windows(field, b + WINDOW * step, nwin - 2, at + nwin - 1 + step, mats)
    place = 0
    for out in outs:
        out[...] = field[place : place + out.shape[0], :]
        place += out.shape[0]


def phase(ph, rounds, nwin, offsets, parts, mats, sizes):
    rows = sum(part.shape[0] for part in parts)
    cols = parts[0].shape[1]
    operands = [offsets, *parts, mats]
    return pl.pallas_call(
        functools.partial(phase_kernel, ph, rounds, nwin, len(parts)),
        out_shape=tuple(jax.ShapeDtypeStruct((n, cols), jnp.float32) for n in sizes),
        in_specs=[VMEM] * len(operands),
        out_specs=(VMEM,) * len(sizes),
        scratch_shapes=[pltpu.VMEM((rows, cols), jnp.float32)],
        compiler_params=pltpu.CompilerParams(vmem_limit_bytes=VMEM_LIMIT),
        cost_estimate=pl.CostEstimate(
            flops=8 * 6 * WINDOW * WINDOW * cols, bytes_accessed=2000000, transcendentals=0
        ),
    )(*operands)


def after(value, earlier):
    return lax.optimization_barrier((value, earlier))[0]


class Gather:
    def __init__(self, plan, packed, size):
        self.plan = plan
        self.size = size
        *own, edge = packed
        devices = lax.axis_size("col")
        self.chips = devices // CORES
        self.stepwise = edge.shape[1] % 8 == 0 and devices == 4 * CORES
        self.held = {}
        self.shared = {}
        if self.stepwise:
            self.direct(0, own[0])
        ahead = shifted(edge, "row", -1)
        self.own = []
        for (_, _, _, edge_tiles, edge_at), tiles in zip(plan.groups, own):
            if edge_tiles:
                tiles = jnp.concatenate([tiles, ahead[edge_at : edge_at + edge_tiles]], 0)
            self.own.append(tiles)
        if self.stepwise:
            self.doubled(1, self.own[1], self.held[0][-1])

    def direct(self, g, tiles):
        others = [swapped(tiles, CORES * m) for m in range(1, self.chips)]
        self.held[g] = [part.reshape((1,) + tiles.shape) for part in [tiles] + others]

    def doubled(self, g, tiles, earlier=None):
        pair = (tiles, swapped(tiles, CORES))
        pair = jnp.stack(pair if earlier is None else after(pair, earlier))
        self.held[g] = [pair, swapped(pair, 2 * CORES)]

    def together(self, groups):
        if self.stepwise:
            self.direct(groups[0], jnp.concatenate([self.own[g] for g in groups], 0))
            at = 0
            for g in groups:
                self.shared[g] = (groups[0], at, self.own[g].shape[0])
                at += self.own[g].shape[0]

    def receive(self, g, earlier=None, ready=None):
        if self.stepwise:
            source, at, count = self.shared.get(g, (g, 0, self.own[g].shape[0]))
            pieces = self.held[source]
            if ready is not None:
                pieces = after(pieces, ready)
            same = jnp.concatenate([piece[:, at : at + count] for piece in pieces], 0)
            if earlier is not None:
                same = after(same, earlier)
            return (same, swapped(same, 1))
        whole = lax.all_gather(self.own[g], "col", axis=0)
        whole = jnp.moveaxis(whole, 0, 1).reshape(1, whole.shape[1], self.size, WINDOW)
        return (whole,)


def shards(evecs, offsets, refl):
    rows = evecs.shape[0]
    nwin = rows // WINDOW
    rounds = refl.shape[0]
    size = refl.shape[4] - WINDOW
    plan = Plan(rounds, nwin)
    offsets = offsets.T
    groups = len(plan.groups)
    gather = Gather(plan, pack(plan, refl), size)
    rest = rows - HALF
    parts = [evecs]
    mats = None
    results, movements = [], []
    gather.together(range(2, groups))
    for ph in range(rounds):
        if ph < groups:
            ready = results[min(ph, 2) - 1] if ph else None
            tiles = gather.receive(ph, movements[1] if ph > 1 else None, ready)
        mats = matrices(plan, ph, offsets, mats, tiles)
        away = ph % 2 == 1
        sizes = (rest, HALF) if away else (HALF, rest)
        halves = phase(ph, rounds, nwin, offsets, parts, mats, sizes)
        result, kept = (halves[1], halves[0]) if away else halves
        results.append(result)
        moved = shifted(result, "row", 1 if away else -1)
        movements.append(moved)
        parts = [moved, kept] if away else [kept, moved]
    mats = matrices(plan, rounds, offsets, mats, tiles)
    (result,) = phase(rounds, rounds, nwin, offsets, parts, mats, (rows,))
    if rounds % 2:
        result = jnp.concatenate([shifted(result[rest:], "row", 1), result[:rest]], 0)
    return result


def solution(mesh):
    placed = (P("row", "col"), P(), P(None, None, "row", "col", None))
    return jax.shard_map(
        shards, mesh=mesh, in_specs=placed, out_specs=P("row", "col"), check_vma=False
    )
```

```python
import functools

import jax
import jax.numpy as jnp
from jax import lax
from jax.experimental import pallas as pl
from jax.experimental.pallas import tpu as pltpu
from jax.sharding import PartitionSpec as P

WINDOW = 128
HALF = 2 * WINDOW
CORES = 2
STAGE = 3
VMEM_LIMIT = 24 * 1024 * 1024
VMEM = pl.BlockSpec(memory_space=pltpu.VMEM)


def shifted(value, axis, by):
    devices = lax.axis_size(axis)
    return lax.ppermute(value, axis, [(i, (i + by) % devices) for i in range(devices)])


def swapped(value, bit):
    devices = lax.axis_size("col")
    return lax.ppermute(value, "col", [(i, i ^ bit) for i in range(devices)])


class Plan:
    def __init__(self, rounds, nwin):
        self.nwin = nwin
        self.phases = []
        for ph in range(rounds + 1):
            away = ph % 2 == 1
            entries = []
            self_carry = None
            if ph > 0:
                a, b = 2 * ph - 2, 2 * ph - 1
                if away:
                    entries += [(a, nwin - 1), None, (b, nwin - 1), (b, nwin)]
                    self_carry = (1, self.count(ph - 1) - 1)
                else:
                    entries += [(a, 1), (b, 0), (b, 1), None]
                    self_carry = (3, self.count(ph - 1) - (nwin - 1))
            if ph < rounds:
                base = 2 if away else 0
                for sweep in (2 * ph, 2 * ph + 1):
                    entries += [(sweep, base + k) for k in range(nwin - 1)]
            self.phases.append((entries, self_carry))
        groups = [[ph] for ph in range(rounds - 1)] + [[rounds - 1, rounds]]
        self.groups = []
        self.where = {}
        edge_at = 0
        for g, members in enumerate(groups):
            wanted = [w for ph in members for w in self.phases[ph][0] if w is not None]
            own = [w for w in wanted if w[1] < nwin]
            edge = [w for w in wanted if w[1] == nwin]
            place = 0
            for part in (own, edge):
                for i, w in enumerate(part):
                    self.where[w] = (g, place + i, place + len(part) + i // 2, i % 2)
                place += len(part) + (len(part) + 1) // 2
            own_tiles = len(own) + (len(own) + 1) // 2
            edge_tiles = place - own_tiles
            self.groups.append((own, edge, own_tiles, edge_tiles, edge_at))
            edge_at += edge_tiles
        self.edge_tiles = edge_at

    def count(self, ph):
        return len(self.phases[ph][0])


def pack_kernel(plan, refl_ref, *outs):
    size = refl_ref.shape[-1] - WINDOW
    mine = refl_ref.shape[-2]

    def fill(out, at, windows):
        for i, (sweep, k) in enumerate(windows):
            out[at + i] = refl_ref[sweep // 2, sweep % 2, k, :, :WINDOW]
        at += len(windows)
        for i in range(0, len(windows), 2):
            halves = []
            for sweep, k in windows[i : i + 2]:
                halves.append(refl_ref[sweep // 2, sweep % 2, k, :, WINDOW:])
            if len(halves) == 1:
                halves.append(jnp.zeros((mine, size), jnp.float32))
            out[at + i // 2] = jnp.concatenate(halves, -1)

    for group, out in zip(plan.groups, outs):
        fill(out, 0, group[0])
    for group in plan.groups:
        if group[1]:
            fill(outs[-1], group[4], [(sweep, 0) for sweep, _ in group[1]])


def pack(plan, refl):
    mine = refl.shape[3]
    counts = [group[2] for group in plan.groups] + [plan.edge_tiles]
    return pl.pallas_call(
        functools.partial(pack_kernel, plan),
        out_shape=tuple(jax.ShapeDtypeStruct((n, mine, WINDOW), jnp.float32) for n in counts),
        in_specs=[VMEM],
        out_specs=(VMEM,) * len(counts),
        compiler_params=pltpu.CompilerParams(vmem_limit_bytes=VMEM_LIMIT),
    )(refl)


def split(value):
    high = value.astype(jnp.bfloat16)
    return high, (value - high.astype(jnp.float32)).astype(jnp.bfloat16)


def fold(value):
    half = value.shape[1] // 2
    return value[:, :half] + value[:, half:]


def matrix_kernel(plan, ph, masked, *refs):
    entries, carry = plan.phases[ph]
    operands = list(refs)
    refs = operands[1:] if masked else operands
    offsets = operands[0][...] if masked else None
    old_ref = refs.pop(0) if carry else None
    tiles = refs.pop()
    out_ref = refs.pop()
    parts = refs
    here = lax.axis_index("col")
    if len(parts) == 2:
        for m in range(parts[0].shape[0]):
            other = lax.bitwise_xor(here, m * CORES)
            tiles[other] = parts[0][m]
            tiles[lax.bitwise_xor(other, 1)] = parts[1][m]
    else:
        tiles = parts[0]
    size = tiles.shape[0] * tiles.shape[2]
    last = lax.axis_index("row") == lax.axis_size("row") - 1
    lane = lax.broadcasted_iota(jnp.int32, (size, WINDOW), 1)
    row_id = lax.broadcasted_iota(jnp.int32, (WINDOW, WINDOW), 0)
    col_id = lax.broadcasted_iota(jnp.int32, (WINDOW, WINDOW), 1)
    unit = jnp.where(row_id == col_id, 1.0, 0.0).astype(jnp.float32)

    def first(window):
        sweep, k = window
        _, vec_tile, fac_tile, side = plan.where[window]
        vectors = tiles[:, vec_tile].reshape(size, WINDOW)
        factors = tiles[:, fac_tile].reshape(size, WINDOW)
        if k == plan.nwin - 1:
            start = offsets[sweep % 2 : sweep % 2 + 1, sweep // 2 : sweep // 2 + 1]
            limit = jnp.where(last, WINDOW - start, WINDOW)
            vectors = jnp.where(lane < limit, vectors, 0.0)
        rows_hi, rows_lo = split(vectors)
        pair = jnp.concatenate([rows_hi, rows_lo], 1)
        blank = jnp.zeros_like(pair)
        stack = [blank, pair, blank, pair] if side else [pair, blank, pair, blank]
        scaled = jnp.dot(
            jnp.concatenate(split(factors), 1),
            jnp.concatenate(stack, 0),
            preferred_element_type=jnp.float32,
        )
        return jnp.concatenate([rows_hi, rows_lo], 0), scaled

    def second(rows, scaled):
        pair = jnp.concatenate(split(fold(scaled)), 1)
        product = lax.dot_general(
            rows,
            jnp.concatenate([pair, pair], 0),
            (((0,), (0,)), ((), ())),
            preferred_element_type=jnp.float32,
        )
        return jnp.concatenate(split(unit - fold(product)), 1)

    fresh = [i for i, window in enumerate(entries) if window is not None]
    for at in range(0, len(fresh), STAGE):
        some = fresh[at : at + STAGE]
        halves = [first(entries[i]) for i in some]
        for i, half in zip(some, halves):
            out_ref[i] = second(*half)
    if carry:
        out_ref[carry[0]] = old_ref[carry[1]]


def matrices(plan, ph, offsets, before, parts):
    count = plan.count(ph)
    carried = (before,) if plan.phases[ph][1] else ()
    masked = any(w is not None and w[1] == plan.nwin - 1 for w in plan.phases[ph][0])
    operands = [*([offsets] if masked else []), *carried, *parts]
    whole = (sum(part.shape[0] for part in parts),) + parts[0].shape[1:]
    return pl.pallas_call(
        functools.partial(matrix_kernel, plan, ph, masked),
        out_shape=jax.ShapeDtypeStruct((count, WINDOW, 2 * WINDOW), jnp.bfloat16),
        in_specs=[VMEM] * len(operands),
        out_specs=VMEM,
        scratch_shapes=[pltpu.VMEM(whole, jnp.float32)],
        compiler_params=pltpu.CompilerParams(vmem_limit_bytes=VMEM_LIMIT),
        cost_estimate=pl.CostEstimate(
            flops=count * 12 * 64 * 128 * 192, bytes_accessed=count * 100000, transcendentals=0
        ),
    )(*operands)


def apply_windows(field, at, count, first, mats):
    rows = field[pl.ds(at, count * WINDOW), :]
    stacks = []
    for k in range(count):
        pair = jnp.concatenate(split(rows[k * WINDOW : (k + 1) * WINDOW]), 1)
        stacks.append(jnp.concatenate([pair, pair], 0))
    products = [
        jnp.dot(mats[first + k], stack, preferred_element_type=jnp.float32)
        for k, stack in enumerate(stacks)
    ]
    updated = jnp.concatenate([fold(product) for product in products], 0)
    field[pl.ds(at, count * WINDOW), :] = updated


def phase_kernel(ph, rounds, nwin, nparts, offsets_ref, *refs):
    parts = refs[:nparts]
    mats = refs[nparts]
    outs = refs[nparts + 1 : -1]
    field = refs[-1]
    place = 0
    for part in parts:
        field[place : place + part.shape[0], :] = part[...]
        place += part.shape[0]
    offsets = offsets_ref[...]
    at = 0
    if ph > 0:
        a, b = offsets[0, ph - 1], offsets[1, ph - 1]
        step = jnp.where(b < a, 1, 0)
        start = nwin - 3 if ph % 2 else 1
        apply_windows(field, a + WINDOW * start, 1, 0, mats)
        start = nwin - 4 if ph % 2 else 0
        apply_windows(field, b + WINDOW * (start + step), 2, 1 + step, mats)
        at = 4
    if ph < rounds:
        a, b = offsets[0, ph], offsets[1, ph]
        step = jnp.where(b < a, 1, 0)
        apply_windows(field, a, nwin - 1, at, mats)
        apply_windows(field, b + WINDOW * step, nwin - 2, at + nwin - 1 + step, mats)
    place = 0
    for out in outs:
        out[...] = field[place : place + out.shape[0], :]
        place += out.shape[0]


def phase(ph, rounds, nwin, offsets, parts, mats, sizes):
    rows = sum(part.shape[0] for part in parts)
    cols = parts[0].shape[1]
    operands = [offsets, *parts, mats]
    return pl.pallas_call(
        functools.partial(phase_kernel, ph, rounds, nwin, len(parts)),
        out_shape=tuple(jax.ShapeDtypeStruct((n, cols), jnp.float32) for n in sizes),
        in_specs=[VMEM] * len(operands),
        out_specs=(VMEM,) * len(sizes),
        scratch_shapes=[pltpu.VMEM((rows, cols), jnp.float32)],
        compiler_params=pltpu.CompilerParams(vmem_limit_bytes=VMEM_LIMIT),
        cost_estimate=pl.CostEstimate(
            flops=8 * 6 * WINDOW * WINDOW * cols, bytes_accessed=2000000, transcendentals=0
        ),
    )(*operands)


def after(value, earlier):
    return lax.optimization_barrier((value, earlier))[0]


class Gather:
    def __init__(self, plan, packed, size):
        self.plan = plan
        self.size = size
        *own, edge = packed
        devices = lax.axis_size("col")
        self.chips = devices // CORES
        self.stepwise = edge.shape[1] % 8 == 0 and devices == 4 * CORES
        self.held = {}
        self.shared = {}
        if self.stepwise:
            self.direct(0, own[0])
        ahead = shifted(edge, "row", -1)
        self.own = []
        for (_, _, _, edge_tiles, edge_at), tiles in zip(plan.groups, own):
            if edge_tiles:
                tiles = jnp.concatenate([tiles, ahead[edge_at : edge_at + edge_tiles]], 0)
            self.own.append(tiles)
        if self.stepwise:
            self.doubled(1, self.own[1], self.held[0][-1])

    def direct(self, g, tiles):
        others = [swapped(tiles, CORES * m) for m in range(1, self.chips)]
        self.held[g] = [part.reshape((1,) + tiles.shape) for part in [tiles] + others]

    def doubled(self, g, tiles, earlier=None):
        pair = (tiles, swapped(tiles, CORES))
        pair = jnp.stack(pair if earlier is None else after(pair, earlier))
        self.held[g] = [pair, swapped(pair, 2 * CORES)]

    def together(self, groups):
        if self.stepwise:
            self.direct(groups[0], jnp.concatenate([self.own[g] for g in groups], 0))
            at = 0
            for g in groups:
                self.shared[g] = (groups[0], at, self.own[g].shape[0])
                at += self.own[g].shape[0]

    def receive(self, g, earlier=None, ready=None):
        if self.stepwise:
            source, at, count = self.shared.get(g, (g, 0, self.own[g].shape[0]))
            pieces = self.held[source]
            if ready is not None:
                pieces = after(pieces, ready)
            same = jnp.concatenate([piece[:, at : at + count] for piece in pieces], 0)
            if earlier is not None:
                same = after(same, earlier)
            return (same, swapped(same, 1))
        whole = lax.all_gather(self.own[g], "col", axis=0)
        whole = jnp.moveaxis(whole, 0, 1).reshape(1, whole.shape[1], self.size, WINDOW)
        return (whole,)


def shards(evecs, offsets, refl):
    rows = evecs.shape[0]
    nwin = rows // WINDOW
    rounds = refl.shape[0]
    size = refl.shape[4] - WINDOW
    plan = Plan(rounds, nwin)
    offsets = offsets.T
    groups = len(plan.groups)
    gather = Gather(plan, pack(plan, refl), size)
    rest = rows - HALF
    parts = [evecs]
    mats = None
    results, movements = [], []
    gather.together(range(2, groups))
    for ph in range(rounds):
        if ph < groups:
            ready = results[min(ph, 2) - 1] if ph else None
            tiles = gather.receive(ph, movements[min(ph, 2) - 1] if ph else None, ready)
        mats = matrices(plan, ph, offsets, mats, tiles)
        away = ph % 2 == 1
        sizes = (rest, HALF) if away else (HALF, rest)
        halves = phase(ph, rounds, nwin, offsets, parts, mats, sizes)
        result, kept = (halves[1], halves[0]) if away else halves
        results.append(result)
        moved = shifted(result, "row", 1 if away else -1)
        movements.append(moved)
        parts = [moved, kept] if away else [kept, moved]
    mats = matrices(plan, rounds, offsets, mats, tiles)
    (result,) = phase(rounds, rounds, nwin, offsets, parts, mats, (rows,))
    if rounds % 2:
        result = jnp.concatenate([shifted(result[rest:], "row", 1), result[:rest]], 0)
    return result


def solution(mesh):
    placed = (P("row", "col"), P(), P(None, None, "row", "col", None))
    return jax.shard_map(
        shards, mesh=mesh, in_specs=placed, out_specs=P("row", "col"), check_vma=False
    )
```

```python
import functools

import jax
import jax.numpy as jnp
from jax import lax
from jax.experimental import pallas as pl
from jax.experimental.pallas import tpu as pltpu
from jax.sharding import PartitionSpec as P

WINDOW = 128
HALF = 2 * WINDOW
CORES = 2
STAGE = 3
VMEM_LIMIT = 24 * 1024 * 1024
VMEM = pl.BlockSpec(memory_space=pltpu.VMEM)


def shifted(value, axis, by):
    devices = lax.axis_size(axis)
    return lax.ppermute(value, axis, [(i, (i + by) % devices) for i in range(devices)])


def swapped(value, bit):
    devices = lax.axis_size("col")
    return lax.ppermute(value, "col", [(i, i ^ bit) for i in range(devices)])


class Plan:
    def __init__(self, rounds, nwin):
        self.nwin = nwin
        self.phases = []
        for ph in range(rounds + 1):
            away = ph % 2 == 1
            entries = []
            self_carry = None
            if ph > 0:
                a, b = 2 * ph - 2, 2 * ph - 1
                if away:
                    entries += [(a, nwin - 1), None, (b, nwin - 1), (b, nwin)]
                    self_carry = (1, self.count(ph - 1) - 1)
                else:
                    entries += [(a, 1), (b, 0), (b, 1), None]
                    self_carry = (3, self.count(ph - 1) - (nwin - 1))
            if ph < rounds:
                base = 2 if away else 0
                for sweep in (2 * ph, 2 * ph + 1):
                    entries += [(sweep, base + k) for k in range(nwin - 1)]
            self.phases.append((entries, self_carry))
        groups = [[ph] for ph in range(rounds - 1)] + [[rounds - 1, rounds]]
        self.groups = []
        self.where = {}
        edge_at = 0
        for g, members in enumerate(groups):
            wanted = [w for ph in members for w in self.phases[ph][0] if w is not None]
            own = [w for w in wanted if w[1] < nwin]
            edge = [w for w in wanted if w[1] == nwin]
            place = 0
            for part in (own, edge):
                for i, w in enumerate(part):
                    self.where[w] = (g, place + i, place + len(part) + i // 2, i % 2)
                place += len(part) + (len(part) + 1) // 2
            own_tiles = len(own) + (len(own) + 1) // 2
            edge_tiles = place - own_tiles
            self.groups.append((own, edge, own_tiles, edge_tiles, edge_at))
            edge_at += edge_tiles
        self.edge_tiles = edge_at

    def count(self, ph):
        return len(self.phases[ph][0])


def pack_kernel(plan, refl_ref, *outs):
    size = refl_ref.shape[-1] - WINDOW
    mine = refl_ref.shape[-2]

    def fill(out, at, windows):
        for i, (sweep, k) in enumerate(windows):
            out[at + i] = refl_ref[sweep // 2, sweep % 2, k, :, :WINDOW]
        at += len(windows)
        for i in range(0, len(windows), 2):
            halves = []
            for sweep, k in windows[i : i + 2]:
                halves.append(refl_ref[sweep // 2, sweep % 2, k, :, WINDOW:])
            if len(halves) == 1:
                halves.append(jnp.zeros((mine, size), jnp.float32))
            out[at + i // 2] = jnp.concatenate(halves, -1)

    for group, out in zip(plan.groups, outs):
        fill(out, 0, group[0])
    for group in plan.groups:
        if group[1]:
            fill(outs[-1], group[4], [(sweep, 0) for sweep, _ in group[1]])


def pack(plan, refl):
    mine = refl.shape[3]
    counts = [group[2] for group in plan.groups] + [plan.edge_tiles]
    return pl.pallas_call(
        functools.partial(pack_kernel, plan),
        out_shape=tuple(jax.ShapeDtypeStruct((n, mine, WINDOW), jnp.float32) for n in counts),
        in_specs=[VMEM],
        out_specs=(VMEM,) * len(counts),
        compiler_params=pltpu.CompilerParams(vmem_limit_bytes=VMEM_LIMIT),
    )(refl)


def split(value):
    high = value.astype(jnp.bfloat16)
    return high, (value - high.astype(jnp.float32)).astype(jnp.bfloat16)


def fold(value):
    half = value.shape[1] // 2
    return value[:, :half] + value[:, half:]


def matrix_kernel(plan, ph, masked, *refs):
    entries, carry = plan.phases[ph]
    operands = list(refs)
    refs = operands[1:] if masked else operands
    offsets = operands[0][...] if masked else None
    old_ref = refs.pop(0) if carry else None
    tiles = refs.pop()
    out_ref = refs.pop()
    parts = refs
    here = lax.axis_index("col")
    if len(parts) == 2:
        for m in range(parts[0].shape[0]):
            other = lax.bitwise_xor(here, m * CORES)
            tiles[other] = parts[0][m]
            tiles[lax.bitwise_xor(other, 1)] = parts[1][m]
    else:
        tiles = parts[0]
    size = tiles.shape[0] * tiles.shape[2]
    last = lax.axis_index("row") == lax.axis_size("row") - 1
    lane = lax.broadcasted_iota(jnp.int32, (size, WINDOW), 1)
    row_id = lax.broadcasted_iota(jnp.int32, (WINDOW, WINDOW), 0)
    col_id = lax.broadcasted_iota(jnp.int32, (WINDOW, WINDOW), 1)
    unit = jnp.where(row_id == col_id, 1.0, 0.0).astype(jnp.float32)

    def first(window):
        sweep, k = window
        _, vec_tile, fac_tile, side = plan.where[window]
        vectors = tiles[:, vec_tile].reshape(size, WINDOW)
        factors = tiles[:, fac_tile].reshape(size, WINDOW)
        if k == plan.nwin - 1:
            start = offsets[sweep % 2 : sweep % 2 + 1, sweep // 2 : sweep // 2 + 1]
            limit = jnp.where(last, WINDOW - start, WINDOW)
            vectors = jnp.where(lane < limit, vectors, 0.0)
        rows_hi, rows_lo = split(vectors)
        pair = jnp.concatenate([rows_hi, rows_lo], 1)
        blank = jnp.zeros_like(pair)
        stack = [blank, pair, blank, pair] if side else [pair, blank, pair, blank]
        scaled = jnp.dot(
            jnp.concatenate(split(factors), 1),
            jnp.concatenate(stack, 0),
            preferred_element_type=jnp.float32,
        )
        return jnp.concatenate([rows_hi, rows_lo], 0), scaled

    def second(rows, scaled):
        pair = jnp.concatenate(split(fold(scaled)), 1)
        product = lax.dot_general(
            rows,
            jnp.concatenate([pair, pair], 0),
            (((0,), (0,)), ((), ())),
            preferred_element_type=jnp.float32,
        )
        return jnp.concatenate(split(unit - fold(product)), 1)

    fresh = [i for i, window in enumerate(entries) if window is not None]
    for at in range(0, len(fresh), STAGE):
        some = fresh[at : at + STAGE]
        halves = [first(entries[i]) for i in some]
        for i, half in zip(some, halves):
            out_ref[i] = second(*half)
    if carry:
        out_ref[carry[0]] = old_ref[carry[1]]


def matrices(plan, ph, offsets, before, parts):
    count = plan.count(ph)
    carried = (before,) if plan.phases[ph][1] else ()
    masked = any(w is not None and w[1] == plan.nwin - 1 for w in plan.phases[ph][0])
    operands = [*([offsets] if masked else []), *carried, *parts]
    whole = (sum(part.shape[0] for part in parts),) + parts[0].shape[1:]
    return pl.pallas_call(
        functools.partial(matrix_kernel, plan, ph, masked),
        out_shape=jax.ShapeDtypeStruct((count, WINDOW, 2 * WINDOW), jnp.bfloat16),
        in_specs=[VMEM] * len(operands),
        out_specs=VMEM,
        scratch_shapes=[pltpu.VMEM(whole, jnp.float32)],
        compiler_params=pltpu.CompilerParams(vmem_limit_bytes=VMEM_LIMIT),
        cost_estimate=pl.CostEstimate(
            flops=count * 12 * 64 * 128 * 192, bytes_accessed=count * 100000, transcendentals=0
        ),
    )(*operands)


def apply_windows(field, at, count, first, mats):
    rows = field[pl.ds(at, count * WINDOW), :]
    stacks = []
    for k in range(count):
        pair = jnp.concatenate(split(rows[k * WINDOW : (k + 1) * WINDOW]), 1)
        stacks.append(jnp.concatenate([pair, pair], 0))
    products = [
        jnp.dot(mats[first + k], stack, preferred_element_type=jnp.float32)
        for k, stack in enumerate(stacks)
    ]
    updated = jnp.concatenate([fold(product) for product in products], 0)
    field[pl.ds(at, count * WINDOW), :] = updated


def phase_kernel(ph, rounds, nwin, nparts, offsets_ref, *refs):
    parts = refs[:nparts]
    mats = refs[nparts]
    outs = refs[nparts + 1 : -1]
    field = refs[-1]
    place = 0
    for part in parts:
        field[place : place + part.shape[0], :] = part[...]
        place += part.shape[0]
    offsets = offsets_ref[...]
    at = 0
    if ph > 0:
        a, b = offsets[0, ph - 1], offsets[1, ph - 1]
        step = jnp.where(b < a, 1, 0)
        start = nwin - 3 if ph % 2 else 1
        apply_windows(field, a + WINDOW * start, 1, 0, mats)
        start = nwin - 4 if ph % 2 else 0
        apply_windows(field, b + WINDOW * (start + step), 2, 1 + step, mats)
        at = 4
    if ph < rounds:
        a, b = offsets[0, ph], offsets[1, ph]
        step = jnp.where(b < a, 1, 0)
        apply_windows(field, a, nwin - 1, at, mats)
        apply_windows(field, b + WINDOW * step, nwin - 2, at + nwin - 1 + step, mats)
    place = 0
    for out in outs:
        out[...] = field[place : place + out.shape[0], :]
        place += out.shape[0]


def phase(ph, rounds, nwin, offsets, parts, mats, sizes):
    rows = sum(part.shape[0] for part in parts)
    cols = parts[0].shape[1]
    operands = [offsets, *parts, mats]
    return pl.pallas_call(
        functools.partial(phase_kernel, ph, rounds, nwin, len(parts)),
        out_shape=tuple(jax.ShapeDtypeStruct((n, cols), jnp.float32) for n in sizes),
        in_specs=[VMEM] * len(operands),
        out_specs=(VMEM,) * len(sizes),
        scratch_shapes=[pltpu.VMEM((rows, cols), jnp.float32)],
        compiler_params=pltpu.CompilerParams(vmem_limit_bytes=VMEM_LIMIT),
        cost_estimate=pl.CostEstimate(
            flops=8 * 6 * WINDOW * WINDOW * cols, bytes_accessed=2000000, transcendentals=0
        ),
    )(*operands)


def after(value, earlier):
    return lax.optimization_barrier((value, earlier))[0]


class Gather:
    def __init__(self, plan, packed, size):
        self.plan = plan
        self.size = size
        *own, edge = packed
        devices = lax.axis_size("col")
        self.chips = devices // CORES
        self.stepwise = edge.shape[1] % 8 == 0 and devices == 4 * CORES
        self.held = {}
        self.shared = {}
        if self.stepwise:
            self.direct(0, own[0])
        ahead = shifted(edge, "row", -1)
        self.own = []
        for (_, _, _, edge_tiles, edge_at), tiles in zip(plan.groups, own):
            if edge_tiles:
                tiles = jnp.concatenate([tiles, ahead[edge_at : edge_at + edge_tiles]], 0)
            self.own.append(tiles)
        if self.stepwise:
            self.direct(1, self.own[1])

    def direct(self, g, tiles):
        others = [swapped(tiles, CORES * m) for m in range(1, self.chips)]
        self.held[g] = [part.reshape((1,) + tiles.shape) for part in [tiles] + others]

    def together(self, groups):
        if self.stepwise:
            self.direct(groups[0], jnp.concatenate([self.own[g] for g in groups], 0))
            at = 0
            for g in groups:
                self.shared[g] = (groups[0], at, self.own[g].shape[0])
                at += self.own[g].shape[0]

    def receive(self, g, earlier=None, ready=None):
        if self.stepwise:
            source, at, count = self.shared.get(g, (g, 0, self.own[g].shape[0]))
            pieces = self.held[source]
            if ready is not None:
                pieces = after(pieces, ready)
            same = jnp.concatenate([piece[:, at : at + count] for piece in pieces], 0)
            if earlier is not None:
                same = after(same, earlier)
            return (same, swapped(same, 1))
        whole = lax.all_gather(self.own[g], "col", axis=0)
        whole = jnp.moveaxis(whole, 0, 1).reshape(1, whole.shape[1], self.size, WINDOW)
        return (whole,)


def shards(evecs, offsets, refl):
    rows = evecs.shape[0]
    nwin = rows // WINDOW
    rounds = refl.shape[0]
    size = refl.shape[4] - WINDOW
    plan = Plan(rounds, nwin)
    offsets = offsets.T
    groups = len(plan.groups)
    gather = Gather(plan, pack(plan, refl), size)
    rest = rows - HALF
    parts = [evecs]
    mats = None
    results, movements = [], []
    gather.together(range(2, groups))
    for ph in range(rounds):
        if ph < groups:
            ready = results[min(ph, 2) - 1] if ph else None
            tiles = gather.receive(ph, movements[1] if ph > 1 else None, ready)
        mats = matrices(plan, ph, offsets, mats, tiles)
        away = ph % 2 == 1
        sizes = (rest, HALF) if away else (HALF, rest)
        halves = phase(ph, rounds, nwin, offsets, parts, mats, sizes)
        result, kept = (halves[1], halves[0]) if away else halves
        results.append(result)
        moved = shifted(result, "row", 1 if away else -1)
        movements.append(moved)
        parts = [moved, kept] if away else [kept, moved]
    mats = matrices(plan, rounds, offsets, mats, tiles)
    (result,) = phase(rounds, rounds, nwin, offsets, parts, mats, (rows,))
    if rounds % 2:
        result = jnp.concatenate([shifted(result[rest:], "row", 1), result[:rest]], 0)
    return result


def solution(mesh):
    placed = (P("row", "col"), P(), P(None, None, "row", "col", None))
    return jax.shard_map(
        shards, mesh=mesh, in_specs=placed, out_specs=P("row", "col"), check_vma=False
    )
```

```python
import functools

import jax
import jax.numpy as jnp
from jax import lax
from jax.experimental import pallas as pl
from jax.experimental.pallas import tpu as pltpu
from jax.sharding import PartitionSpec as P

WINDOW = 128
HALF = 2 * WINDOW
CORES = 2
STAGE = 3
VMEM_LIMIT = 24 * 1024 * 1024
VMEM = pl.BlockSpec(memory_space=pltpu.VMEM)


def shifted(value, axis, by):
    devices = lax.axis_size(axis)
    return lax.ppermute(value, axis, [(i, (i + by) % devices) for i in range(devices)])


def swapped(value, bit):
    devices = lax.axis_size("col")
    return lax.ppermute(value, "col", [(i, i ^ bit) for i in range(devices)])


class Plan:
    def __init__(self, rounds, nwin):
        self.nwin = nwin
        self.phases = []
        for ph in range(rounds + 1):
            away = ph % 2 == 1
            entries = []
            self_carry = None
            if ph > 0:
                a, b = 2 * ph - 2, 2 * ph - 1
                if away:
                    entries += [(a, nwin - 1), None, (b, nwin - 1), (b, nwin)]
                    self_carry = (1, self.count(ph - 1) - 1)
                else:
                    entries += [(a, 1), (b, 0), (b, 1), None]
                    self_carry = (3, self.count(ph - 1) - (nwin - 1))
            if ph < rounds:
                base = 2 if away else 0
                for sweep in (2 * ph, 2 * ph + 1):
                    entries += [(sweep, base + k) for k in range(nwin - 1)]
            self.phases.append((entries, self_carry))
        groups = [[ph] for ph in range(rounds + 1)]
        self.groups = []
        self.where = {}
        edge_at = 0
        for g, members in enumerate(groups):
            wanted = [w for ph in members for w in self.phases[ph][0] if w is not None]
            own = [w for w in wanted if w[1] < nwin]
            edge = [w for w in wanted if w[1] == nwin]
            place = 0
            for part in (own, edge):
                for i, w in enumerate(part):
                    self.where[w] = (g, place + i, place + len(part) + i // 2, i % 2)
                place += len(part) + (len(part) + 1) // 2
            own_tiles = len(own) + (len(own) + 1) // 2
            edge_tiles = place - own_tiles
            self.groups.append((own, edge, own_tiles, edge_tiles, edge_at))
            edge_at += edge_tiles
        self.edge_tiles = edge_at

    def count(self, ph):
        return len(self.phases[ph][0])


def pack_kernel(plan, refl_ref, *outs):
    size = refl_ref.shape[-1] - WINDOW
    mine = refl_ref.shape[-2]

    def fill(out, at, windows):
        for i, (sweep, k) in enumerate(windows):
            out[at + i] = refl_ref[sweep // 2, sweep % 2, k, :, :WINDOW]
        at += len(windows)
        for i in range(0, len(windows), 2):
            halves = []
            for sweep, k in windows[i : i + 2]:
                halves.append(refl_ref[sweep // 2, sweep % 2, k, :, WINDOW:])
            if len(halves) == 1:
                halves.append(jnp.zeros((mine, size), jnp.float32))
            out[at + i // 2] = jnp.concatenate(halves, -1)

    for group, out in zip(plan.groups, outs):
        fill(out, 0, group[0])
    for group in plan.groups:
        if group[1]:
            fill(outs[-1], group[4], [(sweep, 0) for sweep, _ in group[1]])


def pack(plan, refl):
    mine = refl.shape[3]
    counts = [group[2] for group in plan.groups] + [plan.edge_tiles]
    return pl.pallas_call(
        functools.partial(pack_kernel, plan),
        out_shape=tuple(jax.ShapeDtypeStruct((n, mine, WINDOW), jnp.float32) for n in counts),
        in_specs=[VMEM],
        out_specs=(VMEM,) * len(counts),
        compiler_params=pltpu.CompilerParams(vmem_limit_bytes=VMEM_LIMIT),
    )(refl)


def split(value):
    high = value.astype(jnp.bfloat16)
    return high, (value - high.astype(jnp.float32)).astype(jnp.bfloat16)


def fold(value):
    half = value.shape[1] // 2
    return value[:, :half] + value[:, half:]


def matrix_kernel(plan, ph, masked, *refs):
    entries, carry = plan.phases[ph]
    operands = list(refs)
    refs = operands[1:] if masked else operands
    offsets = operands[0][...] if masked else None
    old_ref = refs.pop(0) if carry else None
    tiles = refs.pop()
    out_ref = refs.pop()
    parts = refs
    here = lax.axis_index("col")
    if len(parts) == 2:
        for m in range(parts[0].shape[0]):
            other = lax.bitwise_xor(here, m * CORES)
            tiles[other] = parts[0][m]
            tiles[lax.bitwise_xor(other, 1)] = parts[1][m]
    else:
        tiles = parts[0]
    size = tiles.shape[0] * tiles.shape[2]
    last = lax.axis_index("row") == lax.axis_size("row") - 1
    lane = lax.broadcasted_iota(jnp.int32, (size, WINDOW), 1)
    row_id = lax.broadcasted_iota(jnp.int32, (WINDOW, WINDOW), 0)
    col_id = lax.broadcasted_iota(jnp.int32, (WINDOW, WINDOW), 1)
    unit = jnp.where(row_id == col_id, 1.0, 0.0).astype(jnp.float32)

    def first(window):
        sweep, k = window
        _, vec_tile, fac_tile, side = plan.where[window]
        vectors = tiles[:, vec_tile].reshape(size, WINDOW)
        factors = tiles[:, fac_tile].reshape(size, WINDOW)
        if k == plan.nwin - 1:
            start = offsets[sweep % 2 : sweep % 2 + 1, sweep // 2 : sweep // 2 + 1]
            limit = jnp.where(last, WINDOW - start, WINDOW)
            vectors = jnp.where(lane < limit, vectors, 0.0)
        rows_hi, rows_lo = split(vectors)
        pair = jnp.concatenate([rows_hi, rows_lo], 1)
        blank = jnp.zeros_like(pair)
        stack = [blank, pair, blank, pair] if side else [pair, blank, pair, blank]
        scaled = jnp.dot(
            jnp.concatenate(split(factors), 1),
            jnp.concatenate(stack, 0),
            preferred_element_type=jnp.float32,
        )
        return jnp.concatenate([rows_hi, rows_lo], 0), scaled

    def second(rows, scaled):
        pair = jnp.concatenate(split(fold(scaled)), 1)
        product = lax.dot_general(
            rows,
            jnp.concatenate([pair, pair], 0),
            (((0,), (0,)), ((), ())),
            preferred_element_type=jnp.float32,
        )
        return jnp.concatenate(split(unit - fold(product)), 1)

    fresh = [i for i, window in enumerate(entries) if window is not None]
    for at in range(0, len(fresh), STAGE):
        some = fresh[at : at + STAGE]
        halves = [first(entries[i]) for i in some]
        for i, half in zip(some, halves):
            out_ref[i] = second(*half)
    if carry:
        out_ref[carry[0]] = old_ref[carry[1]]


def matrices(plan, ph, offsets, before, parts):
    count = plan.count(ph)
    carried = (before,) if plan.phases[ph][1] else ()
    masked = any(w is not None and w[1] == plan.nwin - 1 for w in plan.phases[ph][0])
    operands = [*([offsets] if masked else []), *carried, *parts]
    whole = (sum(part.shape[0] for part in parts),) + parts[0].shape[1:]
    return pl.pallas_call(
        functools.partial(matrix_kernel, plan, ph, masked),
        out_shape=jax.ShapeDtypeStruct((count, WINDOW, 2 * WINDOW), jnp.bfloat16),
        in_specs=[VMEM] * len(operands),
        out_specs=VMEM,
        scratch_shapes=[pltpu.VMEM(whole, jnp.float32)],
        compiler_params=pltpu.CompilerParams(vmem_limit_bytes=VMEM_LIMIT),
        cost_estimate=pl.CostEstimate(
            flops=count * 12 * 64 * 128 * 192, bytes_accessed=count * 100000, transcendentals=0
        ),
    )(*operands)


def apply_windows(field, at, count, first, mats):
    rows = field[pl.ds(at, count * WINDOW), :]
    stacks = []
    for k in range(count):
        pair = jnp.concatenate(split(rows[k * WINDOW : (k + 1) * WINDOW]), 1)
        stacks.append(jnp.concatenate([pair, pair], 0))
    products = [
        jnp.dot(mats[first + k], stack, preferred_element_type=jnp.float32)
        for k, stack in enumerate(stacks)
    ]
    updated = jnp.concatenate([fold(product) for product in products], 0)
    field[pl.ds(at, count * WINDOW), :] = updated


def phase_kernel(ph, rounds, nwin, nparts, offsets_ref, *refs):
    parts = refs[:nparts]
    mats = refs[nparts]
    outs = refs[nparts + 1 : -1]
    field = refs[-1]
    place = 0
    for part in parts:
        field[place : place + part.shape[0], :] = part[...]
        place += part.shape[0]
    offsets = offsets_ref[...]
    at = 0
    if ph > 0:
        a, b = offsets[0, ph - 1], offsets[1, ph - 1]
        step = jnp.where(b < a, 1, 0)
        start = nwin - 3 if ph % 2 else 1
        apply_windows(field, a + WINDOW * start, 1, 0, mats)
        start = nwin - 4 if ph % 2 else 0
        apply_windows(field, b + WINDOW * (start + step), 2, 1 + step, mats)
        at = 4
    if ph < rounds:
        a, b = offsets[0, ph], offsets[1, ph]
        step = jnp.where(b < a, 1, 0)
        apply_windows(field, a, nwin - 1, at, mats)
        apply_windows(field, b + WINDOW * step, nwin - 2, at + nwin - 1 + step, mats)
    place = 0
    for out in outs:
        out[...] = field[place : place + out.shape[0], :]
        place += out.shape[0]


def phase(ph, rounds, nwin, offsets, parts, mats, sizes):
    rows = sum(part.shape[0] for part in parts)
    cols = parts[0].shape[1]
    operands = [offsets, *parts, mats]
    return pl.pallas_call(
        functools.partial(phase_kernel, ph, rounds, nwin, len(parts)),
        out_shape=tuple(jax.ShapeDtypeStruct((n, cols), jnp.float32) for n in sizes),
        in_specs=[VMEM] * len(operands),
        out_specs=(VMEM,) * len(sizes),
        scratch_shapes=[pltpu.VMEM((rows, cols), jnp.float32)],
        compiler_params=pltpu.CompilerParams(vmem_limit_bytes=VMEM_LIMIT),
        cost_estimate=pl.CostEstimate(
            flops=8 * 6 * WINDOW * WINDOW * cols, bytes_accessed=2000000, transcendentals=0
        ),
    )(*operands)


def after(value, earlier):
    return lax.optimization_barrier((value, earlier))[0]


class Gather:
    def __init__(self, plan, packed, size):
        self.plan = plan
        self.size = size
        *own, edge = packed
        devices = lax.axis_size("col")
        self.chips = devices // CORES
        self.stepwise = edge.shape[1] % 8 == 0 and devices == 4 * CORES
        self.held = {}
        self.shared = {}
        if self.stepwise:
            self.direct(0, own[0])
        ahead = shifted(edge, "row", -1)
        self.own = []
        for (_, _, _, edge_tiles, edge_at), tiles in zip(plan.groups, own):
            if edge_tiles:
                tiles = jnp.concatenate([tiles, ahead[edge_at : edge_at + edge_tiles]], 0)
            self.own.append(tiles)
        if self.stepwise:
            self.doubled(1, self.own[1], self.held[0][-1])

    def direct(self, g, tiles):
        others = [swapped(tiles, CORES * m) for m in range(1, self.chips)]
        self.held[g] = [part.reshape((1,) + tiles.shape) for part in [tiles] + others]

    def doubled(self, g, tiles, earlier=None):
        pair = (tiles, swapped(tiles, CORES))
        pair = jnp.stack(pair if earlier is None else after(pair, earlier))
        self.held[g] = [pair, swapped(pair, 2 * CORES)]

    def together(self, groups):
        if self.stepwise:
            self.direct(groups[0], jnp.concatenate([self.own[g] for g in groups], 0))
            at = 0
            for g in groups:
                self.shared[g] = (groups[0], at, self.own[g].shape[0])
                at += self.own[g].shape[0]

    def receive(self, g, earlier=None, ready=None):
        if self.stepwise:
            source, at, count = self.shared.get(g, (g, 0, self.own[g].shape[0]))
            pieces = self.held[source]
            if ready is not None:
                pieces = after(pieces, ready)
            same = jnp.concatenate([piece[:, at : at + count] for piece in pieces], 0)
            if earlier is not None:
                same = after(same, earlier)
            return (same, swapped(same, 1))
        whole = lax.all_gather(self.own[g], "col", axis=0)
        whole = jnp.moveaxis(whole, 0, 1).reshape(1, whole.shape[1], self.size, WINDOW)
        return (whole,)


def shards(evecs, offsets, refl):
    rows = evecs.shape[0]
    nwin = rows // WINDOW
    rounds = refl.shape[0]
    size = refl.shape[4] - WINDOW
    plan = Plan(rounds, nwin)
    offsets = offsets.T
    groups = len(plan.groups)
    gather = Gather(plan, pack(plan, refl), size)
    rest = rows - HALF
    parts = [evecs]
    mats = None
    results, movements = [], []
    gather.together(range(2, rounds))
    for ph in range(rounds):
        if ph < rounds:
            ready = results[min(ph, 2) - 1] if ph else None
            tiles = gather.receive(ph, movements[1] if ph > 1 else None, ready)
        mats = matrices(plan, ph, offsets, mats, tiles)
        away = ph % 2 == 1
        sizes = (rest, HALF) if away else (HALF, rest)
        halves = phase(ph, rounds, nwin, offsets, parts, mats, sizes)
        result, kept = (halves[1], halves[0]) if away else halves
        results.append(result)
        moved = shifted(result, "row", 1 if away else -1)
        movements.append(moved)
        parts = [moved, kept] if away else [kept, moved]
    if gather.stepwise:
        gather.doubled(rounds, after(gather.own[rounds], results[min(2, rounds - 1)]))
    tiles = gather.receive(rounds, results[-1], results[-1])
    mats = matrices(plan, rounds, offsets, mats, tiles)
    (result,) = phase(rounds, rounds, nwin, offsets, parts, mats, (rows,))
    if rounds % 2:
        result = jnp.concatenate([shifted(result[rest:], "row", 1), result[:rest]], 0)
    return result


def solution(mesh):
    placed = (P("row", "col"), P(), P(None, None, "row", "col", None))
    return jax.shard_map(
        shards, mesh=mesh, in_specs=placed, out_specs=P("row", "col"), check_vma=False
    )
```

```python
import functools

import jax
import jax.numpy as jnp
from jax import lax
from jax.experimental import pallas as pl
from jax.experimental.pallas import tpu as pltpu
from jax.sharding import PartitionSpec as P

WINDOW = 128
HALF = 2 * WINDOW
CORES = 2
STAGE = 5
VMEM_LIMIT = 24 * 1024 * 1024
VMEM = pl.BlockSpec(memory_space=pltpu.VMEM)


def shifted(value, axis, by):
    devices = lax.axis_size(axis)
    return lax.ppermute(value, axis, [(i, (i + by) % devices) for i in range(devices)])


def swapped(value, bit):
    devices = lax.axis_size("col")
    return lax.ppermute(value, "col", [(i, i ^ bit) for i in range(devices)])


class Plan:
    def __init__(self, rounds, nwin):
        self.nwin = nwin
        self.phases = []
        for ph in range(rounds + 1):
            away = ph % 2 == 1
            entries = []
            self_carry = None
            if ph > 0:
                a, b = 2 * ph - 2, 2 * ph - 1
                if away:
                    entries += [(a, nwin - 1), None, (b, nwin - 1), (b, nwin)]
                    self_carry = (1, self.count(ph - 1) - 1)
                else:
                    entries += [(a, 1), (b, 0), (b, 1), None]
                    self_carry = (3, self.count(ph - 1) - (nwin - 1))
            if ph < rounds:
                base = 2 if away else 0
                for sweep in (2 * ph, 2 * ph + 1):
                    entries += [(sweep, base + k) for k in range(nwin - 1)]
            self.phases.append((entries, self_carry))
        groups = [[ph] for ph in range(rounds - 1)] + [[rounds - 1, rounds]]
        self.groups = []
        self.where = {}
        edge_at = 0
        for g, members in enumerate(groups):
            wanted = [w for ph in members for w in self.phases[ph][0] if w is not None]
            own = [w for w in wanted if w[1] < nwin]
            edge = [w for w in wanted if w[1] == nwin]
            place = 0
            for part in (own, edge):
                for i, w in enumerate(part):
                    self.where[w] = (g, place + i, place + len(part) + i // 2, i % 2)
                place += len(part) + (len(part) + 1) // 2
            own_tiles = len(own) + (len(own) + 1) // 2
            edge_tiles = place - own_tiles
            self.groups.append((own, edge, own_tiles, edge_tiles, edge_at))
            edge_at += edge_tiles
        self.edge_tiles = edge_at

    def count(self, ph):
        return len(self.phases[ph][0])


def pack_kernel(plan, refl_ref, *outs):
    size = refl_ref.shape[-1] - WINDOW
    mine = refl_ref.shape[-2]

    def fill(out, at, windows):
        for i, (sweep, k) in enumerate(windows):
            out[at + i] = refl_ref[sweep // 2, sweep % 2, k, :, :WINDOW]
        at += len(windows)
        for i in range(0, len(windows), 2):
            halves = []
            for sweep, k in windows[i : i + 2]:
                halves.append(refl_ref[sweep // 2, sweep % 2, k, :, WINDOW:])
            if len(halves) == 1:
                halves.append(jnp.zeros((mine, size), jnp.float32))
            out[at + i // 2] = jnp.concatenate(halves, -1)

    for group, out in zip(plan.groups, outs):
        fill(out, 0, group[0])
    for group in plan.groups:
        if group[1]:
            fill(outs[-1], group[4], [(sweep, 0) for sweep, _ in group[1]])


def pack(plan, refl):
    mine = refl.shape[3]
    counts = [group[2] for group in plan.groups] + [plan.edge_tiles]
    return pl.pallas_call(
        functools.partial(pack_kernel, plan),
        out_shape=tuple(jax.ShapeDtypeStruct((n, mine, WINDOW), jnp.float32) for n in counts),
        in_specs=[VMEM],
        out_specs=(VMEM,) * len(counts),
        compiler_params=pltpu.CompilerParams(vmem_limit_bytes=VMEM_LIMIT),
    )(refl)


def split(value):
    high = value.astype(jnp.bfloat16)
    return high, (value - high.astype(jnp.float32)).astype(jnp.bfloat16)


def fold(value):
    half = value.shape[1] // 2
    return value[:, :half] + value[:, half:]


def matrix_kernel(plan, ph, masked, *refs):
    entries, carry = plan.phases[ph]
    operands = list(refs)
    refs = operands[1:] if masked else operands
    offsets = operands[0][...] if masked else None
    old_ref = refs.pop(0) if carry else None
    tiles = refs.pop()
    out_ref = refs.pop()
    parts = refs
    here = lax.axis_index("col")
    if len(parts) == 2:
        for m in range(parts[0].shape[0]):
            other = lax.bitwise_xor(here, m * CORES)
            tiles[other] = parts[0][m]
            tiles[lax.bitwise_xor(other, 1)] = parts[1][m]
    else:
        tiles = parts[0]
    size = tiles.shape[0] * tiles.shape[2]
    last = lax.axis_index("row") == lax.axis_size("row") - 1
    lane = lax.broadcasted_iota(jnp.int32, (size, WINDOW), 1)
    row_id = lax.broadcasted_iota(jnp.int32, (WINDOW, WINDOW), 0)
    col_id = lax.broadcasted_iota(jnp.int32, (WINDOW, WINDOW), 1)
    unit = jnp.where(row_id == col_id, 1.0, 0.0).astype(jnp.float32)

    def first(window):
        sweep, k = window
        _, vec_tile, fac_tile, side = plan.where[window]
        vectors = tiles[:, vec_tile].reshape(size, WINDOW)
        factors = tiles[:, fac_tile].reshape(size, WINDOW)
        if k == plan.nwin - 1:
            start = offsets[sweep % 2 : sweep % 2 + 1, sweep // 2 : sweep // 2 + 1]
            limit = jnp.where(last, WINDOW - start, WINDOW)
            vectors = jnp.where(lane < limit, vectors, 0.0)
        rows_hi, rows_lo = split(vectors)
        pair = jnp.concatenate([rows_hi, rows_lo], 1)
        blank = jnp.zeros_like(pair)
        stack = [blank, pair, blank, pair] if side else [pair, blank, pair, blank]
        scaled = jnp.dot(
            jnp.concatenate(split(factors), 1),
            jnp.concatenate(stack, 0),
            preferred_element_type=jnp.float32,
        )
        return jnp.concatenate([rows_hi, rows_lo], 0), scaled

    def second(rows, scaled):
        pair = jnp.concatenate(split(fold(scaled)), 1)
        product = lax.dot_general(
            rows,
            jnp.concatenate([pair, pair], 0),
            (((0,), (0,)), ((), ())),
            preferred_element_type=jnp.float32,
        )
        return jnp.concatenate(split(unit - fold(product)), 1)

    fresh = [i for i, window in enumerate(entries) if window is not None]
    for at in range(0, len(fresh), STAGE):
        some = fresh[at : at + STAGE]
        halves = [first(entries[i]) for i in some]
        for i, half in zip(some, halves):
            out_ref[i] = second(*half)
    if carry:
        out_ref[carry[0]] = old_ref[carry[1]]


def matrices(plan, ph, offsets, before, parts):
    count = plan.count(ph)
    carried = (before,) if plan.phases[ph][1] else ()
    masked = any(w is not None and w[1] == plan.nwin - 1 for w in plan.phases[ph][0])
    operands = [*([offsets] if masked else []), *carried, *parts]
    whole = (sum(part.shape[0] for part in parts),) + parts[0].shape[1:]
    return pl.pallas_call(
        functools.partial(matrix_kernel, plan, ph, masked),
        out_shape=jax.ShapeDtypeStruct((count, WINDOW, 2 * WINDOW), jnp.bfloat16),
        in_specs=[VMEM] * len(operands),
        out_specs=VMEM,
        scratch_shapes=[pltpu.VMEM(whole, jnp.float32)],
        compiler_params=pltpu.CompilerParams(vmem_limit_bytes=VMEM_LIMIT),
        cost_estimate=pl.CostEstimate(
            flops=count * 12 * 64 * 128 * 192, bytes_accessed=count * 100000, transcendentals=0
        ),
    )(*operands)


def apply_windows(field, at, count, first, mats):
    rows = field[pl.ds(at, count * WINDOW), :]
    stacks = []
    for k in range(count):
        pair = jnp.concatenate(split(rows[k * WINDOW : (k + 1) * WINDOW]), 1)
        stacks.append(jnp.concatenate([pair, pair], 0))
    products = [
        jnp.dot(mats[first + k], stack, preferred_element_type=jnp.float32)
        for k, stack in enumerate(stacks)
    ]
    updated = jnp.concatenate([fold(product) for product in products], 0)
    field[pl.ds(at, count * WINDOW), :] = updated


def phase_kernel(ph, rounds, nwin, nparts, offsets_ref, *refs):
    parts = refs[:nparts]
    mats = refs[nparts]
    outs = refs[nparts + 1 : -1]
    field = refs[-1]
    place = 0
    for part in parts:
        field[place : place + part.shape[0], :] = part[...]
        place += part.shape[0]
    offsets = offsets_ref[...]
    at = 0
    if ph > 0:
        a, b = offsets[0, ph - 1], offsets[1, ph - 1]
        step = jnp.where(b < a, 1, 0)
        start = nwin - 3 if ph % 2 else 1
        apply_windows(field, a + WINDOW * start, 1, 0, mats)
        start = nwin - 4 if ph % 2 else 0
        apply_windows(field, b + WINDOW * (start + step), 2, 1 + step, mats)
        at = 4
    if ph < rounds:
        a, b = offsets[0, ph], offsets[1, ph]
        step = jnp.where(b < a, 1, 0)
        apply_windows(field, a, nwin - 1, at, mats)
        apply_windows(field, b + WINDOW * step, nwin - 2, at + nwin - 1 + step, mats)
    place = 0
    for out in outs:
        out[...] = field[place : place + out.shape[0], :]
        place += out.shape[0]


def phase(ph, rounds, nwin, offsets, parts, mats, sizes):
    rows = sum(part.shape[0] for part in parts)
    cols = parts[0].shape[1]
    operands = [offsets, *parts, mats]
    return pl.pallas_call(
        functools.partial(phase_kernel, ph, rounds, nwin, len(parts)),
        out_shape=tuple(jax.ShapeDtypeStruct((n, cols), jnp.float32) for n in sizes),
        in_specs=[VMEM] * len(operands),
        out_specs=(VMEM,) * len(sizes),
        scratch_shapes=[pltpu.VMEM((rows, cols), jnp.float32)],
        compiler_params=pltpu.CompilerParams(vmem_limit_bytes=VMEM_LIMIT),
        cost_estimate=pl.CostEstimate(
            flops=8 * 6 * WINDOW * WINDOW * cols, bytes_accessed=2000000, transcendentals=0
        ),
    )(*operands)


def after(value, earlier):
    return lax.optimization_barrier((value, earlier))[0]


class Gather:
    def __init__(self, plan, packed, size):
        self.plan = plan
        self.size = size
        *own, edge = packed
        devices = lax.axis_size("col")
        self.chips = devices // CORES
        self.stepwise = edge.shape[1] % 8 == 0 and devices == 4 * CORES
        self.held = {}
        self.shared = {}
        if self.stepwise:
            self.direct(0, own[0])
        ahead = shifted(edge, "row", -1)
        self.own = []
        for (_, _, _, edge_tiles, edge_at), tiles in zip(plan.groups, own):
            if edge_tiles:
                tiles = jnp.concatenate([tiles, ahead[edge_at : edge_at + edge_tiles]], 0)
            self.own.append(tiles)
        if self.stepwise:
            self.doubled(1, self.own[1], self.held[0][-1])

    def direct(self, g, tiles):
        others = [swapped(tiles, CORES * m) for m in range(1, self.chips)]
        self.held[g] = [part.reshape((1,) + tiles.shape) for part in [tiles] + others]

    def doubled(self, g, tiles, earlier=None):
        pair = (tiles, swapped(tiles, CORES))
        pair = jnp.stack(pair if earlier is None else after(pair, earlier))
        self.held[g] = [pair, swapped(pair, 2 * CORES)]

    def together(self, groups):
        if self.stepwise:
            self.direct(groups[0], jnp.concatenate([self.own[g] for g in groups], 0))
            at = 0
            for g in groups:
                self.shared[g] = (groups[0], at, self.own[g].shape[0])
                at += self.own[g].shape[0]

    def receive(self, g, earlier=None, ready=None):
        if self.stepwise:
            source, at, count = self.shared.get(g, (g, 0, self.own[g].shape[0]))
            pieces = self.held[source]
            if ready is not None:
                pieces = after(pieces, ready)
            same = jnp.concatenate([piece[:, at : at + count] for piece in pieces], 0)
            if earlier is not None:
                same = after(same, earlier)
            return (same, swapped(same, 1))
        whole = lax.all_gather(self.own[g], "col", axis=0)
        whole = jnp.moveaxis(whole, 0, 1).reshape(1, whole.shape[1], self.size, WINDOW)
        return (whole,)


def shards(evecs, offsets, refl):
    rows = evecs.shape[0]
    nwin = rows // WINDOW
    rounds = refl.shape[0]
    size = refl.shape[4] - WINDOW
    plan = Plan(rounds, nwin)
    offsets = offsets.T
    groups = len(plan.groups)
    gather = Gather(plan, pack(plan, refl), size)
    rest = rows - HALF
    parts = [evecs]
    mats = None
    results, movements = [], []
    gather.together(range(2, groups))
    for ph in range(rounds):
        if ph < groups:
            ready = results[min(ph, 2) - 1] if ph else None
            tiles = gather.receive(ph, movements[1] if ph > 1 else None, ready)
        mats = matrices(plan, ph, offsets, mats, tiles)
        away = ph % 2 == 1
        sizes = (rest, HALF) if away else (HALF, rest)
        halves = phase(ph, rounds, nwin, offsets, parts, mats, sizes)
        result, kept = (halves[1], halves[0]) if away else halves
        results.append(result)
        moved = shifted(result, "row", 1 if away else -1)
        movements.append(moved)
        parts = [moved, kept] if away else [kept, moved]
    mats = matrices(plan, rounds, offsets, mats, tiles)
    (result,) = phase(rounds, rounds, nwin, offsets, parts, mats, (rows,))
    if rounds % 2:
        result = jnp.concatenate([shifted(result[rest:], "row", 1), result[:rest]], 0)
    return result


def solution(mesh):
    placed = (P("row", "col"), P(), P(None, None, "row", "col", None))
    return jax.shard_map(
        shards, mesh=mesh, in_specs=placed, out_specs=P("row", "col"), check_vma=False
    )
```
